32 devices in a mesh: fsdp: 32 (over z, y, x, core).
Axes of the slice: x: 2, y: 2, z: 4, core: 2. Of those that a mesh axis runs over, the one named last changes fastest.
Arguments:
- tokens: bfloat16 [32768, 768], P('fsdp'), may hold values from -6 to 6
- lengths: int32 [64, 2], P('fsdp'), may hold values from 1 to 448, as said below
- gain_attn: bfloat16 [768], P('fsdp'), may hold values from 0.5 to 1.5
- w_query: bfloat16 [768, 768], P('fsdp'), may hold values from -0.0546875 to 0.0546875
- w_key: bfloat16 [768, 768], P('fsdp'), may hold values from -0.21875 to 0.21875
- w_value: bfloat16 [768, 768], P('fsdp'), may hold values from -0.21875 to 0.21875
- w_attn_out: bfloat16 [768, 768], P('fsdp'), may hold values from -0.875 to 0.875
- gain_ffn: bfloat16 [768], P('fsdp'), may hold values from 0.5 to 1.5
- w_ffn_in: bfloat16 [768, 3072], P('fsdp'), may hold values from -0.21875 to 0.21875
- w_ffn_out: bfloat16 [3072, 768], P('fsdp'), may hold values from -0.15625 to 0.15625
- bucket_bias_matrix: bfloat16 [32, 12], replicated, may hold values from -4 to 4
- cotangent: bfloat16 [32768, 768], P('fsdp'), may hold values from -6 to 6
Outputs:
- output: bfloat16 [32768, 768], P('fsdp')
- grad_tokens: bfloat16 [32768, 768], P('fsdp')
- grad_gain_attn: float32 [768], P('fsdp')
- grad_query: float32 [768, 768], P('fsdp')
- grad_key: float32 [768, 768], P('fsdp')
- grad_value: float32 [768, 768], P('fsdp')
- grad_attn_out: float32 [768, 768], P('fsdp')
- feedforward_gain_gradient: float32 [768], P('fsdp')
- grad_ffn_in: float32 [768, 3072], P('fsdp')
- grad_ffn_out: float32 [3072, 768], P('fsdp')
- grad_bias_table: float32 [32, 12], replicated
The draws below stay inside these ranges and needn't reach their ends.
Inputs may be any that keep to these rules, and one draw needn't show every extreme that they name: Column 0 is the row's query length, 1 to 64; column 1 its passage length, 128 to 448; in every draw some row's two lengths add up to 512.
All inputs are finite; a program needn't handle non-finite values.
Results may differ from the reference program's by a relative error of at most 0.014.
Values may be sent and summed in bfloat16 or wider, within the bound.
No kernel may reach another device: no remote copies, remote signals or barrier semaphores. Data moves between devices by JAX's collectives and lax.ppermute only.
A program may use at most 192 MiB of HBM per device.

```python
import math
import jax
import jax.numpy as jnp
import numpy as np
from jax import lax

D = 768
H = 12
DH = 64
FF = 3072
NB = 32
MAXD = 128
SEQ = 512
QMAX = 64
SEQS = 64
TOKENS = 32768


def draw_lengths(key, part):
    key_query, key_passage, key_full = jax.random.split(jax.random.fold_in(key, 7), 3)
    query_len = jax.random.randint(key_query, (SEQS,), 1, QMAX + 1)
    passage_len = jax.random.randint(key_passage, (SEQS,), SEQ // 4, SEQ - QMAX + 1)
    chosen = jax.random.randint(key_full, (), 0, SEQS)
    filled = jnp.arange(SEQS) == chosen
    query_len = jnp.where(filled, QMAX, query_len)
    passage_len = jnp.where(filled, SEQ - QMAX, passage_len)
    return jnp.stack([query_len, passage_len], axis=-1).astype(jnp.int32)


def spiked(entries, rng, source, target, blocks, factor):
    owner, partner = [(jnp.arange(entries.shape[dim]) // (entries.shape[dim] // blocks)).reshape([-1 if axis == dim else 1 for axis in range(entries.ndim)]) for dim in (source, target)]
    chosen = jax.random.permutation(rng, blocks)[partner]
    strong = (owner == chosen) | (owner == (partner + blocks // 2) % blocks)
    return jnp.where(strong, factor * entries, entries)


def steps_of(own_key, extent, cuts, smallest, top_value):
    def one(axis_at, shards_of):
        steps = jax.random.uniform(jax.random.fold_in(jax.random.fold_in(own_key, 6), axis_at), (shards_of,), jnp.float32, smallest / len(cuts), top_value / len(cuts))
        return jnp.repeat(jnp.exp(steps), extent[axis_at] // shards_of).reshape((-1,) + (1,) * (len(extent) - axis_at - 1))

    level = one(*cuts[0])
    for cut in cuts[1:]:
        level = level * one(*cut)
    return level


def centred(rng, extent, scale, limit, shards=(), kind=jnp.bfloat16):
    array = scale * jax.random.normal(rng, extent, jnp.float32)
    if shards:
        array = array * steps_of(rng, extent, shards, -0.22, 0.18)
    return jnp.clip(array, -limit, limit).astype(kind)


def noise_with(own_key, dims, deviation, limit, shards, heavy, kind=jnp.bfloat16):
    entries = deviation * jax.random.normal(own_key, dims, jnp.float32)
    if shards:
        entries = entries * steps_of(own_key, dims, shards, -0.22, 0.18)
    return jnp.clip(spiked(entries, jax.random.fold_in(own_key, 3), *heavy), -limit, limit).astype(kind)


def setup_inputs(seed: int = 0) -> dict:
    seeds = jax.random.split(jax.random.key(seed), 13)
    tokens = noise_with(seeds[0], (TOKENS, D), 1.0, 6.0, ((0, 32),), (0, 1, 32, 2.75))
    lengths = draw_lengths(jax.random.fold_in(seeds[12], 71), 0)
    gain_attn = jnp.clip(1.0 + 0.1 * jax.random.normal(seeds[2], (D,), jnp.float32), 0.5, 1.5).astype(jnp.bfloat16)
    w_query = centred(seeds[3], (D, D), (16 * D) ** -0.5, 0.0546875, ((0, 32),))
    w_key = centred(seeds[4], (D, D), D ** -0.5, 0.21875, ((0, 32),))
    w_value = centred(seeds[5], (D, D), D ** -0.5, 0.21875, ((0, 32),))
    w_attn_out = centred(seeds[6], (D, D), (D // 16) ** -0.5, 0.875, ((0, 32),))
    gain_ffn = jnp.clip(1.0 + 0.1 * jax.random.normal(seeds[7], (D,), jnp.float32), 0.5, 1.5).astype(jnp.bfloat16)
    w_ffn_in = centred(seeds[8], (D, FF), D ** -0.5, 0.21875, ((0, 32),))
    w_ffn_out = centred(seeds[9], (FF, D), (FF // 2) ** -0.5, 0.15625, ((0, 32),))
    bucket_bias_matrix = centred(seeds[10], (NB, H), 1.0, 4.0)
    cotangent = centred(seeds[11], (TOKENS, D), 1.0, 6.0, ((0, 32),))
    return {"tokens": tokens, "lengths": lengths, "gain_attn": gain_attn, "w_query": w_query, "w_key": w_key, "w_value": w_value, "w_attn_out": w_attn_out, "gain_ffn": gain_ffn, "w_ffn_in": w_ffn_in, "w_ffn_out": w_ffn_out, "bucket_bias_matrix": bucket_bias_matrix, "cotangent": cotangent}


@jax.custom_vjp
def low(v):
    return lax.optimization_barrier(v.astype(jnp.bfloat16)).astype(jnp.float32)

@jax.custom_vjp
def low_back(v):
    return v

def low_keep(v):
    return (low(v), None)

def low_pass(kept, grad):
    return (grad,)

def back_keep(v):
    return (v, None)

def back_low(kept, grad):
    return (low(grad),)
low.defvjp(low_keep, low_pass)
low_back.defvjp(back_keep, back_low)

def bucket_ids(span_length):
    offset = np.arange(span_length)[None, :] - np.arange(span_length)[:, None]
    half_count = NB // 2
    exact_count = half_count // 2
    result = np.where(offset > 0, half_count, 0)
    distance = np.abs(offset)
    spread = exact_count + np.floor(np.log(np.maximum(distance, 1) / exact_count) / math.log(MAXD / exact_count) * (half_count - exact_count))
    spread = np.minimum(spread, half_count - 1)
    result = result + np.where(distance < exact_count, distance, spread)
    return result.astype(np.int32)

def matmul(left, right):
    return jnp.dot(left, right, precision=lax.Precision.HIGHEST, preferred_element_type=jnp.float32)

def smooth_gate(values):
    return jax.nn.gelu(values, approximate=True)

def root_mean_square_scale(values, gain):
    return values * lax.rsqrt(lax.optimization_barrier(jnp.mean(values * values, axis=-1, keepdims=True)) + 1e-06) * gain

def attend(query_seq, key_seq, value_seq, valid_len, bias_patch):
    scores = jnp.einsum('qhd,khd->hqk', query_seq, key_seq, precision=lax.Precision.HIGHEST) + bias_patch
    scores = low_back(scores)
    permitted_pairs = jnp.arange(SEQ, dtype=jnp.int32) < valid_len
    keep = permitted_pairs.astype(jnp.float32)[None, None, :]
    scores = jnp.where(permitted_pairs[None, None, :], scores, -1000000000.0)
    row_peak = lax.optimization_barrier(jnp.max(scores, axis=-1, keepdims=True))
    shifted_exp = jnp.exp(scores - row_peak) * keep
    attention_weights = shifted_exp / lax.optimization_barrier(jnp.sum(shifted_exp, axis=-1, keepdims=True))
    mixed_rows = jnp.einsum('hqk,khd->qhd', low(attention_weights), value_seq, precision=lax.Precision.HIGHEST)
    return mixed_rows.reshape(SEQ, D)

def forward(weights, group_tokens, group_valid, bucket_indicator):
    gain_attn, w_query, w_key, w_value, w_attn_out, gain_ffn, w_ffn_in, w_ffn_out, bucket_bias_matrix = weights
    group_size = group_tokens.shape[0]
    flat_rows = group_tokens.reshape(group_size * SEQ, D)
    normed = low(root_mean_square_scale(flat_rows, gain_attn))
    query_rows = low(low_back(matmul(normed, w_query))).reshape(group_size, SEQ, H, DH)
    key_rows = low(low_back(matmul(normed, w_key))).reshape(group_size, SEQ, H, DH)
    value_rows = low(low_back(matmul(normed, w_value))).reshape(group_size, SEQ, H, DH)
    bias_patch = jnp.einsum('je,jvx->evx', bucket_bias_matrix, bucket_indicator, precision=lax.Precision.HIGHEST)
    checked = jax.checkpoint(attend)

    def one_sequence(carry, block_item):
        return (carry, checked(block_item[0], block_item[1], block_item[2], block_item[3], bias_patch))
    unused, attended = lax.scan(one_sequence, jnp.zeros((), jnp.float32), (query_rows, key_rows, value_rows, group_valid))
    attended = low(low_back(attended.reshape(group_size * SEQ, D)))
    hidden = flat_rows + low_back(matmul(attended, w_attn_out))
    normed_ffn = low(root_mean_square_scale(hidden, gain_ffn))
    activated = low(smooth_gate(low_back(matmul(normed_ffn, w_ffn_in))))
    result = hidden + low_back(matmul(activated, w_ffn_out))
    return result.reshape(group_size, SEQ, D)

def reference(tokens, lengths, gain_attn, w_query, w_key, w_value, w_attn_out, gain_ffn, w_ffn_in, w_ffn_out, bucket_bias_matrix, cotangent):
    weights = tuple((weight.astype(jnp.float32) for weight in (gain_attn, w_query, w_key, w_value, w_attn_out, gain_ffn, w_ffn_in, w_ffn_out, bucket_bias_matrix)))
    groups = SEQS // 8
    tokens_f = tokens.astype(jnp.float32).reshape(groups, 8, SEQ, D)
    cotangent_f = cotangent.astype(jnp.float32).reshape(groups, 8, SEQ, D)
    valid = lax.optimization_barrier(jnp.sum(lengths, axis=-1)).astype(jnp.int32).reshape(groups, 8)
    bucket = jnp.asarray(bucket_ids(SEQ), dtype=jnp.int32)
    bucket_indicator = (jnp.arange(NB, dtype=jnp.int32)[:, None, None] == bucket[None, :, :]).astype(jnp.float32)

    def step(totals, block_item):
        group_tokens, group_cot, group_valid = block_item
        result, pullback = jax.vjp(lambda inputs, params: forward(params, inputs, group_valid, bucket_indicator), group_tokens, weights)
        grad_inputs, grad_weights = pullback(group_cot)
        totals = jax.tree.map(lambda total, grad: total + grad, totals, grad_weights)
        return (totals, (result, grad_inputs))
    zeros = jax.tree.map(jnp.zeros_like, weights)
    totals, (outputs, grad_rows) = lax.scan(step, zeros, (tokens_f, cotangent_f, valid))
    factor = 1.0 / math.sqrt(TOKENS)
    scaled = tuple((total * factor for total in totals))
    return (outputs.reshape(TOKENS, D).astype(jnp.bfloat16), grad_rows.reshape(TOKENS, D).astype(jnp.bfloat16), scaled[0], scaled[1], scaled[2], scaled[3], scaled[4], scaled[5], scaled[6], scaled[7], scaled[8])
```

```python
import math

import jax
import jax.numpy as jnp
import numpy as np
from jax import lax
from jax.experimental import pallas as pl
from jax.experimental.pallas import tpu as pltpu
from jax.sharding import PartitionSpec as P

NB = 32
MAXD = 128
SEQ = 512


def bucket_ids(span_length):
    offset = np.arange(span_length)[None, :] - np.arange(span_length)[:, None]
    half_count = NB // 2
    exact_count = half_count // 2
    result = np.where(offset > 0, half_count, 0)
    distance = np.abs(offset)
    spread = exact_count + np.floor(
        np.log(np.maximum(distance, 1) / exact_count)
        / math.log(MAXD / exact_count)
        * (half_count - exact_count)
    )
    spread = np.minimum(spread, half_count - 1)
    result = result + np.where(distance < exact_count, distance, spread)
    return result.astype(np.int32)


def smooth_gate(values):
    return jax.nn.gelu(values, approximate=True)


def contract_rows(left, right):
    return lax.dot_general(
        left, right, (((0,), (0,)), ((), ())), preferred_element_type=jnp.float32
    )


def contract_cols(left, right):
    return lax.dot_general(
        left, right, (((1,), (1,)), ((), ())), preferred_element_type=jnp.float32
    )


def norm_scale(values):
    return lax.rsqrt(jnp.mean(values * values, axis=-1, keepdims=True) + 1e-06)


def rms_back(values, scale, gain, grad_normed):
    scaled = values * scale
    grad_gain = jnp.sum(grad_normed * scaled, axis=0)
    weighted = grad_normed * gain
    grad_values = scale * (weighted - scaled * jnp.mean(weighted * scaled, axis=-1, keepdims=True))
    return (grad_values, grad_gain)


def masked_scores(query_seq, key_seq, valid_len, bias_patch):
    scores = (
        jnp.einsum("qhd,khd->hqk", query_seq, key_seq, preferred_element_type=jnp.float32)
        + bias_patch
    )
    permitted_pairs = jnp.arange(scores.shape[-1]) < valid_len
    return jnp.where(permitted_pairs[None, None, :], scores, -1e30)


def flip(mask, count):
    return [(i, i ^ mask) for i in range(count)]


def swap(array, mask):
    return lax.ppermute(array, "fsdp", flip(mask, lax.axis_size("fsdp")))


def gather_chips(unit):
    line = lax.axis_size("fsdp") // 8
    half = line // 2
    near = jnp.stack([unit] + [swap(unit, 8 * hop) for hop in range(1, line)])
    over_x, over_y = swap(near, 2), swap(near, 4)
    return (near, over_x, over_y, swap(over_y[:half], 2), swap(over_x[half:], 4))


def chip_distances():
    line = lax.axis_size("fsdp") // 8
    half = line // 2
    blocks = []
    for part, (plane, first, last) in enumerate(
        ((0, 0, line), (1, 0, line), (2, 0, line), (3, 0, half), (3, half, line))
    ):
        blocks += [(part, hop - first, 4 * hop + plane) for hop in range(first, last)]
    return blocks


def scatter_chips(send, keep):
    line = keep.shape[1]
    half = line // 2

    def add(*terms):
        return sum(term.astype(jnp.float32) for term in terms)

    def low(value):
        return value.astype(jnp.bfloat16)

    both = low(add(keep, swap(send, 1)))
    via_x, via_y = swap(both[3, :half], 2), swap(both[3, half:], 4)
    x_low, y_high = swap(both[1, :half], 2), swap(both[2, half:], 4)
    y_low = swap(low(add(both[2, :half], via_x)), 4)
    x_high = swap(low(add(both[1, half:], via_y)), 2)
    total = jnp.concatenate(
        [low(add(both[0, :half], x_low, y_low)), low(add(both[0, half:], x_high, y_high))]
    )
    return add(total[0], *[swap(total[hop], 8 * hop) for hop in range(1, line)])


def copy_blocks(moves, place, sources, out_shapes):
    def kernel(place_ref, *refs):
        ins, outs, sems = refs[: len(sources)], refs[len(sources) : -1], refs[-1]
        copies = [
            pltpu.make_async_copy(source, target, sems.at[index])
            for index, (source, target) in enumerate(moves(place_ref[0], ins, outs))
        ]
        for copy in copies:
            copy.start()
        for copy in copies:
            copy.wait()

    return pl.pallas_call(
        kernel,
        out_shape=out_shapes,
        in_specs=[pl.BlockSpec(memory_space=pltpu.SMEM)]
        + [pl.BlockSpec(memory_space=pl.ANY)] * len(sources),
        out_specs=[pl.BlockSpec(memory_space=pl.ANY)] * len(out_shapes),
        scratch_shapes=[pltpu.SemaphoreType.DMA((lax.axis_size("fsdp"),))],
    )(place, *sources)


def both_cores(parts):
    return parts + tuple(swap(part, 1) for part in parts)


def chip_unit(shard, core):
    half = shard.shape[1] // 2
    mine = lax.dynamic_slice_in_dim(shard, core * half, half, 1)
    other = swap(lax.dynamic_slice_in_dim(shard, (1 - core) * half, half, 1), 1)
    return jnp.where(
        core == 0, jnp.concatenate([mine, other], 0), jnp.concatenate([other, mine], 0)
    )


def place_halves(parts, place, rows):
    parts = both_cores(parts)
    count = len(parts) // 2
    chips = lax.axis_size("fsdp") // 2

    def moves(me, ins, outs):
        chip, core = me // 2, me % 2
        for side in range(2):
            for part, index, distance in chip_distances():
                start = pl.multiple_of((chip ^ distance) * rows, 16)
                yield (
                    ins[side * count + part].at[index],
                    outs[0].at[core ^ side, pl.ds(start, rows), :],
                )

    shape = jax.ShapeDtypeStruct((2, chips * rows, parts[0].shape[-1]), jnp.bfloat16)
    return copy_blocks(moves, place, parts, [shape])[0]


def place_rows(parts, place, rows):
    parts = both_cores(parts)
    count = len(parts) // 2

    def moves(me, ins, outs):
        chip, core = me // 2, me % 2
        for side in range(2):
            for part, index, distance in chip_distances():
                start = pl.multiple_of(((chip ^ distance) * 2 + (core ^ side)) * rows, 16)
                yield (ins[side * count + part].at[index], outs[0].at[pl.ds(start, rows), :])

    shape = jax.ShapeDtypeStruct(
        (lax.axis_size("fsdp") * rows, parts[0].shape[-1]), jnp.bfloat16
    )
    return copy_blocks(moves, place, parts, [shape])[0]


def split_halves(halves, place):
    line = lax.axis_size("fsdp") // 8
    rows = halves.shape[1] // (4 * line)

    def moves(me, ins, outs):
        chip, core = me // 2, me % 2
        for side in range(2):
            for plane in range(4):
                for hop in range(line):
                    start = pl.multiple_of((chip ^ (4 * hop + plane)) * rows, 16)
                    yield (
                        ins[0].at[core ^ side, pl.ds(start, rows), :],
                        outs[side].at[plane, hop],
                    )

    shape = jax.ShapeDtypeStruct((4, line, rows, halves.shape[-1]), jnp.bfloat16)
    keep, send = copy_blocks(moves, place, [halves], [shape, shape])
    return send, keep


def split_rows(array, place):
    line = lax.axis_size("fsdp") // 8
    rows = array.shape[0] // (8 * line)

    def moves(me, ins, outs):
        chip, core = me // 2, me % 2
        for side in range(2):
            for plane in range(4):
                for hop in range(line):
                    start = pl.multiple_of(
                        ((chip ^ (4 * hop + plane)) * 2 + (core ^ side)) * rows, 16
                    )
                    yield (ins[0].at[pl.ds(start, rows), :], outs[side].at[plane, hop])

    shape = jax.ShapeDtypeStruct((4, line, rows, array.shape[-1]), jnp.bfloat16)
    keep, send = copy_blocks(moves, place, [array], [shape, shape])
    return send, keep


def own_rows(chip_sum, core):
    rows = chip_sum.shape[0] // 2
    mine = lax.dynamic_slice_in_dim(chip_sum, core * rows, rows, 0)
    other = swap(lax.dynamic_slice_in_dim(chip_sum, (1 - core) * rows, rows, 0), 1)
    return mine, other


def join_columns(mine, other, core):
    return jnp.where(
        core == 0, jnp.concatenate([mine, other], 1), jnp.concatenate([other, mine], 1)
    )


def gather_by_chips(
    gain_attn, w_query, w_key, w_value, w_attn_out, gain_ffn, w_ffn_in, w_ffn_out
):
    me = lax.axis_index("fsdp")
    core = me % 2
    place = me.astype(jnp.int32)[None]
    gains = jnp.pad(jnp.stack([gain_attn, gain_ffn], 1), ((0, 0), (0, 126)))
    other_gains = swap(gains, 1)
    chip_gains = jnp.where(
        core == 0,
        jnp.concatenate([gains, other_gains], 0),
        jnp.concatenate([other_gains, gains], 0),
    )
    unit_qkv = jnp.concatenate(
        [chip_unit(w_query, core), chip_unit(w_key, core), chip_unit(w_value, core), chip_gains], 1
    )
    unit_in = jnp.concatenate([chip_unit(w_attn_out, core), chip_unit(w_ffn_in, core)], 1)
    chip_rows = unit_qkv.shape[0]
    halves_qkv = place_halves(gather_chips(unit_qkv), place, chip_rows)
    halves_in = place_halves(gather_chips(unit_in), place, chip_rows)
    full_ffn_out = place_rows(gather_chips(w_ffn_out), place, w_ffn_out.shape[0])
    return halves_qkv, halves_in, full_ffn_out


def halves_of(*arrays):
    return jnp.stack(
        [
            jnp.concatenate(
                [
                    array[:, part * array.shape[1] // 2 : (part + 1) * array.shape[1] // 2]
                    for array in arrays
                ],
                1,
            )
            for part in range(2)
        ]
    )


def gather_plain(
    gain_attn, w_query, w_key, w_value, w_attn_out, gain_ffn, w_ffn_in, w_ffn_out
):
    def full(shard):
        return lax.all_gather(shard, "fsdp", axis=0, tiled=True)

    gains = jnp.pad(jnp.stack([full(gain_attn), full(gain_ffn)], 1), ((0, 0), (0, 126)))
    return (
        halves_of(full(w_query), full(w_key), full(w_value), jnp.concatenate([gains, gains], 1)),
        halves_of(full(w_attn_out), full(w_ffn_in)),
        full(w_ffn_out),
    )


def sum_by_chips(half_attn, half_in, grad_out):
    me = lax.axis_index("fsdp")
    core = me % 2
    place = me.astype(jnp.int32)[None]
    side = half_attn.shape[-1] // 4
    sum_out = scatter_chips(*split_rows(grad_out, place))
    sum_in = scatter_chips(*split_halves(half_in, place))
    sum_attn = scatter_chips(*split_halves(half_attn, place))
    mine, other = own_rows(sum_attn, core)
    sums = [
        join_columns(
            mine[:, part * side : (part + 1) * side], other[:, part * side : (part + 1) * side], core
        )
        for part in range(4)
    ]
    return sums + [join_columns(*own_rows(sum_in, core), core), sum_out]


def sum_plain(half_attn, half_in, grad_out):
    side = half_attn.shape[-1] // 4

    def owned(array):
        return lax.psum_scatter(
            array.astype(jnp.float32), "fsdp", scatter_dimension=0, tiled=True
        )

    grads = [
        jnp.concatenate([part[0], part[1]], 1)
        for part in [half_attn[:, :, k * side : (k + 1) * side] for k in range(4)] + [half_in]
    ]
    return [owned(grad) for grad in grads + [grad_out]]


def sum_everywhere(vector):
    mask = 1
    while mask < lax.axis_size("fsdp"):
        vector = vector + swap(vector, mask)
        mask *= 2
    return vector


def per_device(
    tokens,
    lengths,
    gain_attn,
    w_query,
    w_key,
    w_value,
    w_attn_out,
    gain_ffn,
    w_ffn_in,
    w_ffn_out,
    bucket_bias_matrix,
    cotangent,
):
    seq_count = lengths.shape[0]
    slot_count = seq_count * SEQ
    heads = bucket_bias_matrix.shape[1]
    width = tokens.shape[1]
    head_size = width // heads
    valid = jnp.sum(lengths, axis=-1)
    factor = 1.0 / math.sqrt(slot_count * lax.axis_size("fsdp"))
    me = lax.axis_index("fsdp")
    side = width // 2
    by_chips = 2 * gain_attn.shape[0] % 16 == 0
    if by_chips:
        halves_qkv, halves_in, full_ffn_out = gather_by_chips(
            gain_attn, w_query, w_key, w_value, w_attn_out, gain_ffn, w_ffn_in, w_ffn_out
        )
    else:
        halves_qkv, halves_in, full_ffn_out = gather_plain(
            gain_attn, w_query, w_key, w_value, w_attn_out, gain_ffn, w_ffn_in, w_ffn_out
        )

    def whole(halves, first, last):
        return jnp.concatenate([halves[0, :, first:last], halves[1, :, first:last]], 1)

    full_query = whole(halves_qkv, 0, side)
    full_key = whole(halves_qkv, side, 2 * side)
    full_value = whole(halves_qkv, 2 * side, 3 * side)
    full_gain_attn, full_gain_ffn = halves_qkv[0, :, 3 * side], halves_qkv[0, :, 3 * side + 1]
    full_attn_out = whole(halves_in, 0, side)
    full_ffn_in = whole(halves_in, side, halves_in.shape[-1])
    bucket_flat = jnp.asarray(bucket_ids(SEQ)).reshape(-1)
    onehot_table = (
        jnp.arange(bucket_bias_matrix.shape[0], dtype=jnp.int32)[:, None] == bucket_flat[None, :]
    ).astype(jnp.bfloat16)
    bias_patch = contract_rows(bucket_bias_matrix, onehot_table).reshape(heads, SEQ, SEQ)
    inputs_f = tokens.astype(jnp.float32)
    grad_out = cotangent.astype(jnp.float32)
    scale_attn = norm_scale(inputs_f)
    normed_attn = (inputs_f * scale_attn * full_gain_attn.astype(jnp.float32)).astype(jnp.bfloat16)
    query_rows = jnp.dot(normed_attn, full_query, preferred_element_type=jnp.float32).astype(
        jnp.bfloat16
    )
    key_rows = jnp.dot(normed_attn, full_key, preferred_element_type=jnp.float32).astype(
        jnp.bfloat16
    )
    value_rows = jnp.dot(normed_attn, full_value, preferred_element_type=jnp.float32).astype(
        jnp.bfloat16
    )
    query_seqs = query_rows.reshape(seq_count, SEQ, heads, head_size)
    key_seqs = key_rows.reshape(seq_count, SEQ, heads, head_size)
    value_seqs = value_rows.reshape(seq_count, SEQ, heads, head_size)

    def forward_block(block_item):
        query_seq, key_seq, value_seq, valid_len = block_item
        scores = masked_scores(query_seq, key_seq, valid_len, bias_patch)
        row_peak = jnp.max(scores, axis=-1, keepdims=True)
        shifted_exp = jnp.exp(scores - row_peak)
        row_total = jnp.sum(shifted_exp, axis=-1, keepdims=True)
        attention_weights = (shifted_exp / row_total).astype(jnp.bfloat16)
        mixed_rows = jnp.einsum(
            "hqk,khd->qhd", attention_weights, value_seq, preferred_element_type=jnp.float32
        ).astype(jnp.bfloat16)
        return (mixed_rows, row_peak[..., 0] + jnp.log(row_total[..., 0]))

    mixed_seqs, log_totals = lax.map(forward_block, (query_seqs, key_seqs, value_seqs, valid))
    attended = mixed_seqs.reshape(slot_count, width)
    hidden = inputs_f + jnp.dot(attended, full_attn_out, preferred_element_type=jnp.float32)
    scale_ffn = norm_scale(hidden)
    normed_ffn = (hidden * scale_ffn * full_gain_ffn.astype(jnp.float32)).astype(jnp.bfloat16)
    pre_act = jnp.dot(normed_ffn, full_ffn_in, preferred_element_type=jnp.float32)
    activated_f, gate_pullback = jax.vjp(smooth_gate, pre_act)
    activated = activated_f.astype(jnp.bfloat16)
    output = (hidden + jnp.dot(activated, full_ffn_out, preferred_element_type=jnp.float32)).astype(
        jnp.bfloat16
    )
    grad_ffn_out = contract_rows(activated, cotangent)
    grad_act = contract_cols(cotangent, full_ffn_out)
    grad_pre = gate_pullback(grad_act)[0].astype(jnp.bfloat16)
    grad_ffn_in = contract_rows(normed_ffn, grad_pre)
    grad_normed_ffn = contract_cols(grad_pre, full_ffn_in)
    grad_through_ffn, feedforward_gain_gradient = rms_back(
        hidden, scale_ffn, full_gain_ffn.astype(jnp.float32), grad_normed_ffn
    )
    grad_hidden = grad_out + grad_through_ffn
    grad_branch = grad_hidden.astype(jnp.bfloat16)
    grad_attn_out = contract_rows(attended, grad_branch)
    grad_attended = contract_cols(grad_branch, full_attn_out).astype(jnp.bfloat16)
    grad_mixed_seqs = grad_attended.reshape(seq_count, SEQ, heads, head_size)

    def backward_block(table_acc, block_item):
        query_seq, key_seq, value_seq, grad_mixed, log_total, valid_len = block_item
        scores = masked_scores(query_seq, key_seq, valid_len, bias_patch)
        attention_weights = jnp.exp(scores - log_total[..., None])
        grad_value_seq = jnp.einsum(
            "hqk,qhd->khd",
            attention_weights.astype(jnp.bfloat16),
            grad_mixed,
            preferred_element_type=jnp.float32,
        ).astype(jnp.bfloat16)
        grad_weights = jnp.einsum(
            "qhd,khd->hqk", grad_mixed, value_seq, preferred_element_type=jnp.float32
        )
        row_dot = jnp.sum(grad_weights * attention_weights, axis=-1, keepdims=True)
        grad_scores = (attention_weights * (grad_weights - row_dot)).astype(jnp.bfloat16)
        grad_query_seq = jnp.einsum(
            "hqk,khd->qhd", grad_scores, key_seq, preferred_element_type=jnp.float32
        ).astype(jnp.bfloat16)
        grad_key_seq = jnp.einsum(
            "hqk,qhd->khd", grad_scores, query_seq, preferred_element_type=jnp.float32
        ).astype(jnp.bfloat16)
        table_acc = table_acc + contract_cols(grad_scores.reshape(heads, SEQ * SEQ), onehot_table)
        return (table_acc, (grad_query_seq, grad_key_seq, grad_value_seq))

    table_start = jnp.zeros((heads, bucket_bias_matrix.shape[0]), jnp.float32)
    table_local, (grad_query_seqs, grad_key_seqs, grad_value_seqs) = lax.scan(
        backward_block,
        table_start,
        (query_seqs, key_seqs, value_seqs, grad_mixed_seqs, log_totals, valid),
    )
    grad_query_rows = grad_query_seqs.reshape(slot_count, width)
    grad_key_rows = grad_key_seqs.reshape(slot_count, width)
    grad_value_rows = grad_value_seqs.reshape(slot_count, width)
    grad_query = contract_rows(normed_attn, grad_query_rows)
    grad_key = contract_rows(normed_attn, grad_key_rows)
    grad_value = contract_rows(normed_attn, grad_value_rows)
    grad_normed_attn = (
        contract_cols(grad_query_rows, full_query)
        + contract_cols(grad_key_rows, full_key)
        + contract_cols(grad_value_rows, full_value)
    )
    grad_through_attn, grad_gain_attn = rms_back(
        inputs_f, scale_attn, full_gain_attn.astype(jnp.float32), grad_normed_attn
    )
    grad_tokens = (grad_hidden + grad_through_attn).astype(jnp.bfloat16)
    half_attn = halves_of(grad_query, grad_key, grad_value, grad_attn_out).astype(jnp.bfloat16)
    half_in = halves_of(grad_ffn_in).astype(jnp.bfloat16)
    sums = [
        total * factor
        for total in (sum_by_chips if by_chips else sum_plain)(
            half_attn, half_in, grad_ffn_out.astype(jnp.bfloat16)
        )
    ]
    small = sum_everywhere(
        jnp.concatenate(
            [grad_gain_attn, feedforward_gain_gradient, table_local.T.reshape(-1)]
        ).reshape(-1, 128)
    )
    small = small.reshape(-1) * factor
    shard = gain_attn.shape[0]
    return (
        output,
        grad_tokens,
        lax.dynamic_slice_in_dim(small, me * shard, shard),
        sums[0],
        sums[1],
        sums[2],
        sums[3],
        lax.dynamic_slice_in_dim(small, width + me * shard, shard),
        sums[4],
        sums[5],
        small[2 * width :].reshape(bucket_bias_matrix.shape),
    )


def solution(mesh):
    placed = (
        P("fsdp", None),
        P("fsdp", None),
        P("fsdp"),
        P("fsdp", None),
        P("fsdp", None),
        P("fsdp", None),
        P("fsdp", None),
        P("fsdp"),
        P("fsdp", None),
        P("fsdp", None),
        P(),
        P("fsdp", None),
    )
    return jax.shard_map(
        per_device,
        mesh=mesh,
        in_specs=placed,
        out_specs=(
            P("fsdp", None),
            P("fsdp", None),
            P("fsdp"),
            P("fsdp", None),
            P("fsdp", None),
            P("fsdp", None),
            P("fsdp", None),
            P("fsdp"),
            P("fsdp", None),
            P("fsdp", None),
            P(),
        ),
        check_vma=False,
    )
```

```python
import math

import jax
import jax.numpy as jnp
import numpy as np
from jax import lax
from jax.experimental import pallas as pl
from jax.experimental.pallas import tpu as pltpu
from jax.sharding import PartitionSpec as P

NB = 32
MAXD = 128
SEQ = 512


def bucket_ids(span_length):
    offset = np.arange(span_length)[None, :] - np.arange(span_length)[:, None]
    half_count = NB // 2
    exact_count = half_count // 2
    result = np.where(offset > 0, half_count, 0)
    distance = np.abs(offset)
    spread = exact_count + np.floor(
        np.log(np.maximum(distance, 1) / exact_count)
        / math.log(MAXD / exact_count)
        * (half_count - exact_count)
    )
    spread = np.minimum(spread, half_count - 1)
    result = result + np.where(distance < exact_count, distance, spread)
    return result.astype(np.int32)


def smooth_gate(values):
    return jax.nn.gelu(values, approximate=True)


def contract_rows(left, right):
    return lax.dot_general(
        left, right, (((0,), (0,)), ((), ())), preferred_element_type=jnp.float32
    )


def contract_cols(left, right):
    return lax.dot_general(
        left, right, (((1,), (1,)), ((), ())), preferred_element_type=jnp.float32
    )


def norm_scale(values):
    return lax.rsqrt(jnp.mean(values * values, axis=-1, keepdims=True) + 1e-06)


def rms_back(values, scale, gain, grad_normed):
    scaled = values * scale
    grad_gain = jnp.sum(grad_normed * scaled, axis=0)
    weighted = grad_normed * gain
    grad_values = scale * (weighted - scaled * jnp.mean(weighted * scaled, axis=-1, keepdims=True))
    return (grad_values, grad_gain)


def masked_scores(query_seq, key_seq, valid_len, bias_patch):
    scores = (
        jnp.einsum("qhd,khd->hqk", query_seq, key_seq, preferred_element_type=jnp.float32)
        + bias_patch
    )
    permitted_pairs = jnp.arange(scores.shape[-1]) < valid_len
    return jnp.where(permitted_pairs[None, None, :], scores, -1e30)


def flip(mask, count):
    return [(i, i ^ mask) for i in range(count)]


def swap(array, mask):
    return lax.ppermute(array, "fsdp", flip(mask, lax.axis_size("fsdp")))


def gather_chips(unit):
    line = lax.axis_size("fsdp") // 8
    half = line // 2
    near = jnp.stack([unit] + [swap(unit, 8 * hop) for hop in range(1, line)])
    over_x, over_y = swap(near, 2), swap(near, 4)
    return (near, over_x, over_y, swap(over_y[:half], 2), swap(over_x[half:], 4))


def chip_distances():
    line = lax.axis_size("fsdp") // 8
    half = line // 2
    blocks = []
    for part, (plane, first, last) in enumerate(
        ((0, 0, line), (1, 0, line), (2, 0, line), (3, 0, half), (3, half, line))
    ):
        blocks += [(part, hop - first, 4 * hop + plane) for hop in range(first, last)]
    return blocks


def scatter_chips(send, keep):
    line = keep.shape[1]
    half = line // 2

    def add(*terms):
        return sum(term.astype(jnp.float32) for term in terms)

    def low(value):
        return value.astype(jnp.bfloat16)

    both = low(add(keep, swap(send, 1)))
    via_x, via_y = swap(both[3, :half], 2), swap(both[3, half:], 4)
    x_low, y_high = swap(both[1, :half], 2), swap(both[2, half:], 4)
    y_low = swap(low(add(both[2, :half], via_x)), 4)
    x_high = swap(low(add(both[1, half:], via_y)), 2)
    total = jnp.concatenate(
        [low(add(both[0, :half], x_low, y_low)), low(add(both[0, half:], x_high, y_high))]
    )
    return add(total[0], *[swap(total[hop], 8 * hop) for hop in range(1, line)])


def copy_blocks(moves, place, sources, out_shapes):
    inside, outside = pl.BlockSpec(memory_space=pltpu.VMEM), pl.BlockSpec(memory_space=pl.ANY)
    from_vmem = len(sources) == 1
    def kernel(place_ref, *refs):
        ins, outs, sems = refs[: len(sources)], refs[len(sources) : -1], refs[-1]
        copies = [
            pltpu.make_async_copy(source, target, sems.at[index])
            for index, (source, target) in enumerate(moves(place_ref[0], ins, outs))
        ]
        for copy in copies:
            copy.start()
        for copy in copies:
            copy.wait()

    return pl.pallas_call(
        kernel,
        out_shape=out_shapes,
        in_specs=[pl.BlockSpec(memory_space=pltpu.SMEM)]
        + [inside if from_vmem else outside] * len(sources),
        out_specs=[outside if from_vmem else inside] * len(out_shapes),
        scratch_shapes=[pltpu.SemaphoreType.DMA((lax.axis_size("fsdp"),))],
        compiler_params=pltpu.CompilerParams(vmem_limit_bytes=24 * 1024 * 1024),
    )(place, *sources)


def both_cores(parts):
    return parts + tuple(swap(part, 1) for part in parts)


def chip_unit(shard, core):
    half = shard.shape[1] // 2
    mine = lax.dynamic_slice_in_dim(shard, core * half, half, 1)
    other = swap(lax.dynamic_slice_in_dim(shard, (1 - core) * half, half, 1), 1)
    return jnp.where(
        core == 0, jnp.concatenate([mine, other], 0), jnp.concatenate([other, mine], 0)
    )


def place_halves(parts, place, rows):
    parts = both_cores(parts)
    count = len(parts) // 2
    chips = lax.axis_size("fsdp") // 2

    def moves(me, ins, outs):
        chip, core = me // 2, me % 2
        for side in range(2):
            for part, index, distance in chip_distances():
                start = pl.multiple_of((chip ^ distance) * rows, 16)
                yield (
                    ins[side * count + part].at[index],
                    outs[0].at[core ^ side, pl.ds(start, rows), :],
                )

    shape = jax.ShapeDtypeStruct((2, chips * rows, parts[0].shape[-1]), jnp.bfloat16)
    return copy_blocks(moves, place, parts, [shape])[0]


def place_rows(parts, place, rows):
    parts = both_cores(parts)
    count = len(parts) // 2

    def moves(me, ins, outs):
        chip, core = me // 2, me % 2
        for side in range(2):
            for part, index, distance in chip_distances():
                start = pl.multiple_of(((chip ^ distance) * 2 + (core ^ side)) * rows, 16)
                yield (ins[side * count + part].at[index], outs[0].at[pl.ds(start, rows), :])

    shape = jax.ShapeDtypeStruct(
        (lax.axis_size("fsdp") * rows, parts[0].shape[-1]), jnp.bfloat16
    )
    return copy_blocks(moves, place, parts, [shape])[0]


def split_halves(halves, place):
    line = lax.axis_size("fsdp") // 8
    rows = halves.shape[1] // (4 * line)

    def moves(me, ins, outs):
        chip, core = me // 2, me % 2
        for side in range(2):
            for plane in range(4):
                for hop in range(line):
                    start = pl.multiple_of((chip ^ (4 * hop + plane)) * rows, 16)
                    yield (
                        ins[0].at[core ^ side, pl.ds(start, rows), :],
                        outs[side].at[plane, hop],
                    )

    shape = jax.ShapeDtypeStruct((4, line, rows, halves.shape[-1]), jnp.bfloat16)
    keep, send = copy_blocks(moves, place, [halves], [shape, shape])
    return send, keep


def split_rows(array, place):
    line = lax.axis_size("fsdp") // 8
    rows = array.shape[0] // (8 * line)

    def moves(me, ins, outs):
        chip, core = me // 2, me % 2
        for side in range(2):
            for plane in range(4):
                for hop in range(line):
                    start = pl.multiple_of(
                        ((chip ^ (4 * hop + plane)) * 2 + (core ^ side)) * rows, 16
                    )
                    yield (ins[0].at[pl.ds(start, rows), :], outs[side].at[plane, hop])

    shape = jax.ShapeDtypeStruct((4, line, rows, array.shape[-1]), jnp.bfloat16)
    keep, send = copy_blocks(moves, place, [array], [shape, shape])
    return send, keep


def own_rows(chip_sum, core):
    rows = chip_sum.shape[0] // 2
    mine = lax.dynamic_slice_in_dim(chip_sum, core * rows, rows, 0)
    other = swap(lax.dynamic_slice_in_dim(chip_sum, (1 - core) * rows, rows, 0), 1)
    return mine, other


def join_columns(mine, other, core):
    return jnp.where(
        core == 0, jnp.concatenate([mine, other], 1), jnp.concatenate([other, mine], 1)
    )


def gather_by_chips(
    gain_attn, w_query, w_key, w_value, w_attn_out, gain_ffn, w_ffn_in, w_ffn_out
):
    me = lax.axis_index("fsdp")
    core = me % 2
    place = me.astype(jnp.int32)[None]
    gains = jnp.pad(jnp.stack([gain_attn, gain_ffn], 1), ((0, 0), (0, 126)))
    other_gains = swap(gains, 1)
    chip_gains = jnp.where(
        core == 0,
        jnp.concatenate([gains, other_gains], 0),
        jnp.concatenate([other_gains, gains], 0),
    )
    unit_qkv = jnp.concatenate(
        [chip_unit(w_query, core), chip_unit(w_key, core), chip_unit(w_value, core), chip_gains], 1
    )
    unit_in = jnp.concatenate([chip_unit(w_attn_out, core), chip_unit(w_ffn_in, core)], 1)
    chip_rows = unit_qkv.shape[0]
    halves_qkv = place_halves(gather_chips(unit_qkv), place, chip_rows)
    halves_in = place_halves(gather_chips(unit_in), place, chip_rows)
    full_ffn_out = place_rows(gather_chips(w_ffn_out), place, w_ffn_out.shape[0])
    return halves_qkv, halves_in, full_ffn_out


def halves_of(*arrays):
    return jnp.stack(
        [
            jnp.concatenate(
                [
                    array[:, part * array.shape[1] // 2 : (part + 1) * array.shape[1] // 2]
                    for array in arrays
                ],
                1,
            )
            for part in range(2)
        ]
    )


def gather_plain(
    gain_attn, w_query, w_key, w_value, w_attn_out, gain_ffn, w_ffn_in, w_ffn_out
):
    def full(shard):
        return lax.all_gather(shard, "fsdp", axis=0, tiled=True)

    gains = jnp.pad(jnp.stack([full(gain_attn), full(gain_ffn)], 1), ((0, 0), (0, 126)))
    return (
        halves_of(full(w_query), full(w_key), full(w_value), jnp.concatenate([gains, gains], 1)),
        halves_of(full(w_attn_out), full(w_ffn_in)),
        full(w_ffn_out),
    )


def sum_by_chips(half_attn, half_in, grad_out):
    me = lax.axis_index("fsdp")
    core = me % 2
    place = me.astype(jnp.int32)[None]
    side = half_attn.shape[-1] // 4
    sum_out = scatter_chips(*split_rows(grad_out, place))
    sum_in = scatter_chips(*split_halves(half_in, place))
    sum_attn = scatter_chips(*split_halves(half_attn, place))
    mine, other = own_rows(sum_attn, core)
    sums = [
        join_columns(
            mine[:, part * side : (part + 1) * side], other[:, part * side : (part + 1) * side], core
        )
        for part in range(4)
    ]
    return sums + [join_columns(*own_rows(sum_in, core), core), sum_out]


def sum_plain(half_attn, half_in, grad_out):
    side = half_attn.shape[-1] // 4

    def owned(array):
        return lax.psum_scatter(
            array.astype(jnp.float32), "fsdp", scatter_dimension=0, tiled=True
        )

    grads = [
        jnp.concatenate([part[0], part[1]], 1)
        for part in [half_attn[:, :, k * side : (k + 1) * side] for k in range(4)] + [half_in]
    ]
    return [owned(grad) for grad in grads + [grad_out]]


def sum_everywhere(vector):
    mask = 1
    while mask < lax.axis_size("fsdp"):
        vector = vector + swap(vector, mask)
        mask *= 2
    return vector


def per_device(
    tokens,
    lengths,
    gain_attn,
    w_query,
    w_key,
    w_value,
    w_attn_out,
    gain_ffn,
    w_ffn_in,
    w_ffn_out,
    bucket_bias_matrix,
    cotangent,
):
    seq_count = lengths.shape[0]
    slot_count = seq_count * SEQ
    heads = bucket_bias_matrix.shape[1]
    width = tokens.shape[1]
    head_size = width // heads
    valid = jnp.sum(lengths, axis=-1)
    factor = 1.0 / math.sqrt(slot_count * lax.axis_size("fsdp"))
    me = lax.axis_index("fsdp")
    side = width // 2
    by_chips = 2 * gain_attn.shape[0] % 16 == 0
    if by_chips:
        halves_qkv, halves_in, full_ffn_out = gather_by_chips(
            gain_attn, w_query, w_key, w_value, w_attn_out, gain_ffn, w_ffn_in, w_ffn_out
        )
    else:
        halves_qkv, halves_in, full_ffn_out = gather_plain(
            gain_attn, w_query, w_key, w_value, w_attn_out, gain_ffn, w_ffn_in, w_ffn_out
        )

    def whole(halves, first, last):
        return jnp.concatenate([halves[0, :, first:last], halves[1, :, first:last]], 1)

    full_query = whole(halves_qkv, 0, side)
    full_key = whole(halves_qkv, side, 2 * side)
    full_value = whole(halves_qkv, 2 * side, 3 * side)
    full_gain_attn, full_gain_ffn = halves_qkv[0, :, 3 * side], halves_qkv[0, :, 3 * side + 1]
    full_attn_out = whole(halves_in, 0, side)
    full_ffn_in = whole(halves_in, side, halves_in.shape[-1])
    bucket_flat = jnp.asarray(bucket_ids(SEQ)).reshape(-1)
    onehot_table = (
        jnp.arange(bucket_bias_matrix.shape[0], dtype=jnp.int32)[:, None] == bucket_flat[None, :]
    ).astype(jnp.bfloat16)
    bias_patch = contract_rows(bucket_bias_matrix, onehot_table).reshape(heads, SEQ, SEQ)
    inputs_f = tokens.astype(jnp.float32)
    grad_out = cotangent.astype(jnp.float32)
    scale_attn = norm_scale(inputs_f)
    normed_attn = (inputs_f * scale_attn * full_gain_attn.astype(jnp.float32)).astype(jnp.bfloat16)
    query_rows = jnp.dot(normed_attn, full_query, preferred_element_type=jnp.float32).astype(
        jnp.bfloat16
    )
    key_rows = jnp.dot(normed_attn, full_key, preferred_element_type=jnp.float32).astype(
        jnp.bfloat16
    )
    value_rows = jnp.dot(normed_attn, full_value, preferred_element_type=jnp.float32).astype(
        jnp.bfloat16
    )
    query_seqs = query_rows.reshape(seq_count, SEQ, heads, head_size)
    key_seqs = key_rows.reshape(seq_count, SEQ, heads, head_size)
    value_seqs = value_rows.reshape(seq_count, SEQ, heads, head_size)

    def forward_block(block_item):
        query_seq, key_seq, value_seq, valid_len = block_item
        scores = masked_scores(query_seq, key_seq, valid_len, bias_patch)
        row_peak = jnp.max(scores, axis=-1, keepdims=True)
        shifted_exp = jnp.exp(scores - row_peak)
        row_total = jnp.sum(shifted_exp, axis=-1, keepdims=True)
        attention_weights = (shifted_exp / row_total).astype(jnp.bfloat16)
        mixed_rows = jnp.einsum(
            "hqk,khd->qhd", attention_weights, value_seq, preferred_element_type=jnp.float32
        ).astype(jnp.bfloat16)
        return (mixed_rows, row_peak[..., 0] + jnp.log(row_total[..., 0]))

    mixed_seqs, log_totals = lax.map(forward_block, (query_seqs, key_seqs, value_seqs, valid))
    attended = mixed_seqs.reshape(slot_count, width)
    hidden = inputs_f + jnp.dot(attended, full_attn_out, preferred_element_type=jnp.float32)
    scale_ffn = norm_scale(hidden)
    normed_ffn = (hidden * scale_ffn * full_gain_ffn.astype(jnp.float32)).astype(jnp.bfloat16)
    pre_act = jnp.dot(normed_ffn, full_ffn_in, preferred_element_type=jnp.float32)
    activated_f, gate_pullback = jax.vjp(smooth_gate, pre_act)
    activated = activated_f.astype(jnp.bfloat16)
    output = (hidden + jnp.dot(activated, full_ffn_out, preferred_element_type=jnp.float32)).astype(
        jnp.bfloat16
    )
    grad_ffn_out = contract_rows(activated, cotangent)
    grad_act = contract_cols(cotangent, full_ffn_out)
    grad_pre = gate_pullback(grad_act)[0].astype(jnp.bfloat16)
    grad_ffn_in = contract_rows(normed_ffn, grad_pre)
    grad_normed_ffn = contract_cols(grad_pre, full_ffn_in)
    grad_through_ffn, feedforward_gain_gradient = rms_back(
        hidden, scale_ffn, full_gain_ffn.astype(jnp.float32), grad_normed_ffn
    )
    grad_hidden = grad_out + grad_through_ffn
    grad_branch = grad_hidden.astype(jnp.bfloat16)
    grad_attn_out = contract_rows(attended, grad_branch)
    grad_attended = contract_cols(grad_branch, full_attn_out).astype(jnp.bfloat16)
    grad_mixed_seqs = grad_attended.reshape(seq_count, SEQ, heads, head_size)

    def backward_block(table_acc, block_item):
        query_seq, key_seq, value_seq, grad_mixed, log_total, valid_len = block_item
        scores = masked_scores(query_seq, key_seq, valid_len, bias_patch)
        attention_weights = jnp.exp(scores - log_total[..., None])
        grad_value_seq = jnp.einsum(
            "hqk,qhd->khd",
            attention_weights.astype(jnp.bfloat16),
            grad_mixed,
            preferred_element_type=jnp.float32,
        ).astype(jnp.bfloat16)
        grad_weights = jnp.einsum(
            "qhd,khd->hqk", grad_mixed, value_seq, preferred_element_type=jnp.float32
        )
        row_dot = jnp.sum(grad_weights * attention_weights, axis=-1, keepdims=True)
        grad_scores = (attention_weights * (grad_weights - row_dot)).astype(jnp.bfloat16)
        grad_query_seq = jnp.einsum(
            "hqk,khd->qhd", grad_scores, key_seq, preferred_element_type=jnp.float32
        ).astype(jnp.bfloat16)
        grad_key_seq = jnp.einsum(
            "hqk,qhd->khd", grad_scores, query_seq, preferred_element_type=jnp.float32
        ).astype(jnp.bfloat16)
        table_acc = table_acc + contract_cols(grad_scores.reshape(heads, SEQ * SEQ), onehot_table)
        return (table_acc, (grad_query_seq, grad_key_seq, grad_value_seq))

    table_start = jnp.zeros((heads, bucket_bias_matrix.shape[0]), jnp.float32)
    table_local, (grad_query_seqs, grad_key_seqs, grad_value_seqs) = lax.scan(
        backward_block,
        table_start,
        (query_seqs, key_seqs, value_seqs, grad_mixed_seqs, log_totals, valid),
    )
    grad_query_rows = grad_query_seqs.reshape(slot_count, width)
    grad_key_rows = grad_key_seqs.reshape(slot_count, width)
    grad_value_rows = grad_value_seqs.reshape(slot_count, width)
    grad_query = contract_rows(normed_attn, grad_query_rows)
    grad_key = contract_rows(normed_attn, grad_key_rows)
    grad_value = contract_rows(normed_attn, grad_value_rows)
    grad_normed_attn = (
        contract_cols(grad_query_rows, full_query)
        + contract_cols(grad_key_rows, full_key)
        + contract_cols(grad_value_rows, full_value)
    )
    grad_through_attn, grad_gain_attn = rms_back(
        inputs_f, scale_attn, full_gain_attn.astype(jnp.float32), grad_normed_attn
    )
    grad_tokens = (grad_hidden + grad_through_attn).astype(jnp.bfloat16)
    half_attn = halves_of(grad_query, grad_key, grad_value, grad_attn_out).astype(jnp.bfloat16)
    half_in = halves_of(grad_ffn_in).astype(jnp.bfloat16)
    sums = [
        total * factor
        for total in (sum_by_chips if by_chips else sum_plain)(
            half_attn, half_in, grad_ffn_out.astype(jnp.bfloat16)
        )
    ]
    small = sum_everywhere(
        jnp.concatenate(
            [grad_gain_attn, feedforward_gain_gradient, table_local.T.reshape(-1)]
        ).reshape(-1, 128)
    )
    small = small.reshape(-1) * factor
    shard = gain_attn.shape[0]
    return (
        output,
        grad_tokens,
        lax.dynamic_slice_in_dim(small, me * shard, shard),
        sums[0],
        sums[1],
        sums[2],
        sums[3],
        lax.dynamic_slice_in_dim(small, width + me * shard, shard),
        sums[4],
        sums[5],
        small[2 * width :].reshape(bucket_bias_matrix.shape),
    )


def solution(mesh):
    placed = (
        P("fsdp", None),
        P("fsdp", None),
        P("fsdp"),
        P("fsdp", None),
        P("fsdp", None),
        P("fsdp", None),
        P("fsdp", None),
        P("fsdp"),
        P("fsdp", None),
        P("fsdp", None),
        P(),
        P("fsdp", None),
    )
    return jax.shard_map(
        per_device,
        mesh=mesh,
        in_specs=placed,
        out_specs=(
            P("fsdp", None),
            P("fsdp", None),
            P("fsdp"),
            P("fsdp", None),
            P("fsdp", None),
            P("fsdp", None),
            P("fsdp", None),
            P("fsdp"),
            P("fsdp", None),
            P("fsdp", None),
            P(),
        ),
        check_vma=False,
    )
```

```python
import functools
import math

import jax
import jax.numpy as jnp
import numpy as np
from jax import lax
from jax.experimental import pallas as pl
from jax.experimental.pallas import tpu as pltpu
from jax.sharding import PartitionSpec as P

NB = 32
MAXD = 128
SEQ = 512
MIB = 1024 * 1024


def bucket_ids(span_length):
    offset = np.arange(span_length)[None, :] - np.arange(span_length)[:, None]
    half_count = NB // 2
    exact_count = half_count // 2
    result = np.where(offset > 0, half_count, 0)
    distance = np.abs(offset)
    spread = exact_count + np.floor(
        np.log(np.maximum(distance, 1) / exact_count)
        / math.log(MAXD / exact_count)
        * (half_count - exact_count)
    )
    spread = np.minimum(spread, half_count - 1)
    result = result + np.where(distance < exact_count, distance, spread)
    return result.astype(np.int32)


def flip(mask, count):
    return [(i, i ^ mask) for i in range(count)]


def swap(array, mask):
    return lax.ppermute(array, "fsdp", flip(mask, lax.axis_size("fsdp")))


def gather_chips(unit):
    line = lax.axis_size("fsdp") // 8
    half = line // 2
    near = jnp.stack([unit] + [swap(unit, 8 * hop) for hop in range(1, line)])
    over_x, over_y = swap(near, 2), swap(near, 4)
    return (near, over_x, over_y, swap(over_y[:half], 2), swap(over_x[half:], 4))


def chip_distances():
    line = lax.axis_size("fsdp") // 8
    half = line // 2
    blocks = []
    for part, (plane, first, last) in enumerate(
        ((0, 0, line), (1, 0, line), (2, 0, line), (3, 0, half), (3, half, line))
    ):
        blocks += [(part, hop - first, 4 * hop + plane) for hop in range(first, last)]
    return blocks


def scatter_chips(send, keep):
    line = keep.shape[1]
    half = line // 2

    def add(*terms):
        return sum(term.astype(jnp.float32) for term in terms)

    def low(value):
        return value.astype(jnp.bfloat16)

    both = low(add(keep, swap(send, 1)))
    via_x, via_y = swap(both[3, :half], 2), swap(both[3, half:], 4)
    x_low, y_high = swap(both[1, :half], 2), swap(both[2, half:], 4)
    y_low = swap(low(add(both[2, :half], via_x)), 4)
    x_high = swap(low(add(both[1, half:], via_y)), 2)
    total = jnp.concatenate(
        [low(add(both[0, :half], x_low, y_low)), low(add(both[0, half:], x_high, y_high))]
    )
    return add(total[0], *[swap(total[hop], 8 * hop) for hop in range(1, line)])


def both_cores(parts):
    return parts + tuple(swap(part, 1) for part in parts)


def chip_unit(shard, core):
    half = shard.shape[1] // 2
    mine = lax.dynamic_slice_in_dim(shard, core * half, half, 1)
    other = swap(lax.dynamic_slice_in_dim(shard, (1 - core) * half, half, 1), 1)
    return jnp.where(
        core == 0, jnp.concatenate([mine, other], 0), jnp.concatenate([other, mine], 0)
    )


def own_rows(chip_sum, core):
    rows = chip_sum.shape[0] // 2
    mine = lax.dynamic_slice_in_dim(chip_sum, core * rows, rows, 0)
    other = swap(lax.dynamic_slice_in_dim(chip_sum, (1 - core) * rows, rows, 0), 1)
    return mine, other


def join_columns(mine, other, core):
    return jnp.where(
        core == 0, jnp.concatenate([mine, other], 1), jnp.concatenate([other, mine], 1)
    )


def halves_of(*arrays):
    return jnp.stack(
        [
            jnp.concatenate(
                [
                    array[:, part * array.shape[1] // 2 : (part + 1) * array.shape[1] // 2]
                    for array in arrays
                ],
                1,
            )
            for part in range(2)
        ]
    )


def sum_plain(half_attn, half_in, grad_out):
    side = half_attn.shape[-1] // 4

    def owned(array):
        return lax.psum_scatter(
            array.astype(jnp.float32), "fsdp", scatter_dimension=0, tiled=True
        )

    grads = [
        jnp.concatenate([part[0], part[1]], 1)
        for part in [half_attn[:, :, k * side : (k + 1) * side] for k in range(4)] + [half_in]
    ]
    return [owned(grad) for grad in grads + [grad_out]]


def sum_everywhere(vector):
    mask = 1
    while mask < lax.axis_size("fsdp"):
        vector = vector + swap(vector, mask)
        mask *= 2
    return vector


def nn(left, right):
    return lax.dot_general(
        left, right, (((1,), (0,)), ((), ())), preferred_element_type=jnp.float32
    )


def nt(left, right):
    return lax.dot_general(
        left, right, (((1,), (1,)), ((), ())), preferred_element_type=jnp.float32
    )


def tn(left, right):
    return lax.dot_general(
        left, right, (((0,), (0,)), ((), ())), preferred_element_type=jnp.float32
    )


def low(value):
    return value.astype(jnp.bfloat16)


def wide(value):
    return value.astype(jnp.float32)


def norm_scale(values):
    return lax.rsqrt(jnp.mean(values * values, axis=-1, keepdims=True) + 1e-06)


def rms_back(scaled, scale, gain, grad_normed):
    weighted = grad_normed * gain
    return scale * (weighted - scaled * jnp.mean(weighted * scaled, axis=-1, keepdims=True))


IN_HBM = pl.BlockSpec(memory_space=pl.ANY)
IN_SMEM = pl.BlockSpec(memory_space=pltpu.SMEM)
IN_VMEM = pl.BlockSpec(memory_space=pltpu.VMEM)


def cost(flops, bytes_moved):
    return pl.CostEstimate(flops=flops, bytes_accessed=bytes_moved, transcendentals=0)


def plan(me, rows, by_chips, side, per_core):
    chip, core = me // 2, me % 2
    if not by_chips:
        return []
    count = 5
    found = []
    for part, index, distance in chip_distances():
        number = chip ^ distance
        if per_core:
            number = number * 2 + (core ^ side)
        found.append((side * count + part, index, pl.multiple_of(number * rows, 16)))
    return found


def column_copies(me, sources, target, sems, side, by_chips, columns):
    first, last = columns
    if not by_chips:
        half = (me % 2) ^ side
        return [
            pltpu.make_async_copy(sources[0].at[half, :, pl.ds(first, last - first)], target, sems.at[0])
        ]
    rows = sources[0].shape[1]
    return [
        pltpu.make_async_copy(
            sources[part].at[index, :, pl.ds(first, last - first)],
            target.at[pl.ds(start, rows), :],
            sems.at[number],
        )
        for number, (part, index, start) in enumerate(plan(me, rows, True, side, False))
    ]


def row_copies(me, sources, target, sems, side, by_chips):
    if not by_chips:
        half = target.shape[0] // 2
        where = pl.ds(side * half, half)
        return [pltpu.make_async_copy(sources[0].at[where, :], target.at[where, :], sems.at[0])]
    rows = sources[0].shape[1]
    return [
        pltpu.make_async_copy(
            sources[part].at[index], target.at[pl.ds(start, rows), :], sems.at[number]
        )
        for number, (part, index, start) in enumerate(plan(me, rows, True, side, True))
    ]


def start_all(copies):
    for copy in copies:
        copy.start()


def wait_all(copies):
    for copy in copies:
        copy.wait()


def half_copies(me, tile, targets, sems, side, by_chips, columns):
    first, count = columns
    if not by_chips:
        half = (me % 2) ^ side
        return [
            pltpu.make_async_copy(tile, targets[0].at[half, :, pl.ds(first, count)], sems.at[0])
        ]
    planes, line, rows = targets[side].shape[:3]
    chip = me // 2
    return [
        pltpu.make_async_copy(
            tile.at[pl.ds(pl.multiple_of((chip ^ (4 * hop + plane)) * rows, 16), rows), :],
            targets[side].at[plane, hop, :, pl.ds(first, count)],
            sems.at[plane * line + hop],
        )
        for plane in range(planes)
        for hop in range(line)
    ]


def strip_copies(me, tile, targets, sems, strip, by_chips):
    if not by_chips:
        rows = tile.shape[0]
        return [
            pltpu.make_async_copy(
                tile, targets[0].at[pl.ds(pl.multiple_of(strip * rows, 16), rows), :], sems.at[0]
            )
        ]
    planes, line, rows = targets[0].shape[:3]
    chip, core = me // 2, me % 2
    return [
        pltpu.make_async_copy(
            tile.at[
                pl.ds(pl.multiple_of((((chip % 4) ^ plane) * 2 + (core ^ side)) * rows, 16), rows), :
            ],
            targets[side].at[plane, (chip // 4) ^ strip],
            sems.at[side * planes + plane],
        )
        for side in range(2)
        for plane in range(planes)
    ]


def bias_planes(table):
    heads = table.shape[1]
    ids = bucket_ids(SEQ)
    flat = np.concatenate([ids[:, 0], ids[0, :1], ids[0, :0:-1]])
    onehot = (np.arange(table.shape[0])[:, None] == flat[None, :]).astype(np.float32)
    rows = lax.dot_general(
        wide(table), jnp.asarray(onehot), (((0,), (0,)), ((), ())), precision=lax.Precision.HIGHEST
    )

    def kernel(rows_ref, plane_ref):
        row = rows_ref[pl.ds(pl.program_id(0), 1), :]
        spread = jnp.broadcast_to(row, (SEQ, 2 * SEQ))
        moved = pltpu.roll(spread, 0, 1, stride=1, stride_axis=0)
        plane_ref[0] = low(moved[:, :SEQ])

    return pl.pallas_call(
        kernel,
        grid=(heads,),
        out_shape=jax.ShapeDtypeStruct((heads, SEQ, SEQ), jnp.bfloat16),
        in_specs=[IN_VMEM],
        out_specs=pl.BlockSpec((1, SEQ, SEQ), lambda head: (head, 0, 0)),
        compiler_params=pltpu.CompilerParams(vmem_limit_bytes=24 * MIB),
    )(rows)


def line_ids():
    ids = bucket_ids(SEQ)
    ahead = (np.arange(2 * SEQ)[None, :] - np.arange(8)[:, None] - (SEQ - 128) + SEQ) % (2 * SEQ)
    ahead = ahead - SEQ
    return np.where(ahead >= 0, ids[np.maximum(ahead, 0), 0], ids[0, np.minimum(-ahead, SEQ - 1)])


def project_qkv(place, tokens, sources, by_chips):
    slots, width = tokens.shape
    side_cols = width // 2
    packed = sources[0].shape[-1]
    block = 256
    steps = slots // block

    def kernel(place_ref, x_ref, *refs):
        ins = refs[: len(sources)]
        q_ref, k_ref, v_ref, gains_ref, weights, normed, sems = refs[len(sources) :]
        side, step = pl.program_id(0), pl.program_id(1)
        me = place_ref[0]

        def copies(which):
            return column_copies(
                me, ins, weights.at[which], sems.at[which], which, by_chips, (0, packed)
            )

        @pl.when((side == 0) & (step == 0))
        def _():
            start_all(copies(0))
            start_all(copies(1))
            wait_all(copies(0))
            gains = jnp.transpose(wide(weights[0, :, 3 * side_cols :]))
            gains_ref[...] = gains[:8]

            def normalise(index, carry):
                where = pl.ds(pl.multiple_of(index * 128, 128), 128)
                rows = wide(x_ref[where, :])
                normed[where, :] = low(rows * norm_scale(rows) * gains[:1])
                return carry

            lax.fori_loop(0, slots // 128, normalise, 0)

        @pl.when((side == 1) & (step == 0))
        def _():
            wait_all(copies(1))

        rows = normed[pl.ds(pl.multiple_of(step * block, block), block), :]
        for part, out in enumerate((q_ref, k_ref, v_ref)):
            out[...] = low(nn(rows, weights[side, :, part * side_cols : (part + 1) * side_cols]))

    flat = jax.ShapeDtypeStruct((slots, width), jnp.bfloat16)
    out_block = pl.BlockSpec(
        (block, side_cols), lambda side, step, place_ref: (step, (place_ref[0] % 2) ^ side)
    )
    return pl.pallas_call(
        kernel,
        grid_spec=pltpu.PrefetchScalarGridSpec(
            num_scalar_prefetch=1,
            grid=(2, steps),
            in_specs=[pl.BlockSpec((slots, width), lambda side, step, place_ref: (0, 0))]
            + [IN_HBM] * len(sources),
            out_specs=[out_block] * 3
            + [pl.BlockSpec((8, width), lambda side, step, place_ref: (0, 0))],
            scratch_shapes=[
                pltpu.VMEM((2, width, packed), jnp.bfloat16),
                pltpu.VMEM((slots, width), jnp.bfloat16),
                pltpu.SemaphoreType.DMA((2, 16)),
            ],
        ),
        out_shape=[flat] * 3 + [jax.ShapeDtypeStruct((8, width), jnp.float32)],
        compiler_params=pltpu.CompilerParams(vmem_limit_bytes=40 * MIB),
        cost_estimate=cost(6 * slots * width * width, 12 * slots * width),
    )(place, tokens, *sources)


def attend(valid, query, key, value, planes, first, count):
    slots, width = query.shape
    seqs = slots // SEQ
    heads = planes.shape[0]
    pair_cols = 2 * width // heads
    head_size = pair_cols // 2
    piece = 256

    def kernel(valid_ref, q_ref, k_ref, v_ref, planes_ref, out_ref, prob_ref):
        seq = pl.program_id(1)
        limit = valid_ref[seq]
        permitted = lax.broadcasted_iota(jnp.int32, (SEQ, 1), 0) < limit
        own_lane = lax.broadcasted_iota(jnp.int32, (1, pair_cols), 1) < head_size
        keys, values = k_ref[...], v_ref[...]
        zero = jnp.zeros((), jnp.bfloat16)
        value_cols = low(jnp.transpose(wide(values)))
        for part in range(SEQ // piece):
            where = slice(part * piece, (part + 1) * piece)
            mixed = []
            for head in range(2):
                mask = own_lane if head == 0 else ~own_lane
                scores = nt(jnp.where(mask, keys, zero), q_ref[where, :])
                scores = scores + wide(planes_ref[head, :, where])
                scores = jnp.where(permitted, scores, -1e30)
                peak = jnp.max(scores, axis=0, keepdims=True)
                raised = jnp.exp(scores - peak)
                total = jnp.sum(raised, axis=0, keepdims=True)
                prob = low(raised * (1.0 / total))
                prob_ref[0, head, :, where] = prob
                mixed.append(nn(value_cols[head * head_size : (head + 1) * head_size], prob))
            out_ref[where, :] = low(jnp.transpose(jnp.concatenate(mixed, 0)))

    def cols(pair, seq, valid_ref):
        return (seq, first + pair)

    block = pl.BlockSpec((SEQ, pair_cols), cols)
    return pl.pallas_call(
        kernel,
        grid_spec=pltpu.PrefetchScalarGridSpec(
            num_scalar_prefetch=1,
            grid=(count, seqs),
            in_specs=[
                block,
                block,
                block,
                pl.BlockSpec((2, SEQ, SEQ), lambda pair, seq, valid_ref: (first + pair, 0, 0)),
            ],
            out_specs=[
                pl.BlockSpec((SEQ, pair_cols), lambda pair, seq, valid_ref: (seq, pair)),
                pl.BlockSpec(
                    (1, 2, SEQ, SEQ), lambda pair, seq, valid_ref: (seq, pair, 0, 0)
                ),
            ],
        ),
        out_shape=[
            jax.ShapeDtypeStruct((slots, count * pair_cols), jnp.bfloat16),
            jax.ShapeDtypeStruct((seqs, 2 * count, SEQ, SEQ), jnp.bfloat16),
        ],
        compiler_params=pltpu.CompilerParams(vmem_limit_bytes=40 * MIB),
        cost_estimate=cost(count * slots * SEQ * 2048, count * slots * SEQ * 8),
    )(valid, query, key, value, planes)


def attend_back(query, key, value, grad_mixed, prob, first, count, heads):
    slots, width = query.shape
    seqs = slots // SEQ
    pair_cols = 2 * width // heads
    head_size = pair_cols // 2
    piece = 256

    def kernel(q_ref, k_ref, v_ref, g_ref, prob_ref, dq_ref, dk_ref, dv_ref, table_ref, planes):
        seq = pl.program_id(1)
        own_lane = lax.broadcasted_iota(jnp.int32, (1, pair_cols), 1) < head_size
        values = v_ref[...]
        zero = jnp.zeros((), jnp.bfloat16)
        key_cols = low(jnp.transpose(wide(k_ref[...])))
        dk, dv, dq = [], [], [[], []]
        for head in range(2):
            mask = own_lane if head == 0 else ~own_lane
            masked = jnp.where(mask, values, zero)
            sum_k = sum_v = 0.0
            for part in range(SEQ // piece):
                where = slice(part * piece, (part + 1) * piece)
                prob = prob_ref[0, head, :, where]
                grads = g_ref[where, :]
                sum_v += nn(prob, grads)
                prob = wide(prob)
                grad_prob = nt(masked, grads)
                weighted = prob * grad_prob
                dot = jnp.sum(weighted, axis=0, keepdims=True)
                grad_scores = weighted - prob * dot

                @pl.when(seq == 0)
                def _():
                    planes[head, :, where] = grad_scores

                @pl.when(seq > 0)
                def _():
                    planes[head, :, where] += grad_scores

                grad_scores = low(grad_scores)
                sum_k += nn(grad_scores, q_ref[where, :])
                dq[part].append(
                    nn(key_cols[head * head_size : (head + 1) * head_size], grad_scores)
                )
            dk.append(sum_k)
            dv.append(sum_v)
        dk_ref[...] = low(jnp.where(own_lane, dk[0], dk[1]))
        dv_ref[...] = low(jnp.where(own_lane, dv[0], dv[1]))
        for part in range(SEQ // piece):
            dq_ref[part * piece : (part + 1) * piece, :] = low(
                jnp.transpose(jnp.concatenate(dq[part], 0))
            )

        @pl.when(seq == seqs - 1)
        def _():
            for head in range(2):
                lined = jnp.zeros((8, 2 * SEQ), jnp.float32)
                for low_row in range(0, 128, 8):
                    frame = jnp.zeros((8, 2 * SEQ), jnp.float32)
                    for high_row in range(0, SEQ, 128):
                        rows = planes[head, high_row + low_row : high_row + low_row + 8, :]
                        ahead = SEQ - 128 - high_row
                        filled = [rows, jnp.zeros((8, SEQ - ahead), jnp.float32)]
                        if ahead:
                            filled = [jnp.zeros((8, ahead), jnp.float32)] + filled
                        frame = frame + jnp.concatenate(filled, 1)
                    if low_row:
                        frame = pltpu.roll(frame, 2 * SEQ - low_row, 1)
                    lined = lined + frame
                table_ref[0, head] = lined

    def cols(pair, seq):
        return (seq, first + pair)

    def own_cols(pair, seq):
        return (seq, pair)

    block = pl.BlockSpec((SEQ, pair_cols), cols)
    own_block = pl.BlockSpec((SEQ, pair_cols), own_cols)
    flat = jax.ShapeDtypeStruct((slots, count * pair_cols), jnp.bfloat16)
    return pl.pallas_call(
        kernel,
        grid=(count, seqs),
        in_specs=[
            block,
            block,
            block,
            block,
            pl.BlockSpec((1, 2, SEQ, SEQ), lambda pair, seq: (seq, pair, 0, 0)),
        ],
        out_specs=[own_block] * 3
        + [pl.BlockSpec((1, 2, 8, 2 * SEQ), lambda pair, seq: (pair, 0, 0, 0))],
        out_shape=[flat] * 3 + [jax.ShapeDtypeStruct((count, 2, 8, 2 * SEQ), jnp.float32)],
        scratch_shapes=[pltpu.VMEM((2, SEQ, SEQ), jnp.float32)],
        compiler_params=pltpu.CompilerParams(vmem_limit_bytes=40 * MIB),
        cost_estimate=cost(count * slots * SEQ * 4096, count * slots * SEQ * 8),
    )(query, key, value, grad_mixed, prob)


def feed_forward(place, tokens, attended, cotangent, gains, in_sources, out_sources, by_chips):
    slots, width = tokens.shape
    side_cols = width // 2
    hidden_cols = 2 * (in_sources[0].shape[-1] - side_cols)
    block = 256
    blocks = slots // block
    chunk = 768
    per_side = hidden_cols // 2 // chunk
    count_att = len(attended)
    root, bend = math.sqrt(2.0 / math.pi), 0.044715

    def kernel(place_ref, x_hbm, cot_hbm, gains_ref, *refs):
        refs = list(refs)

        def take(number):
            taken, refs[:] = refs[:number], refs[number:]
            return taken

        att_hbm, in_hbm, out_hbm = take(count_att), take(len(in_sources)), take(len(out_sources))
        y_hbm, grad_hbm, back_hbm = take(3)
        in_targets = take(2 if by_chips else 1)
        out_targets = take(2 if by_chips else 1)
        (gain_out,) = take(1)
        x, att, cot, w_o, w_in, w_out, hidden, normed, flipped = take(9)
        sum_y, sum_g, act, grad_pre, tile_in, tile_out = take(6)
        load_sems, o_sems, in_sems, out_sems, store_sems, tile_in_sems, tile_out_sems = take(7)
        me = place_ref[0]
        core = me % 2
        gain = gains_ref[1:2, :]

        def rows_of(index):
            return pl.ds(pl.multiple_of(index * block, block), block)

        loads = [
            pltpu.make_async_copy(x_hbm, x, load_sems.at[0]),
            pltpu.make_async_copy(cot_hbm, cot, load_sems.at[1]),
        ]
        cols = 0
        for number, source in enumerate(att_hbm):
            loads.append(
                pltpu.make_async_copy(
                    source, att.at[:, pl.ds(cols, source.shape[1])], load_sems.at[2 + number]
                )
            )
            cols += source.shape[1]
        o_loads, in_loads, out_loads = [], [], []
        for side in range(2):
            o_cols = pl.ds(pl.multiple_of((core ^ side) * side_cols, 128), side_cols)
            o_loads += column_copies(
                me, in_hbm, w_o.at[:, o_cols], o_sems.at[side], side, by_chips, (0, side_cols)
            )
            in_loads.append(
                column_copies(
                    me,
                    in_hbm,
                    w_in.at[side],
                    in_sems.at[side],
                    side,
                    by_chips,
                    (side_cols, in_sources[0].shape[-1]),
                )
            )
            out_loads += row_copies(me, out_hbm, w_out, out_sems.at[side], side, by_chips)
        start_all(loads)
        start_all(o_loads)
        start_all(in_loads[0])
        start_all(out_loads)
        start_all(in_loads[1])
        wait_all(loads)
        wait_all(o_loads)

        def before(index, carry):
            where = rows_of(index)
            value = wide(x[where, :]) + nn(att[where, :], w_o[...])
            hidden[where, :] = value
            rows = value * norm_scale(value) * gain
            normed[where, :] = low(rows)
            flipped[:, where] = low(jnp.transpose(rows))
            sum_y[where, :] = value
            sum_g[where, :] = jnp.zeros_like(value)
            return carry

        lax.fori_loop(0, blocks, before, 0)
        wait_all(in_loads[0])
        wait_all(out_loads)

        stores = []
        for side in range(2):
            if side:
                wait_all(in_loads[1])
            for part in range(per_side):
                number = side * per_side + part
                strip = (core ^ side) * per_side + part
                unit_rows = pl.ds(pl.multiple_of(strip * chunk, chunk), chunk)
                unit_cols = slice(part * chunk, (part + 1) * chunk)

                def through(index, carry):
                    where = rows_of(index)
                    pre = nn(normed[where, :], w_in[side, :, unit_cols])
                    square = pre * pre
                    slope = jnp.tanh(root * pre * (1.0 + bend * square))
                    opened = 0.5 * (1.0 + slope)
                    gate = opened + (0.5 * root) * pre * (1.0 - slope * slope) * (
                        1.0 + (3.0 * bend) * square
                    )
                    acted = low(pre * opened)
                    act[where, :] = acted
                    back = low(nt(cot[where, :], w_out[unit_rows, :]) * gate)
                    grad_pre[where, :] = back
                    sum_y[where, :] += nn(acted, w_out[unit_rows, :])
                    sum_g[where, :] += nt(back, w_in[side, :, unit_cols])
                    return carry

                lax.fori_loop(0, blocks, through, 0)
                slot = number % 2
                if number >= 2:
                    wait_all(stores[number - 2])
                for third in range(3):
                    some = slice(third * chunk // 3, (third + 1) * chunk // 3)
                    tile_out[slot, some, :] = low(tn(act[:, some], cot[...]))
                for third in range(3):
                    some = slice(third * width // 3, (third + 1) * width // 3)
                    tile_in[slot, some, :] = low(nn(flipped[some, :], grad_pre[...]))
                copies = strip_copies(
                    me, tile_out.at[slot], out_targets, tile_out_sems.at[slot], strip, by_chips
                ) + half_copies(
                    me,
                    tile_in.at[slot],
                    in_targets,
                    tile_in_sems.at[slot],
                    side,
                    by_chips,
                    (side_cols + part * chunk, chunk),
                )
                start_all(copies)
                stores.append(copies)

        def after(index, carry):
            where = rows_of(index)
            value = hidden[where, :]
            normed[where, :] = low(sum_y[where, :])
            scale = norm_scale(value)
            scaled = value * scale
            grad = sum_g[where, :]
            gains_sum = carry + jnp.sum(grad * scaled, axis=0, keepdims=True)
            grad = wide(cot[where, :]) + rms_back(scaled, scale, gain, grad)
            sum_g[where, :] = grad
            branch = low(grad)
            grad_pre[where, :] = branch
            act[where, :] = low(nt(branch, w_o[...]))
            return gains_sum

        gain_sum = lax.fori_loop(0, blocks, after, jnp.zeros((1, width), jnp.float32))
        gain_out[...] = jnp.broadcast_to(gain_sum, gain_out.shape)
        last = [
            pltpu.make_async_copy(normed, y_hbm, store_sems.at[0]),
            pltpu.make_async_copy(sum_g, grad_hbm, store_sems.at[1]),
            pltpu.make_async_copy(act, back_hbm, store_sems.at[2]),
        ]
        start_all(last)
        slot = len(stores) % 2
        wait_all(stores[-2])
        for third in range(3):
            some = slice(third * width // 3, (third + 1) * width // 3)
            tile_in[slot, some, :] = low(tn(att[:, some], grad_pre[...]))
        copies = []
        for side in range(2):
            o_cols = pl.ds(pl.multiple_of((core ^ side) * side_cols, 128), side_cols)
            copies += half_copies(
                me,
                tile_in.at[slot, :, o_cols],
                in_targets,
                o_sems.at[side],
                side,
                by_chips,
                (0, side_cols),
            )
        start_all(copies)
        wait_all(stores[-1])
        wait_all(copies)
        wait_all(last)

    sums = jax.ShapeDtypeStruct
    flat = sums((slots, width), jnp.bfloat16)
    packed = in_sources[0].shape[-1]
    devices = lax.axis_size("fsdp")
    if by_chips:
        line = devices // 8
        in_shapes = [sums((4, line, width // (4 * line), packed), jnp.bfloat16)] * 2
        out_shapes = [sums((4, line, hidden_cols // devices, width), jnp.bfloat16)] * 2
    else:
        in_shapes = [sums((2, width, packed), jnp.bfloat16)]
        out_shapes = [sums((hidden_cols, width), jnp.bfloat16)]
    outs = [flat, sums((slots, width), jnp.float32), flat] + in_shapes + out_shapes
    bf16, f32 = jnp.bfloat16, jnp.float32
    result = pl.pallas_call(
        kernel,
        out_shape=outs + [sums((8, width), f32)],
        in_specs=[IN_SMEM, IN_HBM, IN_HBM, IN_VMEM]
        + [IN_HBM] * (count_att + len(in_sources) + len(out_sources)),
        out_specs=[IN_HBM] * len(outs) + [IN_VMEM],
        scratch_shapes=[
            pltpu.VMEM((slots, width), bf16),
            pltpu.VMEM((slots, width), bf16),
            pltpu.VMEM((slots, width), bf16),
            pltpu.VMEM((width, width), bf16),
            pltpu.VMEM((2, width, hidden_cols // 2), bf16),
            pltpu.VMEM((hidden_cols, width), bf16),
            pltpu.VMEM((slots, width), f32),
            pltpu.VMEM((slots, width), bf16),
            pltpu.VMEM((width, slots), bf16),
            pltpu.VMEM((slots, width), f32),
            pltpu.VMEM((slots, width), f32),
            pltpu.VMEM((slots, chunk), bf16),
            pltpu.VMEM((slots, chunk), bf16),
            pltpu.VMEM((2, width, chunk), bf16),
            pltpu.VMEM((2, chunk, width), bf16),
            pltpu.SemaphoreType.DMA((2 + count_att,)),
            pltpu.SemaphoreType.DMA((2, 16)),
            pltpu.SemaphoreType.DMA((2, 16)),
            pltpu.SemaphoreType.DMA((2, 16)),
            pltpu.SemaphoreType.DMA((3,)),
            pltpu.SemaphoreType.DMA((2, 16)),
            pltpu.SemaphoreType.DMA((2, 8)),
        ],
        compiler_params=pltpu.CompilerParams(vmem_limit_bytes=60 * MIB),
        cost_estimate=cost(
            slots * width * (12 * hidden_cols + 6 * width), 60 * MIB
        ),
    )(place, tokens, cotangent, gains, *attended, *in_sources, *out_sources)
    split = 3 + len(in_shapes)
    return result[:3], result[3:split], result[split:-1], result[-1][0]


def project_back(place, tokens, gains, grad_hidden, grads, sources, by_chips):
    slots, width = tokens.shape
    side_cols = width // 2
    packed = sources[0].shape[-1]
    flat_grads = [grad for half in grads for grad in half]
    block = 256
    blocks = slots // block

    def kernel(place_ref, x_hbm, gh_hbm, gains_ref, *refs):
        refs = list(refs)

        def take(number):
            taken, refs[:] = refs[:number], refs[number:]
            return taken

        g_hbm, w_hbm = take(len(flat_grads)), take(len(sources))
        (out_hbm,) = take(1)
        targets = take(2 if by_chips else 1)
        (gain_out,) = take(1)
        x, grad, weights, parts, flipped, out, tile = take(7)
        load_sems, w_sems, tile_sems, out_sem = take(4)
        me = place_ref[0]
        core = me % 2
        gain = gains_ref[0:1, :]

        def rows_of(index):
            return pl.ds(pl.multiple_of(index * block, block), block)

        loads = [
            pltpu.make_async_copy(x_hbm, x, load_sems.at[0]),
            pltpu.make_async_copy(gh_hbm, grad, load_sems.at[1]),
        ]
        for half in range(2):
            for part in range(3):
                loads.append(
                    pltpu.make_async_copy(
                        g_hbm[3 * half + part],
                        parts.at[half, :, pl.ds(part * side_cols, side_cols)],
                        load_sems.at[2 + 3 * half + part],
                    )
                )
        w_loads = [
            column_copies(
                me, w_hbm, weights.at[side], w_sems.at[side], side, by_chips, (0, packed)
            )
            for side in range(2)
        ]
        start_all(loads)
        start_all(w_loads[0])
        start_all(w_loads[1])
        wait_all(loads)

        def flip(index, carry):
            where = rows_of(index)
            rows = wide(x[where, :])
            flipped[:, where] = low(jnp.transpose(rows * norm_scale(rows) * gain))
            return carry

        lax.fori_loop(0, blocks, flip, 0)
        copies = []
        for side in range(2):
            half = core ^ side
            for third in range(3):
                some = slice(third * width // 3, (third + 1) * width // 3)
                tile[side, some, :] = low(nn(flipped[some, :], parts[half]))
            copies.append(
                half_copies(
                    me,
                    tile.at[side],
                    targets,
                    tile_sems.at[side],
                    side,
                    by_chips,
                    (0, 3 * side_cols),
                )
            )
            start_all(copies[-1])
        wait_all(w_loads[0])
        wait_all(w_loads[1])

        def after(index, carry):
            where = rows_of(index)
            grad_normed = nt(parts[core, where, :], weights[0, :, : 3 * side_cols]) + nt(
                parts[1 - core, where, :], weights[1, :, : 3 * side_cols]
            )
            rows = wide(x[where, :])
            scale = norm_scale(rows)
            scaled = rows * scale
            out[where, :] = low(
                grad[where, :] + rms_back(scaled, scale, gain, grad_normed)
            )
            return carry + jnp.sum(grad_normed * scaled, axis=0, keepdims=True)

        gain_sum = lax.fori_loop(0, blocks, after, jnp.zeros((1, width), jnp.float32))
        gain_out[...] = jnp.broadcast_to(gain_sum, gain_out.shape)
        last = pltpu.make_async_copy(out, out_hbm, out_sem.at[0])
        last.start()
        wait_all(copies[0])
        wait_all(copies[1])
        last.wait()

    sums = jax.ShapeDtypeStruct
    if by_chips:
        line = lax.axis_size("fsdp") // 8
        shapes = [sums((4, line, width // (4 * line), 3 * side_cols), jnp.bfloat16)] * 2
    else:
        shapes = [sums((2, width, 3 * side_cols), jnp.bfloat16)]
    bf16, f32 = jnp.bfloat16, jnp.float32
    result = pl.pallas_call(
        kernel,
        out_shape=[sums((slots, width), bf16)] + shapes + [sums((8, width), f32)],
        in_specs=[IN_SMEM, IN_HBM, IN_HBM, IN_VMEM]
        + [IN_HBM] * (len(flat_grads) + len(sources)),
        out_specs=[IN_HBM] * (1 + len(shapes)) + [IN_VMEM],
        scratch_shapes=[
            pltpu.VMEM((slots, width), bf16),
            pltpu.VMEM((slots, width), f32),
            pltpu.VMEM((2, width, packed), bf16),
            pltpu.VMEM((2, slots, 3 * side_cols), bf16),
            pltpu.VMEM((width, slots), bf16),
            pltpu.VMEM((slots, width), bf16),
            pltpu.VMEM((2, width, 3 * side_cols), bf16),
            pltpu.SemaphoreType.DMA((8,)),
            pltpu.SemaphoreType.DMA((2, 16)),
            pltpu.SemaphoreType.DMA((2, 16)),
            pltpu.SemaphoreType.DMA((1,)),
        ],
        compiler_params=pltpu.CompilerParams(vmem_limit_bytes=56 * MIB),
        cost_estimate=cost(12 * slots * width * width, 30 * MIB),
    )(place, tokens, grad_hidden, gains, *flat_grads, *sources)
    return result[0], result[1:-1], result[-1][0]


def gather_by_chips(
    gain_attn, w_query, w_key, w_value, w_attn_out, gain_ffn, w_ffn_in, w_ffn_out
):
    core = lax.axis_index("fsdp") % 2
    gains = jnp.pad(jnp.stack([gain_attn, gain_ffn], 1), ((0, 0), (0, 126)))
    other_gains = swap(gains, 1)
    chip_gains = jnp.where(
        core == 0,
        jnp.concatenate([gains, other_gains], 0),
        jnp.concatenate([other_gains, gains], 0),
    )
    unit_qkv = jnp.concatenate(
        [chip_unit(w_query, core), chip_unit(w_key, core), chip_unit(w_value, core), chip_gains], 1
    )
    unit_in = jnp.concatenate([chip_unit(w_attn_out, core), chip_unit(w_ffn_in, core)], 1)
    return (
        both_cores(gather_chips(unit_qkv)),
        both_cores(gather_chips(unit_in)),
        both_cores(gather_chips(w_ffn_out)),
    )


def gather_plain(
    gain_attn, w_query, w_key, w_value, w_attn_out, gain_ffn, w_ffn_in, w_ffn_out
):
    def full(shard):
        return lax.all_gather(shard, "fsdp", axis=0, tiled=True)

    gains = jnp.pad(jnp.stack([full(gain_attn), full(gain_ffn)], 1), ((0, 0), (0, 126)))
    return (
        (halves_of(full(w_query), full(w_key), full(w_value), jnp.concatenate([gains, gains], 1)),),
        (halves_of(full(w_attn_out), full(w_ffn_in)),),
        (full(w_ffn_out),),
    )


def chip_unit(shard, core):
    half = shard.shape[1] // 2
    mine = lax.dynamic_slice_in_dim(shard, core * half, half, 1)
    other = swap(lax.dynamic_slice_in_dim(shard, (1 - core) * half, half, 1), 1)
    return jnp.where(
        core == 0, jnp.concatenate([mine, other], 0), jnp.concatenate([other, mine], 0)
    )


def owned_columns(chip_sum, core, parts):
    mine, other = own_rows(chip_sum, core)
    joined, first = [], 0
    for count in parts:
        joined.append(
            join_columns(mine[:, first : first + count], other[:, first : first + count], core)
        )
        first += count
    return joined


def per_device(
    tokens,
    lengths,
    gain_attn,
    w_query,
    w_key,
    w_value,
    w_attn_out,
    gain_ffn,
    w_ffn_in,
    w_ffn_out,
    bucket_bias_matrix,
    cotangent,
):
    slot_count, width = tokens.shape
    heads = bucket_bias_matrix.shape[1]
    devices = lax.axis_size("fsdp")
    valid = jnp.sum(lengths, axis=-1)
    factor = 1.0 / math.sqrt(slot_count * devices)
    me = lax.axis_index("fsdp")
    core = me % 2
    place = me.astype(jnp.int32)[None]
    side = width // 2
    by_chips = devices == 32
    in_qkv, in_ffn, in_out = (gather_by_chips if by_chips else gather_plain)(
        gain_attn, w_query, w_key, w_value, w_attn_out, gain_ffn, w_ffn_in, w_ffn_out
    )
    planes = bias_planes(bucket_bias_matrix)
    query, key, value, gains = project_qkv(place, tokens, in_qkv, by_chips)
    pairs = heads // 2
    first_half = attend(valid, query, key, value, planes, 0, pairs // 2)
    second_half = attend(valid, query, key, value, planes, pairs // 2, pairs // 2)
    attended, probs = zip(first_half, second_half)
    (output, grad_hidden, grad_attended), part_in, part_out, gain_ffn_sum = feed_forward(
        place, tokens, attended, cotangent, gains, in_ffn, in_out, by_chips
    )
    backs = [
        attend_back(
            query, key, value, grad_attended, probs[half], half * pairs // 2, pairs // 2, heads
        )
        for half in range(2)
    ]
    diagonals = jnp.concatenate([back[3].reshape(heads // 2, 16 * SEQ) for back in backs])
    grad_tokens, part_qkv, gain_attn_sum = project_back(
        place, tokens, gains, grad_hidden, [back[:3] for back in backs], in_qkv, by_chips
    )
    onehot = (line_ids().reshape(-1)[:, None] == np.arange(NB)[None, :]).astype(np.float32)
    table = lax.dot_general(
        jnp.asarray(onehot),
        diagonals,
        (((0,), (1,)), ((), ())),
        precision=lax.Precision.HIGHEST,
    )
    if by_chips:
        sum_out = scatter_chips(part_out[1], part_out[0])
        sum_o, sum_in = owned_columns(
            scatter_chips(part_in[1], part_in[0]), core, (side, part_in[0].shape[-1] - side)
        )
        sum_q, sum_k, sum_v = owned_columns(
            scatter_chips(part_qkv[1], part_qkv[0]), core, (side, side, side)
        )
        sums = [sum_q, sum_k, sum_v, sum_o, sum_in, sum_out]
    else:
        sums = sum_plain(
            jnp.concatenate([part_qkv[0], part_in[0][:, :, :side]], 2),
            part_in[0][:, :, side:],
            part_out[0],
        )
    sums = [total * factor for total in sums]
    small = sum_everywhere(
        jnp.concatenate([gain_attn_sum, gain_ffn_sum, table.reshape(-1)]).reshape(-1, 128)
    )
    small = small.reshape(-1) * factor
    shard = gain_attn.shape[0]
    return (
        output,
        grad_tokens,
        lax.dynamic_slice_in_dim(small, me * shard, shard),
        sums[0],
        sums[1],
        sums[2],
        sums[3],
        lax.dynamic_slice_in_dim(small, width + me * shard, shard),
        sums[4],
        sums[5],
        small[2 * width :].reshape(bucket_bias_matrix.shape),
    )


def solution(mesh):
    placed = (
        P("fsdp", None),
        P("fsdp", None),
        P("fsdp"),
        P("fsdp", None),
        P("fsdp", None),
        P("fsdp", None),
        P("fsdp", None),
        P("fsdp"),
        P("fsdp", None),
        P("fsdp", None),
        P(),
        P("fsdp", None),
    )
    return jax.shard_map(
        per_device,
        mesh=mesh,
        in_specs=placed,
        out_specs=(
            P("fsdp", None),
            P("fsdp", None),
            P("fsdp"),
            P("fsdp", None),
            P("fsdp", None),
            P("fsdp", None),
            P("fsdp", None),
            P("fsdp"),
            P("fsdp", None),
            P("fsdp", None),
            P(),
        ),
        check_vma=False,
    )
```

```python
import functools
import math

import jax
import jax.numpy as jnp
import numpy as np
from jax import lax
from jax.experimental import pallas as pl
from jax.experimental.pallas import tpu as pltpu
from jax.sharding import PartitionSpec as P

NB = 32
MAXD = 128
SEQ = 512
MIB = 1024 * 1024


def bucket_ids(span_length):
    offset = np.arange(span_length)[None, :] - np.arange(span_length)[:, None]
    half_count = NB // 2
    exact_count = half_count // 2
    result = np.where(offset > 0, half_count, 0)
    distance = np.abs(offset)
    spread = exact_count + np.floor(
        np.log(np.maximum(distance, 1) / exact_count)
        / math.log(MAXD / exact_count)
        * (half_count - exact_count)
    )
    spread = np.minimum(spread, half_count - 1)
    result = result + np.where(distance < exact_count, distance, spread)
    return result.astype(np.int32)


def flip(mask, count):
    return [(i, i ^ mask) for i in range(count)]


def swap(array, mask):
    return lax.ppermute(array, "fsdp", flip(mask, lax.axis_size("fsdp")))


def gather_line(unit):
    line = lax.axis_size("fsdp") // 8
    return (unit,) + tuple(swap(unit, 8 * hop) for hop in range(1, line))


def gather_plane(near):
    return swap(near, 2), swap(near, 4)


def gather_far(first, second):
    return swap(first, 2), swap(second, 4)


def chip_distances():
    line = lax.axis_size("fsdp") // 8
    half = line // 2
    blocks = []
    for part, (plane, first, last) in enumerate(
        ((0, 0, line), (1, 0, line), (2, 0, line), (3, 0, half), (3, half, line))
    ):
        blocks += [(part, hop - first, 4 * hop + plane) for hop in range(first, last)]
    return blocks


def add(*terms):
    return sum(term.astype(jnp.float32) for term in terms)


def scatter_first(sends):
    return swap(sends[0], 2), swap(sends[1], 4)


def scatter_second(sends):
    return swap(sends[0], 4), swap(sends[1], 2)


def scatter_line(sums):
    return (sums[0],) + tuple(swap(total, 8 * hop) for hop, total in enumerate(sums) if hop)


def both_cores(parts):
    return parts + tuple(swap(part, 1) for part in parts)


def halves_of(*arrays):
    return jnp.stack(
        [
            jnp.concatenate(
                [
                    array[:, part * array.shape[1] // 2 : (part + 1) * array.shape[1] // 2]
                    for array in arrays
                ],
                1,
            )
            for part in range(2)
        ]
    )


def sum_plain(half_attn, half_in, grad_out):
    side = half_attn.shape[-1] // 4

    def owned(array):
        return lax.psum_scatter(
            array.astype(jnp.float32), "fsdp", scatter_dimension=0, tiled=True
        )

    grads = [
        jnp.concatenate([part[0], part[1]], 1)
        for part in [half_attn[:, :, k * side : (k + 1) * side] for k in range(4)] + [half_in]
    ]
    return [owned(grad) for grad in grads + [grad_out]]


def nn(left, right):
    return lax.dot_general(
        left, right, (((1,), (0,)), ((), ())), preferred_element_type=jnp.float32
    )


def nt(left, right):
    return lax.dot_general(
        left, right, (((1,), (1,)), ((), ())), preferred_element_type=jnp.float32
    )


def tn(left, right):
    return lax.dot_general(
        left, right, (((0,), (0,)), ((), ())), preferred_element_type=jnp.float32
    )


def low(value):
    return value.astype(jnp.bfloat16)


def wide(value):
    return value.astype(jnp.float32)


def norm_scale(values):
    return lax.rsqrt(jnp.mean(values * values, axis=-1, keepdims=True) + 1e-06)


def rms_back(scaled, scale, gain, grad_normed):
    weighted = grad_normed * gain
    return scale * (weighted - scaled * jnp.mean(weighted * scaled, axis=-1, keepdims=True))


IN_HBM = pl.BlockSpec(memory_space=pl.ANY)
IN_SMEM = pl.BlockSpec(memory_space=pltpu.SMEM)
IN_VMEM = pl.BlockSpec(memory_space=pltpu.VMEM)
TOKEN_SHAPE = jax.ShapeDtypeStruct((1, 1), jnp.float32)
TOKEN = pl.BlockSpec((1, 1), lambda *_: (0, 0), memory_space=pltpu.SMEM)


def cost(flops, bytes_moved):
    return pl.CostEstimate(flops=flops, bytes_accessed=bytes_moved, transcendentals=0)


def plan(me, rows, by_chips, side, per_core):
    chip, core = me // 2, me % 2
    if not by_chips:
        return []
    count = 5
    found = []
    for part, index, distance in chip_distances():
        number = chip ^ distance
        if per_core:
            number = number * 2 + (core ^ side)
        found.append((side * count + part, index, pl.multiple_of(number * rows, 16)))
    return found


def column_copies(me, sources, target, sems, side, by_chips, columns):
    first, last = columns
    if not by_chips:
        half = (me % 2) ^ side
        return [
            pltpu.make_async_copy(sources[0].at[half, :, pl.ds(first, last - first)], target, sems.at[0])
        ]
    rows = sources[0].shape[1]
    return [
        pltpu.make_async_copy(
            sources[part].at[index, :, pl.ds(first, last - first)],
            target.at[pl.ds(start, rows), :],
            sems.at[number],
        )
        for number, (part, index, start) in enumerate(plan(me, rows, True, side, False))
    ]


def row_copies(me, sources, target, sems, side, by_chips):
    if not by_chips:
        half = target.shape[0] // 2
        where = pl.ds(side * half, half)
        return [pltpu.make_async_copy(sources[0].at[where, :], target.at[where, :], sems.at[0])]
    rows = sources[0].shape[1]
    return [
        pltpu.make_async_copy(
            sources[part].at[index], target.at[pl.ds(start, rows), :], sems.at[number]
        )
        for number, (part, index, start) in enumerate(plan(me, rows, True, side, True))
    ]


def start_all(copies):
    for copy in copies:
        copy.start()


def wait_all(copies):
    for copy in copies:
        copy.wait()


def half_copies(me, tile, targets, sems, side, by_chips, columns):
    first, count = columns
    if not by_chips:
        half = (me % 2) ^ side
        return [
            pltpu.make_async_copy(tile, targets[0].at[half, :, pl.ds(first, count)], sems.at[0])
        ]
    planes, line, rows = targets[side].shape[:3]
    chip = me // 2
    return [
        pltpu.make_async_copy(
            tile.at[pl.ds(pl.multiple_of((chip ^ (4 * hop + plane)) * rows, 16), rows), :],
            targets[side].at[plane, hop, :, pl.ds(first, count)],
            sems.at[plane * line + hop],
        )
        for plane in range(planes)
        for hop in range(line)
    ]


def strip_copies(me, tile, targets, sems, strip, by_chips):
    if not by_chips:
        rows = tile.shape[0]
        return [
            pltpu.make_async_copy(
                tile, targets[0].at[pl.ds(pl.multiple_of(strip * rows, 16), rows), :], sems.at[0]
            )
        ]
    planes, line, rows = targets[0].shape[:3]
    chip, core = me // 2, me % 2
    return [
        pltpu.make_async_copy(
            tile.at[
                pl.ds(pl.multiple_of((((chip % 4) ^ plane) * 2 + (core ^ side)) * rows, 16), rows), :
            ],
            targets[side].at[plane, (chip // 4) ^ strip],
            sems.at[side * planes + plane],
        )
        for side in range(2)
        for plane in range(planes)
    ]


def bias_planes(table, after=()):
    heads = table.shape[1]
    ids = bucket_ids(SEQ)
    flat = np.concatenate([ids[:, 0], ids[0, :1], ids[0, :0:-1]])
    onehot = (np.arange(table.shape[0])[:, None] == flat[None, :]).astype(np.float32)

    def kernel(table_ref, onehot_ref, *refs):
        plane_ref, token_ref, rows = refs[len(after) :]
        token_ref[0, 0] = 0.0
        head = pl.program_id(0)

        @pl.when(head == 0)
        def _():
            rows[:heads] = lax.dot_general(
                wide(table_ref[...]),
                onehot_ref[...],
                (((0,), (0,)), ((), ())),
                precision=lax.Precision.HIGHEST,
                preferred_element_type=jnp.float32,
            )

        spread = jnp.broadcast_to(rows[pl.ds(head, 1), :], (SEQ, 2 * SEQ))
        moved = pltpu.roll(spread, 0, 1, stride=1, stride_axis=0)
        plane_ref[0] = low(moved[:, :SEQ])

    return pl.pallas_call(
        kernel,
        grid=(heads,),
        out_shape=[jax.ShapeDtypeStruct((heads, SEQ, SEQ), jnp.bfloat16), TOKEN_SHAPE],
        in_specs=[IN_VMEM, IN_VMEM] + [IN_HBM] * len(after),
        out_specs=[pl.BlockSpec((1, SEQ, SEQ), lambda head: (head, 0, 0)), TOKEN],
        scratch_shapes=[pltpu.VMEM((-(-heads // 8) * 8, 2 * SEQ), jnp.float32)],
        compiler_params=pltpu.CompilerParams(vmem_limit_bytes=16 * MIB),
    )(table, jnp.asarray(onehot), *after)


def line_ids():
    ids = bucket_ids(SEQ)
    ahead = (np.arange(2 * SEQ) - (SEQ - 128) + SEQ) % (2 * SEQ) - SEQ
    return np.where(ahead >= 0, ids[np.maximum(ahead, 0), 0], ids[0, np.minimum(-ahead, SEQ - 1)])


def project_qkv(place, tokens, sources, by_chips, after=()):
    slots, width = tokens.shape
    side_cols = width // 2
    packed = sources[0].shape[-1]
    block = 256
    steps = slots // block

    def kernel(place_ref, x_ref, *refs):
        ins = refs[: len(sources)]
        outs = refs[len(sources) + len(after) :]
        q_ref, k_ref, v_ref, gains_ref, token_ref, weights, normed, sems = outs
        token_ref[0, 0] = 0.0
        side, step = pl.program_id(0), pl.program_id(1)
        me = place_ref[0]

        def copies(which):
            return column_copies(
                me, ins, weights.at[which], sems.at[which], which, by_chips, (0, packed)
            )

        @pl.when((side == 0) & (step == 0))
        def _():
            start_all(copies(0))
            start_all(copies(1))
            wait_all(copies(0))
            gains = jnp.transpose(wide(weights[0, :, 3 * side_cols :]))
            gains_ref[...] = gains[:8]

            def normalise(index, carry):
                where = pl.ds(pl.multiple_of(index * 128, 128), 128)
                rows = wide(x_ref[where, :])
                normed[where, :] = low(rows * norm_scale(rows) * gains[:1])
                return carry

            lax.fori_loop(0, slots // 128, normalise, 0)

        @pl.when((side == 1) & (step == 0))
        def _():
            wait_all(copies(1))

        rows = normed[pl.ds(pl.multiple_of(step * block, block), block), :]
        for part, out in enumerate((q_ref, k_ref, v_ref)):
            out[...] = low(nn(rows, weights[side, :, part * side_cols : (part + 1) * side_cols]))

    flat = jax.ShapeDtypeStruct((slots, width), jnp.bfloat16)
    out_block = pl.BlockSpec(
        (block, side_cols), lambda side, step, place_ref: (step, (place_ref[0] % 2) ^ side)
    )
    return pl.pallas_call(
        kernel,
        grid_spec=pltpu.PrefetchScalarGridSpec(
            num_scalar_prefetch=1,
            grid=(2, steps),
            in_specs=[pl.BlockSpec((slots, width), lambda side, step, place_ref: (0, 0))]
            + [IN_HBM] * (len(sources) + len(after)),
            out_specs=[out_block] * 3
            + [pl.BlockSpec((8, width), lambda side, step, place_ref: (0, 0)), TOKEN],
            scratch_shapes=[
                pltpu.VMEM((2, width, packed), jnp.bfloat16),
                pltpu.VMEM((slots, width), jnp.bfloat16),
                pltpu.SemaphoreType.DMA((2, 16)),
            ],
        ),
        out_shape=[flat] * 3 + [jax.ShapeDtypeStruct((8, width), jnp.float32), TOKEN_SHAPE],
        compiler_params=pltpu.CompilerParams(vmem_limit_bytes=54 * MIB),
        cost_estimate=cost(6 * slots * width * width, 12 * slots * width),
    )(place, tokens, *sources, *after)


def attend(lengths, query, key, value, planes, first, count, shared=(), after=()):
    slots, width = query.shape
    seqs = slots // SEQ
    heads = planes.shape[0]
    pair_cols = 2 * width // heads
    head_size = pair_cols // 2
    piece = 256

    def kernel(lengths_ref, q_ref, k_ref, v_ref, planes_ref, *refs):
        out_ref, prob_ref, token_ref = refs[len(shared) + len(after) :]
        token_ref[0, 0] = 0.0
        seq = pl.program_id(1)
        limit = lengths_ref[seq, 0] + lengths_ref[seq, 1]
        permitted = lax.broadcasted_iota(jnp.int32, (SEQ, 1), 0) < limit
        own_lane = lax.broadcasted_iota(jnp.int32, (1, pair_cols), 1) < head_size
        keys, values = k_ref[...], v_ref[...]
        zero = jnp.zeros((), jnp.bfloat16)
        value_cols = low(jnp.transpose(wide(values)))
        for part in range(SEQ // piece):
            where = slice(part * piece, (part + 1) * piece)
            mixed = []
            for head in range(2):
                mask = own_lane if head == 0 else ~own_lane
                scores = nt(jnp.where(mask, keys, zero), q_ref[where, :])
                scores = scores + wide(planes_ref[head, :, where])
                scores = jnp.where(permitted, scores, -1e30)
                peak = jnp.max(scores, axis=0, keepdims=True)
                raised = jnp.exp(scores - peak)
                total = jnp.sum(raised, axis=0, keepdims=True)
                prob = low(raised * (1.0 / total))
                prob_ref[0, head, :, where] = prob
                mixed.append(nn(value_cols[head * head_size : (head + 1) * head_size], prob))
            out_ref[where, :] = low(jnp.transpose(jnp.concatenate(mixed, 0)))

    def cols(pair, seq, lengths_ref):
        return (seq, first + pair)

    block = pl.BlockSpec((SEQ, pair_cols), cols)
    return pl.pallas_call(
        kernel,
        grid_spec=pltpu.PrefetchScalarGridSpec(
            num_scalar_prefetch=1,
            grid=(count, seqs),
            in_specs=[
                block,
                block,
                block,
                pl.BlockSpec((2, SEQ, SEQ), lambda pair, seq, lengths_ref: (first + pair, 0, 0)),
            ]
            + [IN_HBM] * (len(shared) + len(after)),
            out_specs=[
                pl.BlockSpec((SEQ, pair_cols), cols),
                pl.BlockSpec(
                    (1, 2, SEQ, SEQ), lambda pair, seq, lengths_ref: (seq, first + pair, 0, 0)
                ),
                TOKEN,
            ],
        ),
        out_shape=[
            jax.ShapeDtypeStruct((slots, width), jnp.bfloat16),
            jax.ShapeDtypeStruct((seqs, heads, SEQ, SEQ), jnp.bfloat16),
            TOKEN_SHAPE,
        ],
        compiler_params=pltpu.CompilerParams(vmem_limit_bytes=24 * MIB),
        cost_estimate=cost(count * slots * SEQ * 2048, count * slots * SEQ * 8),
        input_output_aliases={5: 0, 6: 1} if shared else {},
    )(lengths, query, key, value, planes, *shared, *after)


def attend_back(query, key, value, grad_mixed, prob, first, count, heads, after=()):
    slots, width = query.shape
    seqs = slots // SEQ
    pair_cols = 2 * width // heads
    head_size = pair_cols // 2
    piece = 256

    def kernel(q_ref, k_ref, v_ref, g_ref, prob_ref, *refs):
        dq_ref, dk_ref, dv_ref, table_ref, token_ref, planes = refs[len(after) :]
        token_ref[0, 0] = 0.0
        seq = pl.program_id(1)
        own_lane = lax.broadcasted_iota(jnp.int32, (1, pair_cols), 1) < head_size
        values = v_ref[...]
        zero = jnp.zeros((), jnp.bfloat16)
        key_cols = low(jnp.transpose(wide(k_ref[...])))
        dk, dv, dq = [], [], [[], []]
        for head in range(2):
            mask = own_lane if head == 0 else ~own_lane
            masked = jnp.where(mask, values, zero)
            sum_k = sum_v = 0.0
            for part in range(SEQ // piece):
                where = slice(part * piece, (part + 1) * piece)
                prob = prob_ref[0, head, :, where]
                grads = g_ref[where, :]
                sum_v += nn(prob, grads)
                prob = wide(prob)
                grad_prob = nt(masked, grads)
                weighted = prob * grad_prob
                dot = jnp.sum(weighted, axis=0, keepdims=True)
                grad_scores = weighted - prob * dot

                @pl.when(seq == 0)
                def _():
                    planes[head, :, where] = grad_scores

                @pl.when(seq > 0)
                def _():
                    planes[head, :, where] += grad_scores

                grad_scores = low(grad_scores)
                sum_k += nn(grad_scores, q_ref[where, :])
                dq[part].append(
                    nn(key_cols[head * head_size : (head + 1) * head_size], grad_scores)
                )
            dk.append(sum_k)
            dv.append(sum_v)
        dk_ref[...] = low(jnp.where(own_lane, dk[0], dk[1]))
        dv_ref[...] = low(jnp.where(own_lane, dv[0], dv[1]))
        for part in range(SEQ // piece):
            dq_ref[part * piece : (part + 1) * piece, :] = low(
                jnp.transpose(jnp.concatenate(dq[part], 0))
            )

        @pl.when(seq == seqs - 1)
        def _():
            for head in range(2):
                lined = jnp.zeros((8, 2 * SEQ), jnp.float32)
                for low_row in range(0, 128, 8):
                    frame = jnp.zeros((8, 2 * SEQ), jnp.float32)
                    for high_row in range(0, SEQ, 128):
                        rows = planes[head, high_row + low_row : high_row + low_row + 8, :]
                        ahead = SEQ - 128 - high_row
                        filled = [rows, jnp.zeros((8, SEQ - ahead), jnp.float32)]
                        if ahead:
                            filled = [jnp.zeros((8, ahead), jnp.float32)] + filled
                        frame = frame + jnp.concatenate(filled, 1)
                    if low_row:
                        frame = pltpu.roll(frame, 2 * SEQ - low_row, 1)
                    lined = lined + frame
                moved = lined[:1]
                for row in range(1, 8):
                    moved = moved + pltpu.roll(lined[row : row + 1], 2 * SEQ - row, 1)
                table_ref[0, head : head + 1, :] = moved

    def cols(pair, seq):
        return (seq, first + pair)

    def own_cols(pair, seq):
        return (seq, pair)

    block = pl.BlockSpec((SEQ, pair_cols), cols)
    own_block = pl.BlockSpec((SEQ, pair_cols), own_cols)
    flat = jax.ShapeDtypeStruct((slots, count * pair_cols), jnp.bfloat16)
    return pl.pallas_call(
        kernel,
        grid=(count, seqs),
        in_specs=[
            block,
            block,
            block,
            block,
            pl.BlockSpec((1, 2, SEQ, SEQ), lambda pair, seq: (seq, first + pair, 0, 0)),
        ]
        + [IN_HBM] * len(after),
        out_specs=[own_block] * 3
        + [pl.BlockSpec((1, 8, 2 * SEQ), lambda pair, seq: (pair, 0, 0)), TOKEN],
        out_shape=[flat] * 3 + [jax.ShapeDtypeStruct((count, 8, 2 * SEQ), jnp.float32), TOKEN_SHAPE],
        scratch_shapes=[pltpu.VMEM((2, SEQ, SEQ), jnp.float32)],
        compiler_params=pltpu.CompilerParams(vmem_limit_bytes=28 * MIB),
        cost_estimate=cost(count * slots * SEQ * 4096, count * slots * SEQ * 8),
    )(query, key, value, grad_mixed, prob, *after)


def feed_forward(place, tokens, attended, cotangent, gains, in_sources, out_sources, by_chips):
    slots, width = tokens.shape
    side_cols = width // 2
    hidden_cols = 2 * (in_sources[0].shape[-1] - side_cols)
    block = 256
    blocks = slots // block
    chunk = 768
    per_side = hidden_cols // 2 // chunk
    count_att = len(attended)
    root, bend = math.sqrt(2.0 / math.pi), 0.044715

    def kernel(place_ref, x_hbm, cot_hbm, gains_ref, *refs):
        refs = list(refs)

        def take(number):
            taken, refs[:] = refs[:number], refs[number:]
            return taken

        att_hbm, in_hbm, out_hbm = take(count_att), take(len(in_sources)), take(len(out_sources))
        y_hbm, grad_hbm, back_hbm, branch_hbm, flipped_hbm, pre_hbm = take(6)
        out_targets = take(2 if by_chips else 1)
        x, att, cot, w_o, w_in, w_out, hidden, normed, flipped = take(9)
        sum_y, sum_g, act, grad_pre, tile_out = take(5)
        load_sems, o_sems, in_sems, out_sems, store_sems, pre_sems, tile_out_sems = take(7)
        me = place_ref[0]
        core = me % 2
        gain = gains_ref[1:2, :]

        def rows_of(index):
            return pl.ds(pl.multiple_of(index * block, block), block)

        loads = [
            pltpu.make_async_copy(x_hbm, x, load_sems.at[0]),
            pltpu.make_async_copy(cot_hbm, cot, load_sems.at[1]),
        ]
        cols = 0
        for number, source in enumerate(att_hbm):
            loads.append(
                pltpu.make_async_copy(
                    source, att.at[:, pl.ds(cols, source.shape[1])], load_sems.at[2 + number]
                )
            )
            cols += source.shape[1]
        o_loads, in_loads, out_loads = [], [], []
        for side in range(2):
            o_cols = pl.ds(pl.multiple_of((core ^ side) * side_cols, 128), side_cols)
            o_loads += column_copies(
                me, in_hbm, w_o.at[:, o_cols], o_sems.at[side], side, by_chips, (0, side_cols)
            )
            in_loads.append(
                column_copies(
                    me,
                    in_hbm,
                    w_in.at[side],
                    in_sems.at[side],
                    side,
                    by_chips,
                    (side_cols, in_sources[0].shape[-1]),
                )
            )
            out_loads += row_copies(me, out_hbm, w_out, out_sems.at[side], side, by_chips)
        start_all(loads)
        start_all(o_loads)
        start_all(in_loads[0])
        start_all(out_loads)
        start_all(in_loads[1])
        wait_all(loads)
        wait_all(o_loads)

        def before(index, carry):
            where = rows_of(index)
            value = wide(x[where, :]) + nn(att[where, :], w_o[...])
            hidden[where, :] = value
            rows = value * norm_scale(value) * gain
            normed[where, :] = low(rows)
            flipped[:, where] = low(jnp.transpose(rows))
            sum_y[where, :] = value
            sum_g[where, :] = jnp.zeros_like(value)
            return carry

        lax.fori_loop(0, blocks, before, 0)
        flip_store = pltpu.make_async_copy(flipped, flipped_hbm, store_sems.at[3])
        flip_store.start()
        wait_all(in_loads[0])
        wait_all(out_loads)

        stores = []
        for side in range(2):
            if side:
                wait_all(in_loads[1])
            for part in range(per_side):
                number = side * per_side + part
                strip = (core ^ side) * per_side + part
                unit_rows = pl.ds(pl.multiple_of(strip * chunk, chunk), chunk)
                unit_cols = slice(part * chunk, (part + 1) * chunk)

                def through(index, carry):
                    where = rows_of(index)
                    pre = nn(normed[where, :], w_in[side, :, unit_cols])
                    square = pre * pre
                    slope = jnp.tanh(root * pre * (1.0 + bend * square))
                    opened = 0.5 * (1.0 + slope)
                    gate = opened + (0.5 * root) * pre * (1.0 - slope * slope) * (
                        1.0 + (3.0 * bend) * square
                    )
                    acted = low(pre * opened)
                    act[where, :] = acted
                    back = low(nt(cot[where, :], w_out[unit_rows, :]) * gate)
                    grad_pre[slot, where, :] = back
                    sum_y[where, :] += nn(acted, w_out[unit_rows, :])
                    sum_g[where, :] += nt(back, w_in[side, :, unit_cols])
                    return carry

                slot = number % 2
                if number >= 2:
                    wait_all(stores[number - 2])
                lax.fori_loop(0, blocks, through, 0)
                for third in range(3):
                    some = slice(third * chunk // 3, (third + 1) * chunk // 3)
                    tile_out[slot, some, :] = low(tn(act[:, some], cot[...]))
                copies = strip_copies(
                    me, tile_out.at[slot], out_targets, tile_out_sems.at[slot], strip, by_chips
                ) + [
                    pltpu.make_async_copy(
                        grad_pre.at[slot], pre_hbm.at[strip], pre_sems.at[slot]
                    )
                ]
                start_all(copies)
                stores.append(copies)

        wait_all(stores[-2])

        def after(index, carry):
            where = rows_of(index)
            value = hidden[where, :]
            normed[where, :] = low(sum_y[where, :])
            scale = norm_scale(value)
            scaled = value * scale
            grad = sum_g[where, :]
            grad = wide(cot[where, :]) + rms_back(scaled, scale, gain, grad)
            sum_g[where, :] = grad
            branch = low(grad)
            grad_pre[len(stores) % 2, where, :] = branch
            act[where, :] = low(nt(branch, w_o[...]))
            return carry

        lax.fori_loop(0, blocks, after, 0)
        last = [
            pltpu.make_async_copy(normed, y_hbm, store_sems.at[0]),
            pltpu.make_async_copy(sum_g, grad_hbm, store_sems.at[1]),
            pltpu.make_async_copy(act, back_hbm, store_sems.at[2]),
            pltpu.make_async_copy(
                grad_pre.at[len(stores) % 2], branch_hbm, store_sems.at[4]
            ),
        ]
        start_all(last)
        wait_all(stores[-1])
        wait_all(last)
        flip_store.wait()

    sums = jax.ShapeDtypeStruct
    flat = sums((slots, width), jnp.bfloat16)
    devices = lax.axis_size("fsdp")
    if by_chips:
        line = devices // 8
        out_shapes = [sums((4, line, hidden_cols // devices, width), jnp.bfloat16)] * 2
    else:
        out_shapes = [sums((hidden_cols, width), jnp.bfloat16)]
    outs = [
        flat,
        sums((slots, width), jnp.float32),
        flat,
        flat,
        sums((width, slots), jnp.bfloat16),
        sums((hidden_cols // chunk, slots, chunk), jnp.bfloat16),
    ] + out_shapes
    bf16, f32 = jnp.bfloat16, jnp.float32
    result = pl.pallas_call(
        kernel,
        out_shape=outs,
        in_specs=[IN_SMEM, IN_HBM, IN_HBM, IN_VMEM]
        + [IN_HBM] * (count_att + len(in_sources) + len(out_sources)),
        out_specs=[IN_HBM] * len(outs),
        scratch_shapes=[
            pltpu.VMEM((slots, width), bf16),
            pltpu.VMEM((slots, width), bf16),
            pltpu.VMEM((slots, width), bf16),
            pltpu.VMEM((width, width), bf16),
            pltpu.VMEM((2, width, hidden_cols // 2), bf16),
            pltpu.VMEM((hidden_cols, width), bf16),
            pltpu.VMEM((slots, width), f32),
            pltpu.VMEM((slots, width), bf16),
            pltpu.VMEM((width, slots), bf16),
            pltpu.VMEM((slots, width), f32),
            pltpu.VMEM((slots, width), f32),
            pltpu.VMEM((slots, chunk), bf16),
            pltpu.VMEM((2, slots, chunk), bf16),
            pltpu.VMEM((2, chunk, width), bf16),
            pltpu.SemaphoreType.DMA((2 + count_att,)),
            pltpu.SemaphoreType.DMA((2, 16)),
            pltpu.SemaphoreType.DMA((2, 16)),
            pltpu.SemaphoreType.DMA((2, 16)),
            pltpu.SemaphoreType.DMA((5,)),
            pltpu.SemaphoreType.DMA((2,)),
            pltpu.SemaphoreType.DMA((2, 8)),
        ],
        compiler_params=pltpu.CompilerParams(vmem_limit_bytes=60 * MIB),
        cost_estimate=cost(
            slots * width * (12 * hidden_cols + 6 * width), 60 * MIB
        ),
    )(place, tokens, cotangent, gains, *attended, *in_sources, *out_sources)
    return result[:3], result[3:6], result[6:]


def in_weights_back(place, attended, branch, flipped, grad_pre, by_chips):
    slots, width = branch.shape
    strips, _, chunk = grad_pre.shape
    side_cols = width // 2
    per_side = strips // 2
    packed = side_cols + per_side * chunk
    count_att = len(attended)

    def kernel(place_ref, branch_hbm, flipped_hbm, pre_hbm, *refs):
        att_hbm, refs = refs[:count_att], refs[count_att:]
        targets, refs = refs[:-9], refs[-9:]
        token_ref, att, branch, flipped, pre, tile, load_sems, tile_sems, o_sems = refs
        token_ref[0, 0] = 0.0
        me = place_ref[0]
        core = me % 2
        order = [(side, part) for side in (1, 0) for part in range(per_side)]
        pre_loads = [
            pltpu.make_async_copy(
                pre_hbm.at[(core ^ side) * per_side + part], pre.at[number], load_sems.at[number]
            )
            for number, (side, part) in enumerate(order)
        ]
        flip_load = pltpu.make_async_copy(flipped_hbm, flipped, load_sems.at[strips])
        loads = [pltpu.make_async_copy(branch_hbm, branch, load_sems.at[strips + 1])]
        cols = 0
        for number, source in enumerate(att_hbm):
            loads.append(
                pltpu.make_async_copy(
                    source,
                    att.at[:, pl.ds(cols, source.shape[1])],
                    load_sems.at[strips + 2 + number],
                )
            )
            cols += source.shape[1]
        flip_load.start()
        start_all(pre_loads)
        start_all(loads)
        flip_load.wait()
        stores = []
        for number, (side, part) in enumerate(order):
            pre_loads[number].wait()
            slot = number % 2
            if number >= 2:
                wait_all(stores[number - 2])
            for third in range(3):
                some = slice(third * width // 3, (third + 1) * width // 3)
                tile[slot, some, :] = low(nn(flipped[some, :], pre[number]))
            stores.append(
                half_copies(
                    me,
                    tile.at[slot],
                    targets,
                    tile_sems.at[slot],
                    side,
                    by_chips,
                    (side_cols + part * chunk, chunk),
                )
            )
            start_all(stores[-1])
        wait_all(loads)
        slot = len(stores) % 2
        wait_all(stores[-2])
        for third in range(3):
            some = slice(third * width // 3, (third + 1) * width // 3)
            tile[slot, some, :] = low(tn(att[:, some], branch[...]))
        copies = []
        for side in range(2):
            o_cols = pl.ds(pl.multiple_of((core ^ side) * side_cols, 128), side_cols)
            copies += half_copies(
                me,
                tile.at[slot, :, o_cols],
                targets,
                o_sems.at[side],
                side,
                by_chips,
                (0, side_cols),
            )
        start_all(copies)
        wait_all(stores[-1])
        wait_all(copies)

    sums = jax.ShapeDtypeStruct
    bf16 = jnp.bfloat16
    if by_chips:
        line = lax.axis_size("fsdp") // 8
        shapes = [sums((4, line, width // (4 * line), packed), bf16)] * 2
    else:
        shapes = [sums((2, width, packed), bf16)]
    result = pl.pallas_call(
        kernel,
        out_shape=shapes + [TOKEN_SHAPE],
        in_specs=[IN_SMEM, IN_HBM, IN_HBM, IN_HBM] + [IN_HBM] * count_att,
        out_specs=[IN_HBM] * len(shapes) + [IN_SMEM],
        scratch_shapes=[
            pltpu.VMEM((slots, width), bf16),
            pltpu.VMEM((slots, width), bf16),
            pltpu.VMEM((width, slots), bf16),
            pltpu.VMEM((strips, slots, chunk), bf16),
            pltpu.VMEM((2, width, chunk), bf16),
            pltpu.SemaphoreType.DMA((strips + 2 + count_att,)),
            pltpu.SemaphoreType.DMA((2, 16)),
            pltpu.SemaphoreType.DMA((2, 16)),
        ],
        compiler_params=pltpu.CompilerParams(vmem_limit_bytes=54 * MIB),
        cost_estimate=cost(2 * slots * width * (width + strips * chunk), 20 * MIB),
    )(place, branch, flipped, grad_pre, *attended)
    return result[:-1], result[-1]


def back_places(grads, side_cols):
    places, first = [], 0
    for number, some in enumerate(grads):
        for col in range(0, some[0].shape[1], 128):
            half, start = divmod(first + col, side_cols)
            places += [
                (3 * number + part, col, half, part * side_cols + start) for part in range(3)
            ]
        first += some[0].shape[1]
    return [grad for some in grads for grad in some], places


def column_loads(hbm, places, parts, sems, some=slice(None)):
    return [
        pltpu.make_async_copy(
            hbm[number].at[some, pl.ds(col, 128)],
            parts.at[half, :, pl.ds(start, 128)],
            sems.at[count],
        )
        for count, (number, col, half, start) in enumerate(places)
    ]


def weights_back(place, tokens, gains, grads, diagonals, by_chips, after=()):
    slots, width = tokens.shape
    side_cols = width // 2
    flat_grads, places = back_places(grads, side_cols)
    block = 256

    onehot = np.pad(
        (line_ids()[:, None] == np.arange(NB)[None, :]).astype(np.float32), ((0, 0), (0, 128 - NB))
    )
    pairs = len(diagonals)
    heads = sum(2 * some.shape[0] for some in diagonals)
    table_rows = -(-heads // 8) * 8

    def kernel(place_ref, x_hbm, gains_ref, onehot_ref, *refs):
        diag_refs, refs = refs[:pairs], refs[pairs:]
        g_hbm = refs[: len(flat_grads)]
        refs = refs[len(flat_grads) + len(after) :]
        targets, refs = refs[:-8], refs[-8:]
        table_ref, token_ref, x, parts, flipped, tile, load_sems, tile_sems = refs
        token_ref[0, 0] = 0.0
        me = place_ref[0]
        core = me % 2
        first = pltpu.make_async_copy(x_hbm, x, load_sems.at[len(places)])
        first.start()
        loads = column_loads(g_hbm, places, parts, load_sems)
        start_all(loads)
        first.wait()

        def flip(index, carry):
            where = pl.ds(pl.multiple_of(index * block, block), block)
            rows = wide(x[where, :])
            flipped[:, where] = low(jnp.transpose(rows * norm_scale(rows) * gains_ref[0:1, :]))
            return carry

        lax.fori_loop(0, slots // block, flip, 0)
        rows = [
            ref[one, head : head + 1, :]
            for ref in diag_refs
            for one in range(ref.shape[0])
            for head in range(2)
        ]
        if table_rows > heads:
            rows.append(jnp.zeros((table_rows - heads, 2 * SEQ), jnp.float32))
        table_ref[...] = lax.dot_general(
            jnp.concatenate(rows, 0),
            onehot_ref[...],
            (((1,), (0,)), ((), ())),
            precision=lax.Precision.HIGHEST,
            preferred_element_type=jnp.float32,
        )
        wait_all(loads)
        copies = []
        for side in (1, 0):
            before = len(copies)
            half = core ^ side
            for third in range(3):
                some = slice(third * width // 3, (third + 1) * width // 3)
                tile[side, some, :] = low(nn(flipped[some, :], parts[half]))
            copies += half_copies(
                me,
                tile.at[side],
                targets,
                tile_sems.at[side],
                side,
                by_chips,
                (0, 3 * side_cols),
            )
            start_all(copies[before:])
        wait_all(copies)

    sums = jax.ShapeDtypeStruct
    if by_chips:
        line = lax.axis_size("fsdp") // 8
        shapes = [sums((4, line, width // (4 * line), 3 * side_cols), jnp.bfloat16)] * 2
    else:
        shapes = [sums((2, width, 3 * side_cols), jnp.bfloat16)]
    result = pl.pallas_call(
        kernel,
        out_shape=shapes + [sums((table_rows, 128), jnp.float32), TOKEN_SHAPE],
        in_specs=[IN_SMEM, IN_HBM, IN_VMEM, IN_VMEM]
        + [IN_VMEM] * pairs
        + [IN_HBM] * (len(flat_grads) + len(after)),
        out_specs=[IN_HBM] * len(shapes) + [IN_VMEM, IN_SMEM],
        scratch_shapes=[
            pltpu.VMEM((slots, width), jnp.bfloat16),
            pltpu.VMEM((2, slots, 3 * side_cols), jnp.bfloat16),
            pltpu.VMEM((width, slots), jnp.bfloat16),
            pltpu.VMEM((2, width, 3 * side_cols), jnp.bfloat16),
            pltpu.SemaphoreType.DMA((len(places) + 1,)),
            pltpu.SemaphoreType.DMA((2, 16)),
        ],
        compiler_params=pltpu.CompilerParams(vmem_limit_bytes=54 * MIB),
        cost_estimate=cost(6 * slots * width * width, 15 * MIB),
    )(place, tokens, gains, jnp.asarray(onehot), *diagonals, *flat_grads, *after)
    return result[:-2], result[-2], result[-1]


def inputs_back(
    place, tokens, gains, grad_hidden, grads, sources, by_chips, first, count, done=None, after=()
):
    slots, width = tokens.shape
    side_cols = width // 2
    packed = sources[0].shape[-1]
    flat_grads, places = back_places(grads, side_cols)
    block = 256
    held = () if done is None else (done,)

    def kernel(place_ref, x_hbm, gh_hbm, gains_ref, *refs):
        g_hbm, refs = refs[: len(flat_grads)], refs[len(flat_grads) :]
        w_hbm, refs = refs[: len(sources)], refs[len(sources) + len(after) + len(held) :]
        out_hbm, token_ref, x, grad, weights, parts, out, load_sems, w_sems, out_sems = refs
        token_ref[0, 0] = 0.0
        me = place_ref[0]
        core = me % 2
        gain = gains_ref[0:1, :]
        some = pl.ds(first, count)
        loads = column_loads(g_hbm, places, parts, load_sems, some) + [
            pltpu.make_async_copy(x_hbm.at[some], x, load_sems.at[len(places)]),
            pltpu.make_async_copy(gh_hbm.at[some], grad, load_sems.at[len(places) + 1]),
        ]
        w_loads = [
            copy
            for side in range(2)
            for copy in column_copies(
                me, w_hbm, weights.at[side], w_sems.at[side], side, by_chips, (0, packed)
            )
        ]
        start_all(w_loads)
        start_all(loads)
        wait_all(w_loads)
        wait_all(loads)

        def finish(index, carry):
            where = pl.ds(pl.multiple_of(index * block, block), block)
            grad_normed = nt(parts[core, where, :], weights[0, :, : 3 * side_cols]) + nt(
                parts[1 - core, where, :], weights[1, :, : 3 * side_cols]
            )
            rows = wide(x[where, :])
            scale = norm_scale(rows)
            out[where, :] = low(
                grad[where, :] + rms_back(rows * scale, scale, gain, grad_normed)
            )
            return carry

        lax.fori_loop(0, count // block, finish, 0)
        last = pltpu.make_async_copy(out, out_hbm.at[some], out_sems.at[0])
        last.start()
        last.wait()

    bf16, f32 = jnp.bfloat16, jnp.float32
    return pl.pallas_call(
        kernel,
        out_shape=[jax.ShapeDtypeStruct((slots, width), bf16), TOKEN_SHAPE],
        in_specs=[IN_SMEM, IN_HBM, IN_HBM, IN_VMEM]
        + [IN_HBM] * (len(flat_grads) + len(sources) + len(after) + len(held)),
        out_specs=[IN_HBM, IN_SMEM],
        scratch_shapes=[
            pltpu.VMEM((count, width), bf16),
            pltpu.VMEM((count, width), f32),
            pltpu.VMEM((2, width, packed), bf16),
            pltpu.VMEM((2, count, 3 * side_cols), bf16),
            pltpu.VMEM((count, width), bf16),
            pltpu.SemaphoreType.DMA((len(places) + 2,)),
            pltpu.SemaphoreType.DMA((2, 16)),
            pltpu.SemaphoreType.DMA((1,)),
        ],
        compiler_params=pltpu.CompilerParams(vmem_limit_bytes=54 * MIB),
        cost_estimate=cost(6 * count * width * width, 15 * MIB),
        input_output_aliases={4 + len(flat_grads) + len(sources) + len(after): 0} if held else {},
    )(place, tokens, grad_hidden, gains, *flat_grads, *sources, *after, *held)


def pack_halves(place, gain_attn, gain_ffn, shards_qkv, shards_in):
    rows = shards_qkv[0].shape[0]
    groups = (shards_qkv, shards_in)
    counts = [sum(shard.shape[1] for shard in group) // 2 for group in groups]

    def kernel(place_ref, attn_ref, ffn_ref, *refs):
        ins, outs = refs[: -2 * len(groups)], refs[-2 * len(groups) :]
        core = place_ref[0] % 2
        first = 0
        for number, group in enumerate(groups):
            for other in range(2):
                out, col = outs[2 * number + other], 0
                for ref in ins[first : first + len(group)]:
                    half = ref.shape[1] // 2
                    start = pl.multiple_of((core ^ other) * half, 128)
                    out[:, col : col + half] = ref[:, pl.ds(start, half)]
                    col += half
            first += len(group)
        same = lax.broadcasted_iota(jnp.int32, (rows, rows), 0) == lax.broadcasted_iota(
            jnp.int32, (rows, rows), 1
        )
        lane = lax.broadcasted_iota(jnp.int32, (rows, 128), 1)
        cols = jnp.zeros((rows, 128), jnp.float32)
        for number, ref in enumerate((attn_ref, ffn_ref)):
            row = wide(ref[...])
            col = jnp.sum(jnp.where(same, row, 0.0), axis=1, keepdims=True)
            cols = jnp.where(lane == number, col, cols)
        for other in range(2):
            outs[other][:, counts[0] :] = low(cols)

    shapes = [
        jax.ShapeDtypeStruct((rows, count + extra), jnp.bfloat16)
        for count, extra in zip(counts, (128, 0))
        for _ in range(2)
    ]
    return pl.pallas_call(
        kernel,
        out_shape=shapes,
        in_specs=[IN_SMEM] + [IN_VMEM] * (2 + len(shards_qkv) + len(shards_in)),
        out_specs=[IN_VMEM] * len(shapes),
    )(place, gain_attn, gain_ffn, *shards_qkv, *shards_in)


def prepare(compute, operands, shapes, after=(), place=None, pair=()):
    scalars = [] if place is None else [place]

    def kernel(*refs):
        refs = list(refs)
        where = [ref[0] for ref in refs[: len(scalars)]]
        ins, refs = refs[len(scalars) :][: len(operands)], refs[len(scalars) + len(operands) :]
        outs = refs[len(pair) + len(after) :]
        outs[-1][0, 0] = 0.0
        if pair:
            outs[-2][...] = refs[0][...] + refs[1][...]
        compute(*where, ins, outs)

    result = pl.pallas_call(
        kernel,
        out_shape=list(shapes) + [like(array, *array.shape) for array in pair[:1]] + [TOKEN_SHAPE],
        in_specs=[IN_SMEM] * len(scalars)
        + [IN_VMEM] * (len(operands) + len(pair))
        + [IN_HBM] * len(after),
        out_specs=[IN_VMEM] * (len(shapes) + len(pair[:1])) + [IN_SMEM],
        compiler_params=pltpu.CompilerParams(vmem_limit_bytes=8 * MIB),
        cost_estimate=cost(0, sum(2 * array.size for array in operands)),
    )(*scalars, *operands, *pair, *after)
    return result[:-1], result[-1]


def like(array, *shape):
    return jax.ShapeDtypeStruct(shape, array.dtype)


def stack_units(parts, after=()):
    def compute(ins, outs):
        for number, part in enumerate(ins):
            outs[0][number] = part[...]

    shape = like(parts[0], len(parts), *parts[0].shape)
    (stacked,), token = prepare(compute, list(parts), [shape], after)
    return stacked, token


def chip_unit(place, mine, got, after=()):
    def compute(me, ins, outs):
        first = me % 2 == 0
        own, other = wide(ins[0][...]), wide(ins[1][...])
        outs[0][...] = low(
            jnp.concatenate([jnp.where(first, own, other), jnp.where(first, other, own)], 0)
        )

    shape = like(mine, 2 * mine.shape[0], mine.shape[1])
    (unit,), token = prepare(compute, [mine, got], [shape], after, place)
    return unit, token


def stack_and_unit(place, parts, mine, got, after=()):
    def compute(me, ins, outs):
        for number in range(len(parts)):
            outs[0][number] = ins[number][...]
        first = me % 2 == 0
        own, other = wide(ins[-2][...]), wide(ins[-1][...])
        outs[1][...] = low(
            jnp.concatenate([jnp.where(first, own, other), jnp.where(first, other, own)], 0)
        )

    shapes = [
        like(parts[0], len(parts), *parts[0].shape),
        like(mine, 2 * mine.shape[0], mine.shape[1]),
    ]
    operands = list(tuple(parts) + (mine, got))
    return prepare(compute, operands, shapes, after, place)


def stack_and_copy(parts, array, after=()):
    def compute(ins, outs):
        for number in range(len(parts)):
            outs[0][number] = ins[number][...]
        outs[1][...] = ins[-1][...]

    shapes = [like(parts[0], len(parts), *parts[0].shape), like(array, *array.shape)]
    return prepare(compute, list(tuple(parts) + (array,)), shapes, after)


def stack_units(parts, after=()):
    def compute(ins, outs):
        for number in range(len(parts)):
            outs[0][number] = ins[number][...]

    shape = like(parts[0], len(parts), *parts[0].shape)
    return prepare(compute, list(parts), [shape], after)


def copied(arrays, after=()):
    def compute(ins, outs):
        for number in range(len(arrays)):
            outs[number][...] = ins[number][...]

    shapes = [like(array, *array.shape) for array in arrays]
    return prepare(compute, list(arrays), shapes, after)


def far_and_stack(over_x, over_y, parts=(), after=()):
    half = over_x.shape[0] // 2

    def compute(ins, outs):
        outs[0][...] = ins[0][:half]
        outs[1][...] = ins[1][half:]
        for number in range(len(parts)):
            outs[2][number] = ins[2 + number][...]

    shapes = [like(over_x, half, *over_x.shape[1:])] * 2
    if parts:
        shapes.append(like(parts[0], len(parts), *parts[0].shape))
    return prepare(compute, [over_y, over_x, *parts], shapes, after)


def first_sends(keep, got, after=(), pair=()):
    places = ((3, 0), (1, 0), (3, 1), (2, 1))
    half = keep.shape[1] // 2

    def compute(ins, outs):
        for number, (plane, late) in enumerate(places):
            for hop in range(half):
                at = late * half + hop
                outs[number // 2][number % 2, hop] = low(
                    wide(ins[0][plane, at]) + wide(ins[1][plane, at])
                )

    shapes = [like(keep, 2, half, *keep.shape[2:])] * 2
    return prepare(compute, [keep, got], shapes, after, pair=pair)


def second_sends(keep, got, first, after=(), pair=()):
    half = keep.shape[1] // 2

    def compute(ins, outs):
        for number, (plane, late) in enumerate(((2, 0), (1, 1))):
            for hop in range(half):
                at = late * half + hop
                outs[number][hop] = low(
                    wide(ins[0][plane, at])
                    + wide(ins[1][plane, at])
                    + wide(ins[2 + number][0, hop])
                )

    shapes = [like(keep, half, *keep.shape[2:])] * 2
    return prepare(compute, [keep, got, *first], shapes, after, pair=pair)


def line_sums(keep, got, first, second, after=(), pair=()):
    line = keep.shape[1]
    half = line // 2

    def compute(ins, outs):
        for at in range(line):
            direct, merged = ins[2 + at // half], ins[4 + at // half]
            total = wide(ins[0][0, at]) + wide(ins[1][0, at]) + wide(direct[1, at % half])
            outs[at][...] = low(total + wide(merged[at % half]))

    operands = [keep, got, *first, *second]
    return prepare(compute, operands, [like(keep, *keep.shape[2:])] * line, after, pair=pair)


def chip_sum_halves(place, terms, copied=(), after=(), pair=()):
    rows, cols = terms[0].shape

    def compute(me, ins, outs):
        total = add(*[ref[...] for ref in ins[: len(terms)]])
        first = me % 2 == 0
        upper, lower = total[: rows // 2], total[rows // 2 :]
        outs[0][...] = jnp.where(first, upper, lower)
        outs[1][...] = jnp.where(first, lower, upper)
        for number in range(len(copied)):
            outs[2 + number][...] = ins[len(terms) + number][...]

    shape = jax.ShapeDtypeStruct((rows // 2, cols), jnp.float32)
    shapes = [shape, shape] + [like(array, *array.shape) for array in copied]
    operands = list(tuple(terms) + tuple(copied))
    return prepare(compute, operands, shapes, after, place, pair=pair)


def join_halves(place, mine, other, parts, factor, gain, weights, after=()):
    rows = mine.shape[0]
    skipped = len(parts) - len(weights)

    def compute(me, ins, outs):
        core = me % 2
        first = 0
        for count, out in zip(parts, outs):
            for ref, half in ((ins[0], core), (ins[1], 1 - core)):
                start = pl.multiple_of(half * count, 128)
                out[:, pl.ds(start, count)] = ref[:, first : first + count] * factor
            first += count
        total = jnp.zeros((rows, 1), jnp.float32)
        for number, weight in enumerate(ins[3:]):
            product = wide(weight[...]) * outs[skipped + number][...]
            total = total + jnp.sum(product, axis=1, keepdims=True)
        same = lax.broadcasted_iota(jnp.int32, (rows, rows), 0) == lax.broadcasted_iota(
            jnp.int32, (rows, rows), 1
        )
        column = jnp.sum(jnp.where(same, wide(ins[2][...]), 0.0), axis=1, keepdims=True)
        outs[len(parts)][...] = jnp.broadcast_to(total / column, (rows, 128))

    shapes = [jax.ShapeDtypeStruct((rows, 2 * count), jnp.float32) for count in parts]
    shapes.append(jax.ShapeDtypeStruct((rows, 128), jnp.float32))
    operands = list((mine, other, gain[None]) + tuple(weights))
    return prepare(compute, operands, shapes, after, place)[0]


def gather_plain(shards):
    full = [lax.all_gather(shard, "fsdp", axis=0, tiled=True) for shard in shards]
    gain_attn, w_query, w_key, w_value, w_attn_out, gain_ffn, w_ffn_in, w_ffn_out = full
    gains = jnp.pad(jnp.stack([gain_attn, gain_ffn], 1), ((0, 0), (0, 126)))
    return (
        (halves_of(w_query, w_key, w_value, jnp.concatenate([gains, gains], 1)),),
        (halves_of(w_attn_out, w_ffn_in),),
        (w_ffn_out,),
    )


def gain_back(gain, weights, grads):
    return sum(
        jnp.sum(weight.astype(jnp.float32) * grad, axis=1) for weight, grad in zip(weights, grads)
    ) / gain.astype(jnp.float32)


def per_device(
    tokens,
    lengths,
    gain_attn,
    w_query,
    w_key,
    w_value,
    w_attn_out,
    gain_ffn,
    w_ffn_in,
    w_ffn_out,
    bucket_bias_matrix,
    cotangent,
):
    slot_count, width = tokens.shape
    heads = bucket_bias_matrix.shape[1]
    devices = lax.axis_size("fsdp")
    factor = 1.0 / math.sqrt(slot_count * devices)
    place = lax.axis_index("fsdp").astype(jnp.int32)[None]
    side = width // 2
    by_chips = devices == 32
    pairs = heads // 2
    done, shared, backs = [0], [], []

    def forward(count, after=()):
        out, prob, token = attend(
            lengths, query, key, value, planes, done[0], count, tuple(shared), after
        )
        done[0] += count
        shared[:] = [out, prob]
        return token

    def backward(count, after=()):
        first = sum(some[0].shape[1] for some in backs) * heads // (2 * width)
        result = attend_back(
            query, key, value, grad_attended, prob, first, count, heads, after
        )
        backs.append(result[:4])
        return result[4]

    def weights(after=()):
        return weights_back(
            place,
            tokens,
            gains,
            [some[:3] for some in backs],
            [some[3] for some in backs],
            by_chips,
            after,
        )

    def inputs(first, count, done=None, after=()):
        return inputs_back(
            place,
            tokens,
            gains,
            grad_hidden,
            [some[:3] for some in backs],
            in_qkv,
            by_chips,
            first,
            count,
            done,
            after,
        )

    if by_chips:
        mine_qkv, for_qkv, mine_in, for_in = pack_halves(
            place,
            gain_attn[None],
            gain_ffn[None],
            (w_query, w_key, w_value),
            (w_attn_out, w_ffn_in),
        )
        unit, token = chip_unit(place, mine_qkv, swap(for_qkv, 1))
        line = gather_line(unit)
        planes, token = bias_planes(bucket_bias_matrix, (token,))

        (near_qkv, unit), token = stack_and_copy(line, w_ffn_out, (token,))
        plane_qkv = gather_plane(near_qkv)
        line = gather_line(unit)

        parts, token = far_and_stack(*plane_qkv, (), line + (token,))
        far_qkv = gather_far(*parts)
        other_qkv = (swap(near_qkv, 1), swap(plane_qkv[0], 1), swap(plane_qkv[1], 1))

        (near_out, unit), token = stack_and_unit(
            place, line, mine_in, swap(for_in, 1), far_qkv + other_qkv + (token,)
        )
        other_qkv = other_qkv + (swap(far_qkv[0], 1), swap(far_qkv[1], 1))
        plane_out = gather_plane(near_out)
        in_qkv = (near_qkv,) + plane_qkv + far_qkv + other_qkv
        query, key, value, gains, token = project_qkv(
            place, tokens, in_qkv, by_chips, (planes, token)
        )

        (far_x, far_y, unit), token = far_and_stack(*plane_out, (unit,), (token,))
        far_out = gather_far(far_x, far_y)
        line = gather_line(unit[0])
        token = forward(2, (token,))

        (near_in,), token = stack_units(line, far_out + (token,))
        plane_in = gather_plane(near_in)
        other_out = (swap(near_out, 1), swap(plane_out[0], 1), swap(plane_out[1], 1))
        token = forward(2, (token,))

        parts, token = far_and_stack(*plane_in, (), other_out + (token,))
        far_in = gather_far(*parts)
        other_in = (swap(near_in, 1),)
        other_out = other_out + (swap(far_out[0], 1), swap(far_out[1], 1))
        token = forward(1, (token,))

        parts, token = copied(far_in + plane_in, other_in + other_out[3:] + (token,))
        other_in = other_in + tuple(swap(part, 1) for part in (parts[2], parts[3], parts[0], parts[1]))
        token = forward(1, (token,))

        in_ffn = (near_in,) + plane_in + far_in + other_in
        in_out = (near_out,) + plane_out + far_out + other_out
    else:
        planes, _ = bias_planes(bucket_bias_matrix)
        in_qkv, in_ffn, in_out = gather_plain(
            (gain_attn, w_query, w_key, w_value, w_attn_out, gain_ffn, w_ffn_in, w_ffn_out)
        )
        query, key, value, gains, _ = project_qkv(place, tokens, in_qkv, by_chips)
        for _ in range(pairs):
            forward(1)

    attended, prob = [shared[0]], shared[1]
    (output, grad_hidden, grad_attended), saved, part_out = feed_forward(
        place, tokens, attended, cotangent, gains, in_ffn, in_out, by_chips
    )

    if by_chips:
        keep_out, send_out = part_out
        got_out = swap(send_out, 1)
        (keep_in, send_in), token = in_weights_back(place, attended, *saved, by_chips)

        sends, token = first_sends(keep_out, got_out, (token,))
        first_out = scatter_first(sends)
        got_in = swap(send_in, 1)
        token = backward(2, (token,))

        sends, token = second_sends(keep_out, got_out, first_out, (got_in, token))
        second_out = scatter_second(sends)
        token = backward(1, (token,))

        sums, token = line_sums(keep_out, got_out, first_out, second_out, (token,))
        last_out = scatter_line(sums)
        sends, token = first_sends(keep_in, got_in, (token,))
        first_in = scatter_first(sends)
        token = backward(2, (token,))

        sends, token = second_sends(keep_in, got_in, first_in, last_out + (token,))
        second_in = scatter_second(sends)
        token = backward(1, (token,))

        sums, token = line_sums(keep_in, got_in, first_in, second_in, (token,))
        last_in = scatter_line(sums)
        (keep_qkv, send_qkv), table, token = weights(last_out + (token,))

        parts, token = chip_sum_halves(place, last_in, (send_qkv, table), (token,))
        mine_in, for_in, send_qkv, table = parts
        got_qkv, got_in, got = swap(send_qkv, 1), swap(for_in, 1), swap(table, 1)
        grad_tokens, token = inputs(0, slot_count // 2, None, (token,))

        parts, token = first_sends(keep_qkv, got_qkv, (got_in, token), (table, got))
        first_qkv = scatter_first(parts[:2])
        table, got = parts[2], swap(parts[2], 2)
        grad_tokens, token = inputs(slot_count // 2, slot_count // 2, grad_tokens, (token,))

        parts, token = second_sends(keep_qkv, got_qkv, first_qkv, (token,), (table, got))
        second_qkv = scatter_second(parts[:2])
        table, got = parts[2], swap(parts[2], 4)
        sum_out = add(*last_out) * factor

        parts, token = line_sums(
            keep_qkv, got_qkv, first_qkv, second_qkv, (token,), (table, got)
        )
        last_qkv = scatter_line(parts[:-1])
        table, got = parts[-1], swap(parts[-1], 8)
        sum_o, sum_in, grad_gain_ffn = join_halves(
            place,
            mine_in,
            got_in,
            (side, keep_in.shape[-1] - side),
            factor,
            gain_ffn,
            (w_ffn_in,),
            (token,),
        )

        parts, token = chip_sum_halves(place, last_qkv, (), (token,), (table, got))
        mine_qkv, for_qkv, table = parts
        got_qkv, got = swap(for_qkv, 1), swap(table, 16)
        table = table + got
        sum_q, sum_k, sum_v, grad_gain_attn = join_halves(
            place,
            mine_qkv,
            got_qkv,
            (side, side, side),
            factor,
            gain_attn,
            (w_query, w_key, w_value),
        )
        grad_gain_attn, grad_gain_ffn = grad_gain_attn[:, 0], grad_gain_ffn[:, 0]
        sums = (sum_q, sum_k, sum_v, sum_o, sum_in, sum_out)
    else:
        for _ in range(pairs):
            backward(1)
        part_in, _ = in_weights_back(place, attended, *saved, by_chips)
        part_qkv, table, _ = weights()
        grad_tokens, _ = inputs(0, slot_count)
        sums = sum_plain(
            jnp.concatenate([part_qkv[0], part_in[0][:, :, :side]], 2),
            part_in[0][:, :, side:],
            part_out[0],
        )
        sums = [total * factor for total in sums]
        table = lax.psum(table, "fsdp")
        grad_gain_attn = gain_back(gain_attn, (w_query, w_key, w_value), sums[:3])
        grad_gain_ffn = gain_back(gain_ffn, (w_ffn_in,), sums[4:5])

    return (
        output,
        grad_tokens,
        grad_gain_attn,
        sums[0],
        sums[1],
        sums[2],
        sums[3],
        grad_gain_ffn,
        sums[4],
        sums[5],
        table[:heads, :NB].T * factor,
    )


def solution(mesh):
    placed = (
        P("fsdp", None),
        P("fsdp", None),
        P("fsdp"),
        P("fsdp", None),
        P("fsdp", None),
        P("fsdp", None),
        P("fsdp", None),
        P("fsdp"),
        P("fsdp", None),
        P("fsdp", None),
        P(),
        P("fsdp", None),
    )
    return jax.shard_map(
        per_device,
        mesh=mesh,
        in_specs=placed,
        out_specs=(
            P("fsdp", None),
            P("fsdp", None),
            P("fsdp"),
            P("fsdp", None),
            P("fsdp", None),
            P("fsdp", None),
            P("fsdp", None),
            P("fsdp"),
            P("fsdp", None),
            P("fsdp", None),
            P(),
        ),
        check_vma=False,
    )
```

```python
import functools
import math

import jax
import jax.numpy as jnp
import numpy as np
from jax import lax
from jax.experimental import pallas as pl
from jax.experimental.pallas import tpu as pltpu
from jax.sharding import PartitionSpec as P

NB = 32
MAXD = 128
SEQ = 512
MIB = 1024 * 1024


def bucket_ids(span_length):
    offset = np.arange(span_length)[None, :] - np.arange(span_length)[:, None]
    half_count = NB // 2
    exact_count = half_count // 2
    result = np.where(offset > 0, half_count, 0)
    distance = np.abs(offset)
    spread = exact_count + np.floor(
        np.log(np.maximum(distance, 1) / exact_count)
        / math.log(MAXD / exact_count)
        * (half_count - exact_count)
    )
    spread = np.minimum(spread, half_count - 1)
    result = result + np.where(distance < exact_count, distance, spread)
    return result.astype(np.int32)


def flip(mask, count):
    return [(i, i ^ mask) for i in range(count)]


def swap(array, mask):
    return lax.ppermute(array, "fsdp", flip(mask, lax.axis_size("fsdp")))


def gather_line(unit):
    line = lax.axis_size("fsdp") // 8
    return (unit,) + tuple(swap(unit, 8 * hop) for hop in range(1, line))


def gather_plane(near):
    return swap(near, 2), swap(near, 4)


def gather_far(first, second):
    return swap(first, 2), swap(second, 4)


def chip_distances():
    line = lax.axis_size("fsdp") // 8
    half = line // 2
    blocks = []
    for part, (plane, first, last) in enumerate(
        ((0, 0, line), (1, 0, line), (2, 0, line), (3, 0, half), (3, half, line))
    ):
        blocks += [(part, hop - first, 4 * hop + plane) for hop in range(first, last)]
    return blocks


def add(*terms):
    return sum(term.astype(jnp.float32) for term in terms)


def scatter_first(sends):
    return swap(sends[0], 2), swap(sends[1], 4)


def scatter_second(sends):
    return swap(sends[0], 4), swap(sends[1], 2)


def scatter_line(sums):
    return (sums[0],) + tuple(swap(total, 8 * hop) for hop, total in enumerate(sums) if hop)


def halves_of(*arrays):
    return jnp.stack(
        [
            jnp.concatenate(
                [
                    array[:, part * array.shape[1] // 2 : (part + 1) * array.shape[1] // 2]
                    for array in arrays
                ],
                1,
            )
            for part in range(2)
        ]
    )


def sum_plain(half_attn, half_in, grad_out):
    side = half_attn.shape[-1] // 4

    def owned(array):
        return lax.psum_scatter(
            array.astype(jnp.float32), "fsdp", scatter_dimension=0, tiled=True
        )

    grads = [
        jnp.concatenate([part[0], part[1]], 1)
        for part in [half_attn[:, :, k * side : (k + 1) * side] for k in range(4)] + [half_in]
    ]
    return [owned(grad) for grad in grads + [grad_out]]


def nn(left, right):
    return lax.dot_general(
        left, right, (((1,), (0,)), ((), ())), preferred_element_type=jnp.float32
    )


def nt(left, right):
    return lax.dot_general(
        left, right, (((1,), (1,)), ((), ())), preferred_element_type=jnp.float32
    )


def tn(left, right):
    return lax.dot_general(
        left, right, (((0,), (0,)), ((), ())), preferred_element_type=jnp.float32
    )


def low(value):
    return value.astype(jnp.bfloat16)


def wide(value):
    return value.astype(jnp.float32)


def norm_scale(values):
    return lax.rsqrt(jnp.mean(values * values, axis=-1, keepdims=True) + 1e-06)


def rms_back(scaled, scale, gain, grad_normed):
    weighted = grad_normed * gain
    return scale * (weighted - scaled * jnp.mean(weighted * scaled, axis=-1, keepdims=True))


IN_HBM = pl.BlockSpec(memory_space=pl.ANY)
IN_SMEM = pl.BlockSpec(memory_space=pltpu.SMEM)
IN_VMEM = pl.BlockSpec(memory_space=pltpu.VMEM)
TOKEN_SHAPE = jax.ShapeDtypeStruct((1, 1), jnp.float32)
TOKEN = pl.BlockSpec((1, 1), lambda *_: (0, 0), memory_space=pltpu.SMEM)


def cost(flops, bytes_moved):
    return pl.CostEstimate(flops=flops, bytes_accessed=bytes_moved, transcendentals=0)


def plan(me, rows, by_chips, side, per_core):
    chip, core = me // 2, me % 2
    if not by_chips:
        return []
    count = 5
    found = []
    for part, index, distance in chip_distances():
        number = chip ^ distance
        if per_core:
            number = number * 2 + (core ^ side)
        found.append((side * count + part, index, pl.multiple_of(number * rows, 16)))
    return found


def column_copies(me, sources, target, sems, side, by_chips, columns):
    first, last = columns
    if not by_chips:
        half = (me % 2) ^ side
        return [
            pltpu.make_async_copy(sources[0].at[half, :, pl.ds(first, last - first)], target, sems.at[0])
        ]
    rows = sources[0].shape[1]
    return [
        pltpu.make_async_copy(
            sources[part].at[index, :, pl.ds(first, last - first)],
            target.at[pl.ds(start, rows), :],
            sems.at[number],
        )
        for number, (part, index, start) in enumerate(plan(me, rows, True, side, False))
    ]


def row_copies(me, sources, target, sems, side, by_chips):
    if not by_chips:
        half = target.shape[0] // 2
        where = pl.ds(side * half, half)
        return [pltpu.make_async_copy(sources[0].at[where, :], target.at[where, :], sems.at[0])]
    rows = sources[0].shape[1]
    return [
        pltpu.make_async_copy(
            sources[part].at[index], target.at[pl.ds(start, rows), :], sems.at[number]
        )
        for number, (part, index, start) in enumerate(plan(me, rows, True, side, True))
    ]


def start_all(copies):
    for copy in copies:
        copy.start()


def wait_all(copies):
    for copy in copies:
        copy.wait()


def half_copies(me, tile, targets, sems, side, by_chips, columns):
    first, count = columns
    if not by_chips:
        half = (me % 2) ^ side
        return [
            pltpu.make_async_copy(tile, targets[0].at[half, :, pl.ds(first, count)], sems.at[0])
        ]
    planes, line, rows = targets[side].shape[:3]
    chip = me // 2
    return [
        pltpu.make_async_copy(
            tile.at[pl.ds(pl.multiple_of((chip ^ (4 * hop + plane)) * rows, 16), rows), :],
            targets[side].at[plane, hop, :, pl.ds(first, count)],
            sems.at[plane * line + hop],
        )
        for plane in range(planes)
        for hop in range(line)
    ]


def strip_copies(me, tile, targets, sems, strip, by_chips):
    if not by_chips:
        rows = tile.shape[0]
        return [
            pltpu.make_async_copy(
                tile, targets[0].at[pl.ds(pl.multiple_of(strip * rows, 16), rows), :], sems.at[0]
            )
        ]
    planes, line, rows = targets[0].shape[:3]
    chip, core = me // 2, me % 2
    return [
        pltpu.make_async_copy(
            tile.at[
                pl.ds(pl.multiple_of((((chip % 4) ^ plane) * 2 + (core ^ side)) * rows, 16), rows), :
            ],
            targets[side].at[plane, (chip // 4) ^ strip],
            sems.at[side * planes + plane],
        )
        for side in range(2)
        for plane in range(planes)
    ]


def bias_planes(table, after=()):
    heads = table.shape[1]
    ids = bucket_ids(SEQ)
    flat = np.concatenate([ids[:, 0], ids[0, :1], ids[0, :0:-1]])
    onehot = (np.arange(table.shape[0])[:, None] == flat[None, :]).astype(np.float32)

    def kernel(table_ref, onehot_ref, *refs):
        plane_ref, token_ref, rows = refs[len(after) :]
        token_ref[0, 0] = 0.0
        head = pl.program_id(0)

        @pl.when(head == 0)
        def _():
            rows[:heads] = lax.dot_general(
                wide(table_ref[...]),
                onehot_ref[...],
                (((0,), (0,)), ((), ())),
                precision=lax.Precision.HIGHEST,
                preferred_element_type=jnp.float32,
            )

        spread = jnp.broadcast_to(rows[pl.ds(head, 1), :], (SEQ, 2 * SEQ))
        moved = pltpu.roll(spread, 0, 1, stride=1, stride_axis=0)
        plane_ref[0] = low(moved[:, :SEQ])

    return pl.pallas_call(
        kernel,
        grid=(heads,),
        out_shape=[jax.ShapeDtypeStruct((heads, SEQ, SEQ), jnp.bfloat16), TOKEN_SHAPE],
        in_specs=[IN_VMEM, IN_VMEM] + [IN_HBM] * len(after),
        out_specs=[pl.BlockSpec((1, SEQ, SEQ), lambda head: (head, 0, 0)), TOKEN],
        scratch_shapes=[pltpu.VMEM((-(-heads // 8) * 8, 2 * SEQ), jnp.float32)],
        compiler_params=pltpu.CompilerParams(vmem_limit_bytes=16 * MIB),
    )(table, jnp.asarray(onehot), *after)


def line_ids():
    ids = bucket_ids(SEQ)
    ahead = (np.arange(2 * SEQ) - (SEQ - 128) + SEQ) % (2 * SEQ) - SEQ
    return np.where(ahead >= 0, ids[np.maximum(ahead, 0), 0], ids[0, np.minimum(-ahead, SEQ - 1)])


def project_qkv(place, tokens, sources, by_chips, after=()):
    slots, width = tokens.shape
    side_cols = width // 2
    packed = sources[0].shape[-1]
    block = 256

    def kernel(place_ref, x_hbm, *refs):
        ins = refs[: len(sources)]
        q_ref, k_ref, v_ref, gains_ref, token_ref, *refs = refs[len(sources) + len(after) :]
        x, weights, normed, x_sem, sems = refs
        token_ref[0, 0] = 0.0
        me = place_ref[0]
        core = me % 2
        x_load = pltpu.make_async_copy(x_hbm, x, x_sem.at[0])
        copies = [
            column_copies(
                me, ins, weights.at[side], sems.at[side], side, by_chips, (0, packed)
            )
            for side in range(2)
        ]
        start_all(copies[0])
        x_load.start()
        start_all(copies[1])
        wait_all(copies[0])
        gains = jnp.transpose(wide(weights[0, :, 3 * side_cols :]))
        gains_ref[...] = gains[:8]
        x_load.wait()

        def normalise(index, carry):
            where = pl.ds(pl.multiple_of(index * block, block), block)
            rows = wide(x[where, :])
            normed[where, :] = low(rows * norm_scale(rows) * gains_ref[0:1, :])
            return carry

        lax.fori_loop(0, slots // block, normalise, 0)
        for side in range(2):
            if side:
                wait_all(copies[1])
            cols = pl.ds(pl.multiple_of((core ^ side) * side_cols, 128), side_cols)
            for part, out in enumerate((q_ref, k_ref, v_ref)):
                here = slice(part * side_cols, (part + 1) * side_cols)
                out[:, cols] = low(nn(normed[...], weights[side, :, here]))

    flat = jax.ShapeDtypeStruct((slots, width), jnp.bfloat16)
    return pl.pallas_call(
        kernel,
        out_shape=[flat] * 3 + [jax.ShapeDtypeStruct((8, width), jnp.float32), TOKEN_SHAPE],
        in_specs=[IN_SMEM] + [IN_HBM] * (1 + len(sources) + len(after)),
        out_specs=[IN_VMEM] * 4 + [IN_SMEM],
        scratch_shapes=[
            pltpu.VMEM((slots, width), jnp.bfloat16),
            pltpu.VMEM((2, width, packed), jnp.bfloat16),
            pltpu.VMEM((slots, width), jnp.bfloat16),
            pltpu.SemaphoreType.DMA((1,)),
            pltpu.SemaphoreType.DMA((2, 16)),
        ],
        compiler_params=pltpu.CompilerParams(vmem_limit_bytes=24 * MIB),
        cost_estimate=cost(6 * slots * width * width, 12 * slots * width),
    )(place, tokens, *sources, *after)


def attend(lengths, query, key, value, planes, first, count, shared=(), after=()):
    slots, width = query.shape
    seqs = slots // SEQ
    heads = planes.shape[0]
    pair_cols = 2 * width // heads
    head_size = pair_cols // 2

    def kernel(lengths_ref, q, k, v, planes_ref, *refs):
        out, prob_hbm, token_ref, scores, prob, prob_sems = refs[len(shared) + len(after) :]
        token_ref[0, 0] = 0.0

        def prob_store(step):
            slot = step % 2
            return pltpu.make_async_copy(
                prob.at[slot],
                prob_hbm.at[step % seqs, pl.ds(2 * (first + step // seqs), 2)],
                prob_sems.at[slot],
            )

        own_lane = lax.broadcasted_iota(jnp.int32, (1, pair_cols), 1) < head_size
        key_number = lax.broadcasted_iota(jnp.int32, (SEQ, 1), 0)
        zero = jnp.zeros((), jnp.bfloat16)

        def both_heads(rows):
            return jnp.concatenate(
                [jnp.where(own_lane, rows, zero), jnp.where(own_lane, zero, rows)], 0
            )

        def one(step, carry):
            pair, seq = step // seqs, step % seqs
            slot = step % 2
            rows = pl.ds(pl.multiple_of(seq * SEQ, SEQ), SEQ)
            own = pl.ds(pl.multiple_of(pair * pair_cols, pair_cols), pair_cols)
            lanes = pl.ds(pl.multiple_of((first + pair) * pair_cols, pair_cols), pair_cols)

            @pl.when(step >= 2)
            def _():
                prob_store(step - 2).wait()

            permitted = key_number < lengths_ref[seq, 0] + lengths_ref[seq, 1]
            scores[...] = nt(both_heads(k[rows, lanes]), q[rows, lanes])
            for head in range(2):
                these = scores[head * SEQ : (head + 1) * SEQ, :] + wide(planes_ref[2 * (first + pair) + head])
                these = jnp.where(permitted, these, -1e30)
                raised = jnp.exp(these - jnp.max(these, axis=0, keepdims=True))
                total = jnp.sum(raised, axis=0, keepdims=True)
                prob[slot, head] = low(raised * (1.0 / total))
            mixed = tn(prob[slot].reshape(2 * SEQ, SEQ), both_heads(v[rows, lanes]))
            out[rows, own] = low(mixed)
            prob_store(step).start()
            return carry

        lax.fori_loop(0, count * seqs, one, 0)
        for step in range(max(0, count * seqs - 2), count * seqs):
            prob_store(step).wait()

    return pl.pallas_call(
        kernel,
        out_shape=[
            jax.ShapeDtypeStruct((slots, count * pair_cols), jnp.bfloat16),
            jax.ShapeDtypeStruct((seqs, heads, SEQ, SEQ), jnp.bfloat16),
            TOKEN_SHAPE,
        ],
        in_specs=[IN_SMEM] + [IN_VMEM] * 4 + [IN_HBM] * (len(shared) + len(after)),
        out_specs=[IN_VMEM, IN_HBM, IN_SMEM],
        scratch_shapes=[
            pltpu.VMEM((2 * SEQ, SEQ), jnp.float32),
            pltpu.VMEM((2, 2, SEQ, SEQ), jnp.bfloat16),
            pltpu.SemaphoreType.DMA((2,)),
        ],
        compiler_params=pltpu.CompilerParams(vmem_limit_bytes=16 * MIB),
        cost_estimate=cost(count * slots * SEQ * 2048, count * slots * SEQ * 8),
        input_output_aliases={5: 1} if shared else {},
    )(lengths, query, key, value, planes, *shared, *after)


def attend_back(query, key, value, grad_mixed, prob, first, count, heads, after=()):
    slots, width = query.shape
    seqs = slots // SEQ
    pair_cols = 2 * width // heads
    head_size = pair_cols // 2
    steps = count * seqs

    def kernel(q, k, v, g, prob_hbm, *refs):
        dq, dk, dv, table_ref, token_ref, prob, grads, scored, planes, prob_sems = refs[len(after) :]
        token_ref[0, 0] = 0.0

        def prob_load(step):
            slot = step % 2
            return pltpu.make_async_copy(
                prob_hbm.at[step % seqs, pl.ds(2 * (first + step // seqs), 2)],
                prob.at[slot],
                prob_sems.at[slot],
            )

        prob_load(0).start()
        own_lane = lax.broadcasted_iota(jnp.int32, (1, pair_cols), 1) < head_size
        zero = jnp.zeros((), jnp.bfloat16)

        def both_heads(rows):
            return jnp.concatenate(
                [jnp.where(own_lane, rows, zero), jnp.where(own_lane, zero, rows)], 0
            )

        def one(step, carry):
            pair, seq = step // seqs, step % seqs
            slot = step % 2
            rows = pl.ds(pl.multiple_of(seq * SEQ, SEQ), SEQ)
            own = pl.ds(pl.multiple_of(pair * pair_cols, pair_cols), pair_cols)
            lanes = pl.ds(pl.multiple_of((first + pair) * pair_cols, pair_cols), pair_cols)

            @pl.when(step + 1 < steps)
            def _():
                prob_load(step + 1).start()

            grads[...] = nt(both_heads(v[rows, lanes]), g[rows, lanes])
            prob_load(step).wait()
            summed = nn(prob[slot].reshape(2 * SEQ, SEQ), g[rows, lanes])
            dv[rows, own] = low(jnp.where(own_lane, summed[:SEQ], summed[SEQ:]))
            keep = jnp.where(seq == 0, 0.0, 1.0)
            for head in range(2):
                there = slice(head * SEQ, (head + 1) * SEQ)
                weights = wide(prob[slot, head])
                weighted = weights * grads[there, :]
                dot = jnp.sum(weighted, axis=0, keepdims=True)
                grad_scores = weighted - weights * dot
                planes[head] = planes[head] * keep + grad_scores
                scored[there, :] = low(grad_scores)
            summed = nn(scored[...], q[rows, lanes])
            dk[rows, own] = low(jnp.where(own_lane, summed[:SEQ], summed[SEQ:]))
            dq[rows, own] = low(tn(scored[...], both_heads(k[rows, lanes])))

            @pl.when(seq == seqs - 1)
            def _():
                for head in range(2):
                    lined = jnp.zeros((8, 2 * SEQ), jnp.float32)
                    for low_row in range(0, 128, 8):
                        frame = jnp.zeros((8, 2 * SEQ), jnp.float32)
                        for high_row in range(0, SEQ, 128):
                            some = planes[head, high_row + low_row : high_row + low_row + 8, :]
                            ahead = SEQ - 128 - high_row
                            filled = [some, jnp.zeros((8, SEQ - ahead), jnp.float32)]
                            if ahead:
                                filled = [jnp.zeros((8, ahead), jnp.float32)] + filled
                            frame = frame + jnp.concatenate(filled, 1)
                        if low_row:
                            frame = pltpu.roll(frame, 2 * SEQ - low_row, 1)
                        lined = lined + frame
                    moved = lined[:1]
                    for row in range(1, 8):
                        moved = moved + pltpu.roll(lined[row : row + 1], 2 * SEQ - row, 1)
                    table_ref[pair, head : head + 1, :] = moved

            return carry

        planes[...] = jnp.zeros_like(planes)
        lax.fori_loop(0, steps, one, 0)

    result = jax.ShapeDtypeStruct((slots, count * pair_cols), jnp.bfloat16)
    return pl.pallas_call(
        kernel,
        in_specs=[IN_VMEM] * 4 + [IN_HBM] * (1 + len(after)),
        out_specs=[IN_VMEM] * 4 + [IN_SMEM],
        out_shape=[result] * 3
        + [jax.ShapeDtypeStruct((count, 8, 2 * SEQ), jnp.float32), TOKEN_SHAPE],
        scratch_shapes=[
            pltpu.VMEM((2, 2, SEQ, SEQ), jnp.bfloat16),
            pltpu.VMEM((2 * SEQ, SEQ), jnp.float32),
            pltpu.VMEM((2 * SEQ, SEQ), jnp.bfloat16),
            pltpu.VMEM((2, SEQ, SEQ), jnp.float32),
            pltpu.SemaphoreType.DMA((2,)),
        ],
        compiler_params=pltpu.CompilerParams(vmem_limit_bytes=20 * MIB),
        cost_estimate=cost(count * slots * SEQ * 4096, count * slots * SEQ * 8),
    )(query, key, value, grad_mixed, prob, *after)


def feed_forward(place, tokens, attended, cotangent, gains, in_sources, out_sources, by_chips):
    slots, width = tokens.shape
    side_cols = width // 2
    hidden_cols = 2 * (in_sources[0].shape[-1] - side_cols)
    block = 256
    blocks = slots // block
    chunk = 768
    per_side = hidden_cols // 2 // chunk
    count_att = len(attended)
    root, bend = math.sqrt(2.0 / math.pi), 0.044715

    def kernel(place_ref, x_hbm, cot_hbm, gains_ref, *refs):
        refs = list(refs)

        def take(number):
            taken, refs[:] = refs[:number], refs[number:]
            return taken

        att_hbm, in_hbm, out_hbm = take(count_att), take(len(in_sources)), take(len(out_sources))
        y_hbm, grad_hbm, back_hbm, branch_hbm, flipped_hbm, pre_hbm = take(6)
        out_targets = take(2 if by_chips else 1)
        x, att, cot, w_o, w_in, w_out, hidden, normed, flipped = take(9)
        sum_g, act, grad_pre, tile_out = take(4)
        load_sems, o_sems, in_sems, out_sems, store_sems, pre_sems, tile_out_sems = take(7)
        me = place_ref[0]
        core = me % 2
        gain = gains_ref[1:2, :]

        def rows_of(index):
            return pl.ds(pl.multiple_of(index * block, block), block)

        loads = [
            pltpu.make_async_copy(x_hbm, x, load_sems.at[0]),
            pltpu.make_async_copy(cot_hbm, cot, load_sems.at[1]),
        ]
        cols = 0
        for number, source in enumerate(att_hbm):
            loads.append(
                pltpu.make_async_copy(
                    source, att.at[:, pl.ds(cols, source.shape[1])], load_sems.at[2 + number]
                )
            )
            cols += source.shape[1]
        o_loads, in_loads, out_loads = [], [], []
        for side in range(2):
            o_cols = pl.ds(pl.multiple_of((core ^ side) * side_cols, 128), side_cols)
            o_loads += column_copies(
                me, in_hbm, w_o.at[:, o_cols], o_sems.at[side], side, by_chips, (0, side_cols)
            )
            in_loads.append(
                column_copies(
                    me,
                    in_hbm,
                    w_in.at[side],
                    in_sems.at[side],
                    side,
                    by_chips,
                    (side_cols, in_sources[0].shape[-1]),
                )
            )
            out_loads += row_copies(me, out_hbm, w_out, out_sems.at[side], side, by_chips)
        start_all(loads)
        start_all(o_loads)
        start_all(in_loads[0])
        start_all(out_loads)
        start_all(in_loads[1])
        wait_all(loads)
        wait_all(o_loads)

        parts = [slice(first, first + block) for first in range(0, width, block)]
        for cols in parts:
            hidden[:, cols] = wide(x[:, cols]) + nn(att[...], w_o[:, cols])

        def before(index, carry):
            where = rows_of(index)
            value = hidden[where, :]
            rows = value * norm_scale(value) * gain
            normed[where, :] = low(rows)
            flipped[:, where] = low(jnp.transpose(rows))
            return carry

        lax.fori_loop(0, blocks, before, 0)
        flip_store = pltpu.make_async_copy(flipped, flipped_hbm, store_sems.at[3])
        flip_store.start()
        wait_all(in_loads[0])
        wait_all(out_loads)

        stores, pre_stores = [], []
        for side in range(2):
            if side:
                wait_all(in_loads[1])
            for part in range(per_side):
                number = side * per_side + part
                strip = (core ^ side) * per_side + part
                for first in range(0, chunk, block):
                    unit_rows = pl.ds(pl.multiple_of(strip * chunk + first, block), block)
                    unit_cols = slice(part * chunk + first, part * chunk + first + block)
                    pre = nn(normed[...], w_in[side, :, unit_cols])
                    square = pre * pre
                    slope = jnp.tanh(pre * (root + (root * bend) * square))
                    opened = 0.5 + 0.5 * slope
                    gate = opened + pre * (1.0 - slope * slope) * (
                        0.5 * root + (1.5 * bend * root) * square
                    )
                    act[side, :, unit_cols] = low(pre * opened)
                    grad_pre[side, :, unit_cols] = low(nt(cot[...], w_out[unit_rows, :]) * gate)
                slot = number % 2
                if number >= 2:
                    wait_all(stores[number - 2])
                for first in range(0, chunk, block):
                    units = slice(part * chunk + first, part * chunk + first + block)
                    tile_out[slot, first : first + block, :] = low(
                        tn(act[side, :, units], cot[...])
                    )
                copies = strip_copies(
                    me, tile_out.at[slot], out_targets, tile_out_sems.at[slot], strip, by_chips
                )
                units = pl.ds(part * chunk, chunk)
                copies.append(
                    pltpu.make_async_copy(
                        grad_pre.at[side, :, units], pre_hbm.at[strip], pre_sems.at[number]
                    )
                )
                start_all(copies)
                stores.append(copies[:-1])
                pre_stores.append(copies[-1])

        half = hidden_cols // 2
        halves = [pl.ds(pl.multiple_of((core ^ side) * half, block), half) for side in range(2)]
        for cols in parts:
            value = nn(act[0], w_out[halves[0], cols]) + nn(act[1], w_out[halves[1], cols])
            x[:, cols] = low(hidden[:, cols] + value)
        for cols in parts:
            sum_g[:, cols] = nt(grad_pre[0], w_in[0, cols, :]) + nt(grad_pre[1], w_in[1, cols, :])

        def after(index, carry):
            where = rows_of(index)
            value = hidden[where, :]
            scale = norm_scale(value)
            scaled = value * scale
            grad = wide(cot[where, :]) + rms_back(scaled, scale, gain, sum_g[where, :])
            sum_g[where, :] = grad
            normed[where, :] = low(grad)
            return carry

        lax.fori_loop(0, blocks, after, 0)
        for cols in parts:
            att[:, cols] = low(nt(normed[...], w_o[cols, :]))
        last = [
            pltpu.make_async_copy(x, y_hbm, store_sems.at[0]),
            pltpu.make_async_copy(sum_g, grad_hbm, store_sems.at[1]),
            pltpu.make_async_copy(att, back_hbm, store_sems.at[2]),
            pltpu.make_async_copy(normed, branch_hbm, store_sems.at[4]),
        ]
        start_all(last)
        wait_all(stores[-2] + stores[-1])
        wait_all(pre_stores)
        wait_all(last)
        flip_store.wait()

    sums = jax.ShapeDtypeStruct
    flat = sums((slots, width), jnp.bfloat16)
    devices = lax.axis_size("fsdp")
    if by_chips:
        line = devices // 8
        out_shapes = [sums((4, line, hidden_cols // devices, width), jnp.bfloat16)] * 2
    else:
        out_shapes = [sums((hidden_cols, width), jnp.bfloat16)]
    outs = [
        flat,
        sums((slots, width), jnp.float32),
        flat,
        flat,
        sums((width, slots), jnp.bfloat16),
        sums((hidden_cols // chunk, slots, chunk), jnp.bfloat16),
    ] + out_shapes
    bf16, f32 = jnp.bfloat16, jnp.float32
    result = pl.pallas_call(
        kernel,
        out_shape=outs,
        in_specs=[IN_SMEM, IN_HBM, IN_HBM, IN_VMEM]
        + [IN_HBM] * (count_att + len(in_sources) + len(out_sources)),
        out_specs=[IN_HBM] * len(outs),
        scratch_shapes=[
            pltpu.VMEM((slots, width), bf16),
            pltpu.VMEM((slots, width), bf16),
            pltpu.VMEM((slots, width), bf16),
            pltpu.VMEM((width, width), bf16),
            pltpu.VMEM((2, width, hidden_cols // 2), bf16),
            pltpu.VMEM((hidden_cols, width), bf16),
            pltpu.VMEM((slots, width), f32),
            pltpu.VMEM((slots, width), bf16),
            pltpu.VMEM((width, slots), bf16),
            pltpu.VMEM((slots, width), f32),
            pltpu.VMEM((2, slots, hidden_cols // 2), bf16),
            pltpu.VMEM((2, slots, hidden_cols // 2), bf16),
            pltpu.VMEM((2, chunk, width), bf16),
            pltpu.SemaphoreType.DMA((2 + count_att,)),
            pltpu.SemaphoreType.DMA((2, 16)),
            pltpu.SemaphoreType.DMA((2, 16)),
            pltpu.SemaphoreType.DMA((2, 16)),
            pltpu.SemaphoreType.DMA((5,)),
            pltpu.SemaphoreType.DMA((2 * per_side,)),
            pltpu.SemaphoreType.DMA((2, 8)),
        ],
        compiler_params=pltpu.CompilerParams(vmem_limit_bytes=56 * MIB),
        cost_estimate=cost(
            slots * width * (12 * hidden_cols + 6 * width), 60 * MIB
        ),
    )(place, tokens, cotangent, gains, *attended, *in_sources, *out_sources)
    return result[:3], result[3:6], result[6:]


def in_weights_back(place, attended, branch, flipped, grad_pre, by_chips):
    slots, width = branch.shape
    strips, _, chunk = grad_pre.shape
    side_cols = width // 2
    per_side = strips // 2
    packed = side_cols + per_side * chunk
    count_att = len(attended)

    def kernel(place_ref, branch_hbm, flipped_hbm, pre_hbm, *refs):
        att_hbm, refs = refs[:count_att], refs[count_att:]
        targets, refs = refs[:-9], refs[-9:]
        token_ref, att, branch, flipped, pre, tile, load_sems, tile_sems, o_sems = refs
        token_ref[0, 0] = 0.0
        me = place_ref[0]
        core = me % 2
        order = [(side, part) for side in (1, 0) for part in range(per_side)]
        pre_loads = [
            pltpu.make_async_copy(
                pre_hbm.at[(core ^ side) * per_side + part], pre.at[number], load_sems.at[number]
            )
            for number, (side, part) in enumerate(order)
        ]
        flip_load = pltpu.make_async_copy(flipped_hbm, flipped, load_sems.at[strips])
        loads = [pltpu.make_async_copy(branch_hbm, branch, load_sems.at[strips + 1])]
        cols = 0
        for number, source in enumerate(att_hbm):
            loads.append(
                pltpu.make_async_copy(
                    source,
                    att.at[:, pl.ds(cols, source.shape[1])],
                    load_sems.at[strips + 2 + number],
                )
            )
            cols += source.shape[1]
        flip_load.start()
        start_all(pre_loads)
        start_all(loads)
        flip_load.wait()
        stores = []
        for number, (side, part) in enumerate(order):
            pre_loads[number].wait()
            slot = number % 2
            if number >= 2:
                wait_all(stores[number - 2])
            for first in range(0, chunk, 256):
                some = slice(first, first + 256)
                tile[slot, :, some] = low(nn(flipped[...], pre[number, :, some]))
            stores.append(
                half_copies(
                    me,
                    tile.at[slot],
                    targets,
                    tile_sems.at[slot],
                    side,
                    by_chips,
                    (side_cols + part * chunk, chunk),
                )
            )
            start_all(stores[-1])
        wait_all(loads)
        slot = len(stores) % 2
        wait_all(stores[-2])
        for third in range(3):
            some = slice(third * width // 3, (third + 1) * width // 3)
            tile[slot, some, :] = low(tn(att[:, some], branch[...]))
        copies = []
        for side in range(2):
            o_cols = pl.ds(pl.multiple_of((core ^ side) * side_cols, 128), side_cols)
            copies += half_copies(
                me,
                tile.at[slot, :, o_cols],
                targets,
                o_sems.at[side],
                side,
                by_chips,
                (0, side_cols),
            )
        start_all(copies)
        wait_all(stores[-1])
        wait_all(copies)

    sums = jax.ShapeDtypeStruct
    bf16 = jnp.bfloat16
    if by_chips:
        line = lax.axis_size("fsdp") // 8
        shapes = [sums((4, line, width // (4 * line), packed), bf16)] * 2
    else:
        shapes = [sums((2, width, packed), bf16)]
    result = pl.pallas_call(
        kernel,
        out_shape=shapes + [TOKEN_SHAPE],
        in_specs=[IN_SMEM, IN_HBM, IN_HBM, IN_HBM] + [IN_HBM] * count_att,
        out_specs=[IN_HBM] * len(shapes) + [IN_SMEM],
        scratch_shapes=[
            pltpu.VMEM((slots, width), bf16),
            pltpu.VMEM((slots, width), bf16),
            pltpu.VMEM((width, slots), bf16),
            pltpu.VMEM((strips, slots, chunk), bf16),
            pltpu.VMEM((2, width, chunk), bf16),
            pltpu.SemaphoreType.DMA((strips + 2 + count_att,)),
            pltpu.SemaphoreType.DMA((2, 16)),
            pltpu.SemaphoreType.DMA((2, 16)),
        ],
        compiler_params=pltpu.CompilerParams(vmem_limit_bytes=56 * MIB),
        cost_estimate=cost(2 * slots * width * (width + strips * chunk), 20 * MIB),
    )(place, branch, flipped, grad_pre, *attended)
    return result[:-1], result[-1]


def back_places(grads, side_cols):
    places, first = [], 0
    for number, some in enumerate(grads):
        for col in range(0, some[0].shape[1], 128):
            half, start = divmod(first + col, side_cols)
            places += [
                (3 * number + part, col, half, part * side_cols + start) for part in range(3)
            ]
        first += some[0].shape[1]
    return [grad for some in grads for grad in some], places


def column_loads(hbm, places, parts, sems, some=slice(None)):
    return [
        pltpu.make_async_copy(
            hbm[number].at[some, pl.ds(col, 128)],
            parts.at[half, :, pl.ds(start, 128)],
            sems.at[count],
        )
        for count, (number, col, half, start) in enumerate(places)
    ]


def weights_back(place, tokens, gains, grads, diagonals, by_chips, after=()):
    slots, width = tokens.shape
    side_cols = width // 2
    flat_grads, places = back_places(grads, side_cols)
    block = 256

    onehot = np.pad(
        (line_ids()[:, None] == np.arange(NB)[None, :]).astype(np.float32), ((0, 0), (0, 128 - NB))
    )
    pairs = len(diagonals)
    heads = sum(2 * some.shape[0] for some in diagonals)
    table_rows = -(-heads // 8) * 8

    def kernel(place_ref, x_hbm, gains_ref, onehot_ref, *refs):
        diag_refs, refs = refs[:pairs], refs[pairs:]
        g_hbm = refs[: len(flat_grads)]
        refs = refs[len(flat_grads) + len(after) :]
        targets, refs = refs[:-8], refs[-8:]
        table_ref, token_ref, x, parts, flipped, tile, load_sems, tile_sems = refs
        token_ref[0, 0] = 0.0
        me = place_ref[0]
        core = me % 2
        first = pltpu.make_async_copy(x_hbm, x, load_sems.at[len(places)])
        first.start()
        loads = column_loads(g_hbm, places, parts, load_sems)
        start_all(loads)
        first.wait()

        def flip(index, carry):
            where = pl.ds(pl.multiple_of(index * block, block), block)
            rows = wide(x[where, :])
            flipped[:, where] = low(jnp.transpose(rows * norm_scale(rows) * gains_ref[0:1, :]))
            return carry

        lax.fori_loop(0, slots // block, flip, 0)
        rows = [
            ref[one, head : head + 1, :]
            for ref in diag_refs
            for one in range(ref.shape[0])
            for head in range(2)
        ]
        if table_rows > heads:
            rows.append(jnp.zeros((table_rows - heads, 2 * SEQ), jnp.float32))
        table_ref[...] = lax.dot_general(
            jnp.concatenate(rows, 0),
            onehot_ref[...],
            (((1,), (0,)), ((), ())),
            precision=lax.Precision.HIGHEST,
            preferred_element_type=jnp.float32,
        )
        wait_all(loads)
        copies = []
        for side in (1, 0):
            before = len(copies)
            half = core ^ side
            for part in range(3):
                some = slice(part * side_cols, (part + 1) * side_cols)
                tile[side, :, some] = low(nn(flipped[...], parts[half, :, some]))
            copies += half_copies(
                me,
                tile.at[side],
                targets,
                tile_sems.at[side],
                side,
                by_chips,
                (0, 3 * side_cols),
            )
            start_all(copies[before:])
        wait_all(copies)

    sums = jax.ShapeDtypeStruct
    if by_chips:
        line = lax.axis_size("fsdp") // 8
        shapes = [sums((4, line, width // (4 * line), 3 * side_cols), jnp.bfloat16)] * 2
    else:
        shapes = [sums((2, width, 3 * side_cols), jnp.bfloat16)]
    result = pl.pallas_call(
        kernel,
        out_shape=shapes + [sums((table_rows, 128), jnp.float32), TOKEN_SHAPE],
        in_specs=[IN_SMEM, IN_HBM, IN_VMEM, IN_VMEM]
        + [IN_VMEM] * pairs
        + [IN_HBM] * (len(flat_grads) + len(after)),
        out_specs=[IN_HBM] * len(shapes) + [IN_VMEM, IN_SMEM],
        scratch_shapes=[
            pltpu.VMEM((slots, width), jnp.bfloat16),
            pltpu.VMEM((2, slots, 3 * side_cols), jnp.bfloat16),
            pltpu.VMEM((width, slots), jnp.bfloat16),
            pltpu.VMEM((2, width, 3 * side_cols), jnp.bfloat16),
            pltpu.SemaphoreType.DMA((len(places) + 1,)),
            pltpu.SemaphoreType.DMA((2, 16)),
        ],
        compiler_params=pltpu.CompilerParams(vmem_limit_bytes=56 * MIB),
        cost_estimate=cost(6 * slots * width * width, 15 * MIB),
    )(place, tokens, gains, jnp.asarray(onehot), *diagonals, *flat_grads, *after)
    return result[:-2], result[-2], result[-1]


def inputs_back(
    place, tokens, gains, grad_hidden, grads, sources, by_chips, first, count, done=None, after=()
):
    slots, width = tokens.shape
    side_cols = width // 2
    packed = sources[0].shape[-1]
    flat_grads, places = back_places(grads, side_cols)
    block = 256
    held = () if done is None else (done,)

    def kernel(place_ref, x_hbm, gh_hbm, gains_ref, *refs):
        g_hbm, refs = refs[: len(flat_grads)], refs[len(flat_grads) :]
        w_hbm, refs = refs[: len(sources)], refs[len(sources) + len(after) + len(held) :]
        out_hbm, token_ref, x, grad, weights, parts, out, summed, load_sems, w_sems, out_sems = refs
        token_ref[0, 0] = 0.0
        me = place_ref[0]
        core = me % 2
        gain = gains_ref[0:1, :]
        some = pl.ds(first, count)
        loads = column_loads(g_hbm, places, parts, load_sems, some) + [
            pltpu.make_async_copy(x_hbm.at[some], x, load_sems.at[len(places)]),
            pltpu.make_async_copy(gh_hbm.at[some], grad, load_sems.at[len(places) + 1]),
        ]
        w_loads = [
            copy
            for side in range(2)
            for copy in column_copies(
                me, w_hbm, weights.at[side], w_sems.at[side], side, by_chips, (0, packed)
            )
        ]
        start_all(w_loads)
        start_all(loads)
        wait_all(w_loads)
        wait_all(loads)

        for first_col in range(0, width, 256):
            cols = slice(first_col, first_col + 256)
            summed[:, cols] = nt(parts[core], weights[0, cols, : 3 * side_cols]) + nt(
                parts[1 - core], weights[1, cols, : 3 * side_cols]
            )

        def finish(index, carry):
            where = pl.ds(pl.multiple_of(index * block, block), block)
            rows = wide(x[where, :])
            scale = norm_scale(rows)
            out[where, :] = low(
                grad[where, :] + rms_back(rows * scale, scale, gain, summed[where, :])
            )
            return carry

        lax.fori_loop(0, count // block, finish, 0)
        last = pltpu.make_async_copy(out, out_hbm.at[some], out_sems.at[0])
        last.start()
        last.wait()

    bf16, f32 = jnp.bfloat16, jnp.float32
    return pl.pallas_call(
        kernel,
        out_shape=[jax.ShapeDtypeStruct((slots, width), bf16), TOKEN_SHAPE],
        in_specs=[IN_SMEM, IN_HBM, IN_HBM, IN_VMEM]
        + [IN_HBM] * (len(flat_grads) + len(sources) + len(after) + len(held)),
        out_specs=[IN_HBM, IN_SMEM],
        scratch_shapes=[
            pltpu.VMEM((count, width), bf16),
            pltpu.VMEM((count, width), f32),
            pltpu.VMEM((2, width, packed), bf16),
            pltpu.VMEM((2, count, 3 * side_cols), bf16),
            pltpu.VMEM((count, width), bf16),
            pltpu.VMEM((count, width), f32),
            pltpu.SemaphoreType.DMA((len(places) + 2,)),
            pltpu.SemaphoreType.DMA((2, 16)),
            pltpu.SemaphoreType.DMA((1,)),
        ],
        compiler_params=pltpu.CompilerParams(vmem_limit_bytes=56 * MIB),
        cost_estimate=cost(6 * count * width * width, 15 * MIB),
        input_output_aliases={4 + len(flat_grads) + len(sources) + len(after): 0} if held else {},
    )(place, tokens, grad_hidden, gains, *flat_grads, *sources, *after, *held)


def pack_halves(place, gain_attn, gain_ffn, shards_qkv, shards_in):
    rows = shards_qkv[0].shape[0]
    groups = (shards_qkv, shards_in)
    counts = [sum(shard.shape[1] for shard in group) // 2 for group in groups]

    def kernel(place_ref, attn_ref, ffn_ref, *refs):
        ins, outs = refs[: -2 * len(groups)], refs[-2 * len(groups) :]
        core = place_ref[0] % 2
        first = 0
        for number, group in enumerate(groups):
            for other in range(2):
                out, col = outs[2 * number + other], 0
                for ref in ins[first : first + len(group)]:
                    half = ref.shape[1] // 2
                    start = pl.multiple_of((core ^ other) * half, 128)
                    out[:, col : col + half] = ref[:, pl.ds(start, half)]
                    col += half
            first += len(group)
        same = lax.broadcasted_iota(jnp.int32, (rows, rows), 0) == lax.broadcasted_iota(
            jnp.int32, (rows, rows), 1
        )
        lane = lax.broadcasted_iota(jnp.int32, (rows, 128), 1)
        cols = jnp.zeros((rows, 128), jnp.float32)
        for number, ref in enumerate((attn_ref, ffn_ref)):
            row = wide(ref[...])
            col = jnp.sum(jnp.where(same, row, 0.0), axis=1, keepdims=True)
            cols = jnp.where(lane == number, col, cols)
        for other in range(2):
            outs[other][:, counts[0] :] = low(cols)

    shapes = [
        jax.ShapeDtypeStruct((rows, count + extra), jnp.bfloat16)
        for count, extra in zip(counts, (128, 0))
        for _ in range(2)
    ]
    return pl.pallas_call(
        kernel,
        out_shape=shapes,
        in_specs=[IN_SMEM] + [IN_VMEM] * (2 + len(shards_qkv) + len(shards_in)),
        out_specs=[IN_VMEM] * len(shapes),
    )(place, gain_attn, gain_ffn, *shards_qkv, *shards_in)


def prepare(compute, operands, shapes, after=(), place=None, pair=()):
    scalars = [] if place is None else [place]

    def kernel(*refs):
        refs = list(refs)
        where = [ref[0] for ref in refs[: len(scalars)]]
        ins, refs = refs[len(scalars) :][: len(operands)], refs[len(scalars) + len(operands) :]
        outs = refs[len(pair) + len(after) :]
        outs[-1][0, 0] = 0.0
        if pair:
            outs[-2][...] = refs[0][...] + refs[1][...]
        compute(*where, ins, outs)

    result = pl.pallas_call(
        kernel,
        out_shape=list(shapes) + [like(array, *array.shape) for array in pair[:1]] + [TOKEN_SHAPE],
        in_specs=[IN_SMEM] * len(scalars)
        + [IN_VMEM] * (len(operands) + len(pair))
        + [IN_HBM] * len(after),
        out_specs=[IN_VMEM] * (len(shapes) + len(pair[:1])) + [IN_SMEM],
        compiler_params=pltpu.CompilerParams(vmem_limit_bytes=8 * MIB),
        cost_estimate=cost(0, sum(2 * array.size for array in operands)),
    )(*scalars, *operands, *pair, *after)
    return result[:-1], result[-1]


def like(array, *shape):
    return jax.ShapeDtypeStruct(shape, array.dtype)


def chip_unit(place, mine, got, after=()):
    def compute(me, ins, outs):
        first = me % 2 == 0
        own, other = wide(ins[0][...]), wide(ins[1][...])
        outs[0][...] = low(
            jnp.concatenate([jnp.where(first, own, other), jnp.where(first, other, own)], 0)
        )

    shape = like(mine, 2 * mine.shape[0], mine.shape[1])
    (unit,), token = prepare(compute, [mine, got], [shape], after, place)
    return unit, token


def stack_and_unit(place, parts, mine, got, after=()):
    def compute(me, ins, outs):
        for number in range(len(parts)):
            outs[0][number] = ins[number][...]
        first = me % 2 == 0
        own, other = wide(ins[-2][...]), wide(ins[-1][...])
        outs[1][...] = low(
            jnp.concatenate([jnp.where(first, own, other), jnp.where(first, other, own)], 0)
        )

    shapes = [
        like(parts[0], len(parts), *parts[0].shape),
        like(mine, 2 * mine.shape[0], mine.shape[1]),
    ]
    operands = list(tuple(parts) + (mine, got))
    return prepare(compute, operands, shapes, after, place)


def stack_and_copies(parts, arrays, after=()):
    def compute(ins, outs):
        for number in range(len(parts)):
            outs[0][number] = ins[number][...]
        for number in range(len(arrays)):
            outs[1 + number][...] = ins[len(parts) + number][...]

    shapes = [like(parts[0], len(parts), *parts[0].shape)]
    shapes += [like(array, *array.shape) for array in arrays]
    return prepare(compute, [*parts, *arrays], shapes, after)


def copied(arrays, after=()):
    def compute(ins, outs):
        for number in range(len(arrays)):
            outs[number][...] = ins[number][...]

    shapes = [like(array, *array.shape) for array in arrays]
    return prepare(compute, list(arrays), shapes, after)


def far_and_copies(over_x, over_y, arrays, after=()):
    half = over_x.shape[0] // 2

    def compute(ins, outs):
        outs[0][...] = ins[0][:half]
        outs[1][...] = ins[1][half:]
        for number in range(len(arrays)):
            outs[2 + number][...] = ins[2 + number][...]

    shapes = [like(over_x, half, *over_x.shape[1:])] * 2
    shapes += [like(array, *array.shape) for array in arrays]
    return prepare(compute, [over_y, over_x, *arrays], shapes, after)


def first_sends(keep, got, after=(), pair=()):
    places = ((3, 0), (1, 0), (3, 1), (2, 1))
    half = keep.shape[1] // 2

    def compute(ins, outs):
        for number, (plane, late) in enumerate(places):
            for hop in range(half):
                at = late * half + hop
                outs[number // 2][number % 2, hop] = low(
                    wide(ins[0][plane, at]) + wide(ins[1][plane, at])
                )

    shapes = [like(keep, 2, half, *keep.shape[2:])] * 2
    return prepare(compute, [keep, got], shapes, after, pair=pair)


def second_sends(keep, got, first, after=(), pair=()):
    half = keep.shape[1] // 2

    def compute(ins, outs):
        for number, (plane, late) in enumerate(((2, 0), (1, 1))):
            for hop in range(half):
                at = late * half + hop
                outs[number][hop] = low(
                    wide(ins[0][plane, at])
                    + wide(ins[1][plane, at])
                    + wide(ins[2 + number][0, hop])
                )

    shapes = [like(keep, half, *keep.shape[2:])] * 2
    return prepare(compute, [keep, got, *first], shapes, after, pair=pair)


def line_sums(keep, got, first, second, after=(), pair=()):
    line = keep.shape[1]
    half = line // 2

    def compute(ins, outs):
        for at in range(line):
            direct, merged = ins[2 + at // half], ins[4 + at // half]
            total = wide(ins[0][0, at]) + wide(ins[1][0, at]) + wide(direct[1, at % half])
            outs[at][...] = low(total + wide(merged[at % half]))

    operands = [keep, got, *first, *second]
    return prepare(compute, operands, [like(keep, *keep.shape[2:])] * line, after, pair=pair)


def chip_sum_halves(place, terms, copied=(), after=(), pair=()):
    rows, cols = terms[0].shape

    def compute(me, ins, outs):
        total = add(*[ref[...] for ref in ins[: len(terms)]])
        first = me % 2 == 0
        upper, lower = total[: rows // 2], total[rows // 2 :]
        outs[0][...] = jnp.where(first, upper, lower)
        outs[1][...] = jnp.where(first, lower, upper)
        for number in range(len(copied)):
            outs[2 + number][...] = ins[len(terms) + number][...]

    shape = jax.ShapeDtypeStruct((rows // 2, cols), jnp.float32)
    shapes = [shape, shape] + [like(array, *array.shape) for array in copied]
    operands = list(tuple(terms) + tuple(copied))
    return prepare(compute, operands, shapes, after, place, pair=pair)


def join_halves(place, mine, other, parts, factor, gain, weights, after=()):
    rows = mine.shape[0]
    skipped = len(parts) - len(weights)

    def compute(me, ins, outs):
        core = me % 2
        first = 0
        for count, out in zip(parts, outs):
            for ref, half in ((ins[0], core), (ins[1], 1 - core)):
                start = pl.multiple_of(half * count, 128)
                out[:, pl.ds(start, count)] = ref[:, first : first + count] * factor
            first += count
        total = jnp.zeros((rows, 1), jnp.float32)
        for number, weight in enumerate(ins[3:]):
            product = wide(weight[...]) * outs[skipped + number][...]
            total = total + jnp.sum(product, axis=1, keepdims=True)
        same = lax.broadcasted_iota(jnp.int32, (rows, rows), 0) == lax.broadcasted_iota(
            jnp.int32, (rows, rows), 1
        )
        column = jnp.sum(jnp.where(same, wide(ins[2][...]), 0.0), axis=1, keepdims=True)
        outs[len(parts)][...] = jnp.broadcast_to(total / column, (rows, 128))

    shapes = [jax.ShapeDtypeStruct((rows, 2 * count), jnp.float32) for count in parts]
    shapes.append(jax.ShapeDtypeStruct((rows, 128), jnp.float32))
    operands = list((mine, other, gain[None]) + tuple(weights))
    return prepare(compute, operands, shapes, after, place)[0]


def gather_plain(shards):
    full = [lax.all_gather(shard, "fsdp", axis=0, tiled=True) for shard in shards]
    gain_attn, w_query, w_key, w_value, w_attn_out, gain_ffn, w_ffn_in, w_ffn_out = full
    gains = jnp.pad(jnp.stack([gain_attn, gain_ffn], 1), ((0, 0), (0, 126)))
    return (
        (halves_of(w_query, w_key, w_value, jnp.concatenate([gains, gains], 1)),),
        (halves_of(w_attn_out, w_ffn_in),),
        (w_ffn_out,),
    )


def gain_back(gain, weights, grads):
    return sum(
        jnp.sum(weight.astype(jnp.float32) * grad, axis=1) for weight, grad in zip(weights, grads)
    ) / gain.astype(jnp.float32)


def per_device(
    tokens,
    lengths,
    gain_attn,
    w_query,
    w_key,
    w_value,
    w_attn_out,
    gain_ffn,
    w_ffn_in,
    w_ffn_out,
    bucket_bias_matrix,
    cotangent,
):
    slot_count, width = tokens.shape
    heads = bucket_bias_matrix.shape[1]
    devices = lax.axis_size("fsdp")
    factor = 1.0 / math.sqrt(slot_count * devices)
    place = lax.axis_index("fsdp").astype(jnp.int32)[None]
    side = width // 2
    by_chips = devices == 32
    pairs = heads // 2
    done, shared, attended, backs = [0], [], [], []

    def forward(count, after=()):
        out, prob, token = attend(
            lengths, query, key, value, planes, done[0], count, tuple(shared), after
        )
        done[0] += count
        attended.append(out)
        shared[:] = [prob]
        return token

    def backward(count, after=()):
        first = sum(some[0].shape[1] for some in backs) * heads // (2 * width)
        result = attend_back(
            query, key, value, grad_attended, prob, first, count, heads, after
        )
        backs.append(result[:4])
        return result[4]

    def weights(after=()):
        return weights_back(
            place,
            tokens,
            gains,
            [some[:3] for some in backs],
            [some[3] for some in backs],
            by_chips,
            after,
        )

    def inputs(first, count, done=None, after=()):
        return inputs_back(
            place,
            tokens,
            gains,
            grad_hidden,
            [some[:3] for some in backs],
            in_qkv,
            by_chips,
            first,
            count,
            done,
            after,
        )

    if by_chips:
        mine_qkv, for_qkv, mine_in, for_in = pack_halves(
            place,
            gain_attn[None],
            gain_ffn[None],
            (w_query, w_key, w_value),
            (w_attn_out, w_ffn_in),
        )
        unit, token = chip_unit(place, mine_qkv, swap(for_qkv, 1))
        line = gather_line(unit)
        planes, token = bias_planes(bucket_bias_matrix, (token,))

        (near_qkv, unit), token = stack_and_copies(line, (w_ffn_out,), (token,))
        plane_qkv = gather_plane(near_qkv)
        line = gather_line(unit)

        parts, token = far_and_copies(*plane_qkv, (near_qkv,) + plane_qkv, line + (token,))
        far_qkv = gather_far(*parts[:2])
        other_qkv = tuple(swap(part, 1) for part in parts[2:])

        (near_out, unit), token = stack_and_unit(
            place, line, mine_in, swap(for_in, 1), far_qkv + other_qkv + (token,)
        )
        plane_out = gather_plane(near_out)
        other_qkv = other_qkv + (swap(far_qkv[0], 1), swap(far_qkv[1], 1))
        in_qkv = (near_qkv,) + plane_qkv + far_qkv + other_qkv
        query, key, value, gains, token = project_qkv(
            place, tokens, in_qkv, by_chips, (planes, token)
        )

        parts, token = far_and_copies(*plane_out, (unit,), (token,))
        far_out = gather_far(*parts[:2])
        line = gather_line(parts[2])
        token = forward(2, (token,))

        parts, token = stack_and_copies(line, (near_out,) + plane_out, far_out + (token,))
        near_in = parts[0]
        plane_in = gather_plane(near_in)
        other_out = tuple(swap(part, 1) for part in parts[1:])
        token = forward(2, (token,))

        parts, token = far_and_copies(*plane_in, far_out + (near_in,), other_out + (token,))
        far_in = gather_far(*parts[:2])
        other_out = other_out + (swap(parts[2], 1), swap(parts[3], 1))
        other_in = (swap(parts[4], 1),)
        token = forward(1, (token,))

        parts, token = copied(plane_in + far_in, other_in + other_out[3:] + (token,))
        other_in = other_in + tuple(swap(part, 1) for part in parts)
        token = forward(1, (token,))

        in_ffn = (near_in,) + plane_in + far_in + other_in
        in_out = (near_out,) + plane_out + far_out + other_out
    else:
        planes, _ = bias_planes(bucket_bias_matrix)
        in_qkv, in_ffn, in_out = gather_plain(
            (gain_attn, w_query, w_key, w_value, w_attn_out, gain_ffn, w_ffn_in, w_ffn_out)
        )
        query, key, value, gains, _ = project_qkv(place, tokens, in_qkv, by_chips)
        for _ in range(pairs):
            forward(1)

    (prob,) = shared
    (output, grad_hidden, grad_attended), saved, part_out = feed_forward(
        place, tokens, attended, cotangent, gains, in_ffn, in_out, by_chips
    )

    if by_chips:
        keep_out, send_out = part_out
        got_out = swap(send_out, 1)
        (keep_in, send_in), token = in_weights_back(place, attended, *saved, by_chips)

        sends, token = first_sends(keep_out, got_out, (token,))
        first_out = scatter_first(sends)
        got_in = swap(send_in, 1)
        token = backward(2, (token,))

        sends, token = second_sends(keep_out, got_out, first_out, (got_in, token))
        second_out = scatter_second(sends)
        token = backward(1, (token,))

        sums, token = line_sums(keep_out, got_out, first_out, second_out, (token,))
        last_out = scatter_line(sums)
        sends, token = first_sends(keep_in, got_in, (token,))
        first_in = scatter_first(sends)
        token = backward(2, (token,))

        sends, token = second_sends(keep_in, got_in, first_in, last_out + (token,))
        second_in = scatter_second(sends)
        token = backward(1, (token,))

        sums, token = line_sums(keep_in, got_in, first_in, second_in, (token,))
        last_in = scatter_line(sums)
        (keep_qkv, send_qkv), table, token = weights(last_out + (token,))

        parts, token = chip_sum_halves(place, last_in, (send_qkv, table), (token,))
        mine_in, for_in, send_qkv, table = parts
        got_qkv, got_in, got = swap(send_qkv, 1), swap(for_in, 1), swap(table, 1)
        grad_tokens, token = inputs(0, slot_count // 2, None, (token,))

        parts, token = first_sends(keep_qkv, got_qkv, (got_in, token), (table, got))
        first_qkv = scatter_first(parts[:2])
        table, got = parts[2], swap(parts[2], 2)
        grad_tokens, token = inputs(slot_count // 2, slot_count // 2, grad_tokens, (token,))

        parts, token = second_sends(keep_qkv, got_qkv, first_qkv, (token,), (table, got))
        second_qkv = scatter_second(parts[:2])
        table, got = parts[2], swap(parts[2], 4)
        sum_out = add(*last_out) * factor

        parts, token = line_sums(
            keep_qkv, got_qkv, first_qkv, second_qkv, (token,), (table, got)
        )
        last_qkv = scatter_line(parts[:-1])
        table, got = parts[-1], swap(parts[-1], 8)
        sum_o, sum_in, grad_gain_ffn = join_halves(
            place,
            mine_in,
            got_in,
            (side, keep_in.shape[-1] - side),
            factor,
            gain_ffn,
            (w_ffn_in,),
            (token,),
        )

        parts, token = chip_sum_halves(place, last_qkv, (), (token,), (table, got))
        mine_qkv, for_qkv, table = parts
        got_qkv, got = swap(for_qkv, 1), swap(table, 16)
        table = table + got
        sum_q, sum_k, sum_v, grad_gain_attn = join_halves(
            place,
            mine_qkv,
            got_qkv,
            (side, side, side),
            factor,
            gain_attn,
            (w_query, w_key, w_value),
        )
        grad_gain_attn, grad_gain_ffn = grad_gain_attn[:, 0], grad_gain_ffn[:, 0]
        sums = (sum_q, sum_k, sum_v, sum_o, sum_in, sum_out)
    else:
        for _ in range(pairs):
            backward(1)
        part_in, _ = in_weights_back(place, attended, *saved, by_chips)
        part_qkv, table, _ = weights()
        grad_tokens, _ = inputs(0, slot_count)
        sums = sum_plain(
            jnp.concatenate([part_qkv[0], part_in[0][:, :, :side]], 2),
            part_in[0][:, :, side:],
            part_out[0],
        )
        sums = [total * factor for total in sums]
        table = lax.psum(table, "fsdp")
        grad_gain_attn = gain_back(gain_attn, (w_query, w_key, w_value), sums[:3])
        grad_gain_ffn = gain_back(gain_ffn, (w_ffn_in,), sums[4:5])

    return (
        output,
        grad_tokens,
        grad_gain_attn,
        sums[0],
        sums[1],
        sums[2],
        sums[3],
        grad_gain_ffn,
        sums[4],
        sums[5],
        table[:heads, :NB].T * factor,
    )


def solution(mesh):
    placed = (
        P("fsdp", None),
        P("fsdp", None),
        P("fsdp"),
        P("fsdp", None),
        P("fsdp", None),
        P("fsdp", None),
        P("fsdp", None),
        P("fsdp"),
        P("fsdp", None),
        P("fsdp", None),
        P(),
        P("fsdp", None),
    )
    return jax.shard_map(
        per_device,
        mesh=mesh,
        in_specs=placed,
        out_specs=(
            P("fsdp", None),
            P("fsdp", None),
            P("fsdp"),
            P("fsdp", None),
            P("fsdp", None),
            P("fsdp", None),
            P("fsdp", None),
            P("fsdp"),
            P("fsdp", None),
            P("fsdp", None),
            P(),
        ),
        check_vma=False,
    )
```

```python
import functools
import math

import jax
import jax.numpy as jnp
import numpy as np
from jax import lax
from jax.experimental import pallas as pl
from jax.experimental.pallas import tpu as pltpu
from jax.sharding import PartitionSpec as P

NB = 32
MAXD = 128
SEQ = 512
MIB = 1024 * 1024


def bucket_ids(span_length):
    offset = np.arange(span_length)[None, :] - np.arange(span_length)[:, None]
    half_count = NB // 2
    exact_count = half_count // 2
    result = np.where(offset > 0, half_count, 0)
    distance = np.abs(offset)
    spread = exact_count + np.floor(
        np.log(np.maximum(distance, 1) / exact_count)
        / math.log(MAXD / exact_count)
        * (half_count - exact_count)
    )
    spread = np.minimum(spread, half_count - 1)
    result = result + np.where(distance < exact_count, distance, spread)
    return result.astype(np.int32)


def flip(mask, count):
    return [(i, i ^ mask) for i in range(count)]


def swap(array, mask):
    return lax.ppermute(array, "fsdp", flip(mask, lax.axis_size("fsdp")))


def gather_line(unit):
    line = lax.axis_size("fsdp") // 8
    return (unit,) + tuple(swap(unit, 8 * hop) for hop in range(1, line))


def gather_plane(near):
    return swap(near, 2), swap(near, 4)


def gather_far(first, second):
    return swap(first, 2), swap(second, 4)


def chip_distances():
    line = lax.axis_size("fsdp") // 8
    half = line // 2
    blocks = []
    for part, (plane, first, last) in enumerate(
        ((0, 0, line), (1, 0, line), (2, 0, line), (3, 0, half), (3, half, line))
    ):
        blocks += [(part, hop - first, 4 * hop + plane) for hop in range(first, last)]
    return blocks


def add(*terms):
    return sum(term.astype(jnp.float32) for term in terms)


def scatter_first(sends):
    return swap(sends[0], 2), swap(sends[1], 4)


def scatter_second(sends):
    return swap(sends[0], 4), swap(sends[1], 2)


def scatter_line(sums):
    return (sums[0],) + tuple(swap(total, 8 * hop) for hop, total in enumerate(sums) if hop)


def halves_of(*arrays):
    return jnp.stack(
        [
            jnp.concatenate(
                [
                    array[:, part * array.shape[1] // 2 : (part + 1) * array.shape[1] // 2]
                    for array in arrays
                ],
                1,
            )
            for part in range(2)
        ]
    )


def sum_plain(half_attn, half_in, grad_out):
    side = half_attn.shape[-1] // 4

    def owned(array):
        return lax.psum_scatter(
            array.astype(jnp.float32), "fsdp", scatter_dimension=0, tiled=True
        )

    grads = [
        jnp.concatenate([part[0], part[1]], 1)
        for part in [half_attn[:, :, k * side : (k + 1) * side] for k in range(4)] + [half_in]
    ]
    return [owned(grad) for grad in grads + [grad_out]]


def nn(left, right):
    return lax.dot_general(
        left, right, (((1,), (0,)), ((), ())), preferred_element_type=jnp.float32
    )


def nt(left, right):
    return lax.dot_general(
        left, right, (((1,), (1,)), ((), ())), preferred_element_type=jnp.float32
    )


def tn(left, right):
    return lax.dot_general(
        left, right, (((0,), (0,)), ((), ())), preferred_element_type=jnp.float32
    )


def low(value):
    return value.astype(jnp.bfloat16)


def wide(value):
    return value.astype(jnp.float32)


def norm_scale(values):
    return lax.rsqrt(jnp.mean(values * values, axis=-1, keepdims=True) + 1e-06)


def rms_back(scaled, scale, gain, grad_normed):
    weighted = grad_normed * gain
    return scale * (weighted - scaled * jnp.mean(weighted * scaled, axis=-1, keepdims=True))


IN_HBM = pl.BlockSpec(memory_space=pl.ANY)
IN_SMEM = pl.BlockSpec(memory_space=pltpu.SMEM)
IN_VMEM = pl.BlockSpec(memory_space=pltpu.VMEM)
TOKEN_SHAPE = jax.ShapeDtypeStruct((1, 1), jnp.float32)
TOKEN = pl.BlockSpec((1, 1), lambda *_: (0, 0), memory_space=pltpu.SMEM)


def cost(flops, bytes_moved):
    return pl.CostEstimate(flops=flops, bytes_accessed=bytes_moved, transcendentals=0)


def plan(me, rows, by_chips, side, per_core):
    chip, core = me // 2, me % 2
    if not by_chips:
        return []
    count = 5
    found = []
    for part, index, distance in chip_distances():
        number = chip ^ distance
        if per_core:
            number = number * 2 + (core ^ side)
        found.append((side * count + part, index, pl.multiple_of(number * rows, 16)))
    return found


def column_copies(me, sources, target, sems, side, by_chips, columns):
    first, last = columns
    if not by_chips:
        half = (me % 2) ^ side
        return [
            pltpu.make_async_copy(sources[0].at[half, :, pl.ds(first, last - first)], target, sems.at[0])
        ]
    rows = sources[0].shape[1]
    return [
        pltpu.make_async_copy(
            sources[part].at[index, :, pl.ds(first, last - first)],
            target.at[pl.ds(start, rows), :],
            sems.at[number],
        )
        for number, (part, index, start) in enumerate(plan(me, rows, True, side, False))
    ]


def row_copies(me, sources, target, sems, side, by_chips):
    if not by_chips:
        half = target.shape[0] // 2
        where = pl.ds(side * half, half)
        return [pltpu.make_async_copy(sources[0].at[where, :], target.at[where, :], sems.at[0])]
    rows = sources[0].shape[1]
    return [
        pltpu.make_async_copy(
            sources[part].at[index], target.at[pl.ds(start, rows), :], sems.at[number]
        )
        for number, (part, index, start) in enumerate(plan(me, rows, True, side, True))
    ]


def start_all(copies):
    for copy in copies:
        copy.start()


def wait_all(copies):
    for copy in copies:
        copy.wait()


def half_copies(me, tile, targets, sems, side, by_chips, columns):
    first, count = columns
    if not by_chips:
        half = (me % 2) ^ side
        return [
            pltpu.make_async_copy(tile, targets[0].at[half, :, pl.ds(first, count)], sems.at[0])
        ]
    planes, line, rows = targets[side].shape[:3]
    chip = me // 2
    return [
        pltpu.make_async_copy(
            tile.at[pl.ds(pl.multiple_of((chip ^ (4 * hop + plane)) * rows, 16), rows), :],
            targets[side].at[plane, hop, :, pl.ds(first, count)],
            sems.at[plane * line + hop],
        )
        for plane in range(planes)
        for hop in range(line)
    ]


def strip_copies(me, tile, targets, sems, strip, by_chips):
    if not by_chips:
        rows = tile.shape[0]
        return [
            pltpu.make_async_copy(
                tile, targets[0].at[pl.ds(pl.multiple_of(strip * rows, 16), rows), :], sems.at[0]
            )
        ]
    planes, line, rows = targets[0].shape[:3]
    chip, core = me // 2, me % 2
    return [
        pltpu.make_async_copy(
            tile.at[
                pl.ds(pl.multiple_of((((chip % 4) ^ plane) * 2 + (core ^ side)) * rows, 16), rows), :
            ],
            targets[side].at[plane, (chip // 4) ^ strip],
            sems.at[side * planes + plane],
        )
        for side in range(2)
        for plane in range(planes)
    ]


def bias_planes(table, after=()):
    heads = table.shape[1]
    ids = bucket_ids(SEQ)
    flat = np.concatenate([ids[:, 0], ids[0, :1], ids[0, :0:-1]])
    onehot = (np.arange(table.shape[0])[:, None] == flat[None, :]).astype(np.float32)

    def kernel(table_ref, onehot_ref, *refs):
        plane_ref, token_ref, rows = refs[len(after) :]
        token_ref[0, 0] = 0.0
        head = pl.program_id(0)

        @pl.when(head == 0)
        def _():
            rows[:heads] = lax.dot_general(
                wide(table_ref[...]),
                onehot_ref[...],
                (((0,), (0,)), ((), ())),
                precision=lax.Precision.HIGHEST,
                preferred_element_type=jnp.float32,
            )

        spread = jnp.broadcast_to(rows[pl.ds(head, 1), :], (SEQ, 2 * SEQ))
        moved = pltpu.roll(spread, 0, 1, stride=1, stride_axis=0)
        plane_ref[0] = low(moved[:, :SEQ])

    return pl.pallas_call(
        kernel,
        grid=(heads,),
        out_shape=[jax.ShapeDtypeStruct((heads, SEQ, SEQ), jnp.bfloat16), TOKEN_SHAPE],
        in_specs=[IN_VMEM, IN_VMEM] + [IN_HBM] * len(after),
        out_specs=[pl.BlockSpec((1, SEQ, SEQ), lambda head: (head, 0, 0)), TOKEN],
        scratch_shapes=[pltpu.VMEM((-(-heads // 8) * 8, 2 * SEQ), jnp.float32)],
        compiler_params=pltpu.CompilerParams(vmem_limit_bytes=16 * MIB),
    )(table, jnp.asarray(onehot), *after)


def line_ids():
    ids = bucket_ids(SEQ)
    ahead = (np.arange(2 * SEQ) - (SEQ - 128) + SEQ) % (2 * SEQ) - SEQ
    return np.where(ahead >= 0, ids[np.maximum(ahead, 0), 0], ids[0, np.minimum(-ahead, SEQ - 1)])


def project_qkv(place, tokens, sources, by_chips, after=()):
    slots, width = tokens.shape
    side_cols = width // 2
    packed = sources[0].shape[-1]
    block = 256

    def kernel(place_ref, x_ref, *refs):
        ins, refs = refs[: len(sources)], refs[len(sources) + len(after) :]
        out_ref, normed_hbm, weights_hbm, gains_ref, token_ref, normed_ref, weights, sems = refs
        token_ref[0, 0] = 0.0
        me = place_ref[0]
        core = me % 2

        def put(side):
            if not by_chips:
                weights[side] = ins[0][(me % 2) ^ side]
                return
            rows = ins[0].shape[1]
            for part, index, start in plan(me, rows, True, side, False):
                weights[side, pl.ds(start, rows), :] = ins[part][index]

        put(0)
        gains = jnp.transpose(wide(weights[0, :, 3 * side_cols :]))
        gains_ref[...] = gains[:8]

        def normalise(index, carry):
            where = pl.ds(pl.multiple_of(index * block, block), block)
            rows = wide(x_ref[where, :])
            normed_ref[where, :] = low(rows * norm_scale(rows) * gains_ref[0:1, :])
            return carry

        lax.fori_loop(0, slots // block, normalise, 0)
        put(1)
        stores = [
            pltpu.make_async_copy(normed_ref, normed_hbm, sems.at[0]),
            pltpu.make_async_copy(weights, weights_hbm, sems.at[1]),
        ]
        start_all(stores)

        def one(index, carry):
            side, part = index // 3, index % 3
            here = pl.ds(pl.multiple_of(part * side_cols, 128), side_cols)
            cols = pl.ds(pl.multiple_of((core ^ side) * side_cols, 128), side_cols)
            out_ref[part, :, cols] = low(nn(normed_ref[...], weights[side, :, here]))
            return carry

        lax.fori_loop(0, 6, one, 0)
        wait_all(stores)

    sums = jax.ShapeDtypeStruct
    return pl.pallas_call(
        kernel,
        out_shape=[
            sums((3, slots, width), jnp.bfloat16),
            sums((slots, width), jnp.bfloat16),
            sums((2, width, packed), jnp.bfloat16),
            sums((8, width), jnp.float32),
            TOKEN_SHAPE,
        ],
        in_specs=[IN_SMEM] + [IN_VMEM] * (1 + len(sources)) + [IN_HBM] * len(after),
        out_specs=[IN_VMEM, IN_HBM, IN_HBM, IN_VMEM, IN_SMEM],
        scratch_shapes=[
            pltpu.VMEM((slots, width), jnp.bfloat16),
            pltpu.VMEM((2, width, packed), jnp.bfloat16),
            pltpu.SemaphoreType.DMA((2,)),
        ],
        compiler_params=pltpu.CompilerParams(vmem_limit_bytes=24 * MIB),
        cost_estimate=cost(6 * slots * width * width, 12 * slots * width),
    )(place, tokens, *sources, *after)


def attend(lengths, qkv, planes, first, count, shared=(), after=()):
    _, slots, width = qkv.shape
    seqs = slots // SEQ
    heads = planes.shape[0]
    pair_cols = 2 * width // heads
    head_size = pair_cols // 2

    def kernel(lengths_ref, qkv_ref, planes_ref, *refs):
        q, k, v = (qkv_ref.at[part] for part in range(3))
        out, prob, token_ref, scores = refs[len(shared) + len(after) :]
        token_ref[0, 0] = 0.0

        own_lane = lax.broadcasted_iota(jnp.int32, (1, pair_cols), 1) < head_size
        key_number = lax.broadcasted_iota(jnp.int32, (SEQ, 1), 0)
        zero = jnp.zeros((), jnp.bfloat16)

        def both_heads(rows):
            return jnp.concatenate(
                [jnp.where(own_lane, rows, zero), jnp.where(own_lane, zero, rows)], 0
            )

        def one(step, carry):
            pair, seq = step // seqs, step % seqs
            rows = pl.ds(pl.multiple_of(seq * SEQ, SEQ), SEQ)
            own = pl.ds(pl.multiple_of(pair * pair_cols, pair_cols), pair_cols)
            lanes = pl.ds(pl.multiple_of((first + pair) * pair_cols, pair_cols), pair_cols)

            permitted = key_number < lengths_ref[seq, 0] + lengths_ref[seq, 1]
            scores[...] = nt(both_heads(k[rows, lanes]), q[rows, lanes])
            for head in range(2):
                these = scores[head * SEQ : (head + 1) * SEQ, :] + wide(planes_ref[2 * (first + pair) + head])
                these = jnp.where(permitted, these, -1e30)
                raised = jnp.exp(these - jnp.max(these, axis=0, keepdims=True))
                total = jnp.sum(raised, axis=0, keepdims=True)
                prob[seq, 2 * (first + pair) + head] = low(raised * (1.0 / total))
            both = prob[seq, pl.ds(2 * (first + pair), 2)].reshape(2 * SEQ, SEQ)
            mixed = tn(both, both_heads(v[rows, lanes]))
            out[rows, own] = low(mixed)
            return carry

        lax.fori_loop(0, count * seqs, one, 0)

    return pl.pallas_call(
        kernel,
        out_shape=[
            jax.ShapeDtypeStruct((slots, count * pair_cols), jnp.bfloat16),
            jax.ShapeDtypeStruct((seqs, heads, SEQ, SEQ), jnp.bfloat16),
            TOKEN_SHAPE,
        ],
        in_specs=[IN_SMEM] + [IN_VMEM] * (2 + len(shared)) + [IN_HBM] * len(after),
        out_specs=[IN_VMEM, IN_VMEM, IN_SMEM],
        scratch_shapes=[
            pltpu.VMEM((2 * SEQ, SEQ), jnp.float32),
        ],
        compiler_params=pltpu.CompilerParams(vmem_limit_bytes=12 * MIB),
        cost_estimate=cost(count * slots * SEQ * 2048, count * slots * SEQ * 8),
        input_output_aliases={3: 1} if shared else {},
    )(lengths, qkv, planes, *shared, *after)


def attend_back(qkv, grad_mixed, prob, first, count, heads, after=()):
    _, slots, width = qkv.shape
    seqs = slots // SEQ
    pair_cols = 2 * width // heads
    head_size = pair_cols // 2
    steps = count * seqs

    def kernel(qkv_ref, g, prob_ref, *refs):
        q, k, v = (qkv_ref.at[part] for part in range(3))
        dq, dk, dv, table_ref, token_ref, grads, scored, planes = refs[len(after) :]
        token_ref[0, 0] = 0.0

        own_lane = lax.broadcasted_iota(jnp.int32, (1, pair_cols), 1) < head_size
        zero = jnp.zeros((), jnp.bfloat16)

        def both_heads(rows):
            return jnp.concatenate(
                [jnp.where(own_lane, rows, zero), jnp.where(own_lane, zero, rows)], 0
            )

        def one(step, carry):
            pair, seq = step // seqs, step % seqs
            prob = prob_ref.at[seq, pl.ds(2 * (first + pair), 2)]
            rows = pl.ds(pl.multiple_of(seq * SEQ, SEQ), SEQ)
            own = pl.ds(pl.multiple_of(pair * pair_cols, pair_cols), pair_cols)
            lanes = pl.ds(pl.multiple_of((first + pair) * pair_cols, pair_cols), pair_cols)

            grads[...] = nt(both_heads(v[rows, lanes]), g[rows, lanes])
            summed = nn(prob[...].reshape(2 * SEQ, SEQ), g[rows, lanes])
            dv[rows, own] = low(jnp.where(own_lane, summed[:SEQ], summed[SEQ:]))
            keep = jnp.where(seq == 0, 0.0, 1.0)
            for head in range(2):
                there = slice(head * SEQ, (head + 1) * SEQ)
                weights = wide(prob[head])
                weighted = weights * grads[there, :]
                dot = jnp.sum(weighted, axis=0, keepdims=True)
                grad_scores = weighted - weights * dot
                planes[head] = planes[head] * keep + grad_scores
                scored[there, :] = low(grad_scores)
            summed = nn(scored[...], q[rows, lanes])
            dk[rows, own] = low(jnp.where(own_lane, summed[:SEQ], summed[SEQ:]))
            dq[rows, own] = low(tn(scored[...], both_heads(k[rows, lanes])))

            @pl.when(seq == seqs - 1)
            def _():
                for head in range(2):
                    lined = jnp.zeros((8, 2 * SEQ), jnp.float32)
                    for low_row in range(0, 128, 8):
                        frame = jnp.zeros((8, 2 * SEQ), jnp.float32)
                        for high_row in range(0, SEQ, 128):
                            some = planes[head, high_row + low_row : high_row + low_row + 8, :]
                            ahead = SEQ - 128 - high_row
                            filled = [some, jnp.zeros((8, SEQ - ahead), jnp.float32)]
                            if ahead:
                                filled = [jnp.zeros((8, ahead), jnp.float32)] + filled
                            frame = frame + jnp.concatenate(filled, 1)
                        if low_row:
                            frame = pltpu.roll(frame, 2 * SEQ - low_row, 1)
                        lined = lined + frame
                    moved = lined[:1]
                    for row in range(1, 8):
                        moved = moved + pltpu.roll(lined[row : row + 1], 2 * SEQ - row, 1)
                    table_ref[pair, head : head + 1, :] = moved

            return carry

        planes[...] = jnp.zeros_like(planes)
        lax.fori_loop(0, steps, one, 0)

    result = jax.ShapeDtypeStruct((slots, count * pair_cols), jnp.bfloat16)
    return pl.pallas_call(
        kernel,
        in_specs=[IN_VMEM] * 3 + [IN_HBM] * len(after),
        out_specs=[IN_VMEM] * 4 + [IN_SMEM],
        out_shape=[result] * 3
        + [jax.ShapeDtypeStruct((count, 8, 2 * SEQ), jnp.float32), TOKEN_SHAPE],
        scratch_shapes=[
            pltpu.VMEM((2 * SEQ, SEQ), jnp.float32),
            pltpu.VMEM((2 * SEQ, SEQ), jnp.bfloat16),
            pltpu.VMEM((2, SEQ, SEQ), jnp.float32),
        ],
        compiler_params=pltpu.CompilerParams(vmem_limit_bytes=16 * MIB),
        cost_estimate=cost(count * slots * SEQ * 4096, count * slots * SEQ * 8),
    )(qkv, grad_mixed, prob, *after)


def feed_forward(place, tokens, attended, cotangent, gains, in_sources, out_sources, by_chips):
    slots, width = tokens.shape
    side_cols = width // 2
    hidden_cols = 2 * (in_sources[0].shape[-1] - side_cols)
    block = 256
    blocks = slots // block
    chunk = 768
    per_side = hidden_cols // 2 // chunk
    count_att = len(attended)
    root, bend = math.sqrt(2.0 / math.pi), 0.044715

    def kernel(place_ref, x_hbm, cot_hbm, gains_ref, *refs):
        refs = list(refs)

        def take(number):
            taken, refs[:] = refs[:number], refs[number:]
            return taken

        att_hbm, in_hbm, out_hbm = take(count_att), take(len(in_sources)), take(len(out_sources))
        y_hbm, back_hbm, branch_hbm, flipped_hbm, pre_hbm = take(5)
        out_targets = take(2 if by_chips else 1)
        x, att, cot, w_o, w_in, w_out, hidden, normed, flipped = take(9)
        sum_g, act, grad_pre, tile_out = take(4)
        load_sems, o_sems, in_sems, out_sems, store_sems, pre_sems, tile_out_sems = take(7)
        me = place_ref[0]
        core = me % 2
        gain = gains_ref[1:2, :]

        def rows_of(index):
            return pl.ds(pl.multiple_of(index * block, block), block)

        loads = [
            pltpu.make_async_copy(x_hbm, x, load_sems.at[0]),
            pltpu.make_async_copy(cot_hbm, cot, load_sems.at[1]),
        ]
        cols = 0
        for number, source in enumerate(att_hbm):
            loads.append(
                pltpu.make_async_copy(
                    source, att.at[:, pl.ds(cols, source.shape[1])], load_sems.at[2 + number]
                )
            )
            cols += source.shape[1]
        o_loads, in_loads, out_loads = [], [], []
        for side in range(2):
            o_cols = pl.ds(pl.multiple_of((core ^ side) * side_cols, 128), side_cols)
            o_loads += column_copies(
                me, in_hbm, w_o.at[:, o_cols], o_sems.at[side], side, by_chips, (0, side_cols)
            )
            in_loads.append(
                column_copies(
                    me,
                    in_hbm,
                    w_in.at[side],
                    in_sems.at[side],
                    side,
                    by_chips,
                    (side_cols, in_sources[0].shape[-1]),
                )
            )
            out_loads += row_copies(me, out_hbm, w_out, out_sems.at[side], side, by_chips)
        start_all(loads[2:])
        start_all(o_loads)
        start_all(loads[:2])
        start_all(in_loads[0])
        start_all(out_loads)
        wait_all(loads)
        wait_all(o_loads)
        start_all(in_loads[1])

        count = width // block

        def cols_of(index):
            return pl.ds(pl.multiple_of(index * block, block), block)

        def residual(index, carry):
            cols = cols_of(index)
            hidden[:, cols] = wide(x[:, cols]) + nn(att[...], w_o[:, cols])
            return carry

        lax.fori_loop(0, count, residual, 0)

        def before(index, carry):
            where = rows_of(index)
            value = hidden[where, :]
            rows = value * norm_scale(value) * gain
            normed[where, :] = low(rows)
            flipped[:, where] = low(jnp.transpose(rows))
            return carry

        lax.fori_loop(0, blocks, before, 0)
        flip_store = pltpu.make_async_copy(flipped, flipped_hbm, store_sems.at[3])
        flip_store.start()
        wait_all(in_loads[0])
        wait_all(out_loads)

        per_chunk = chunk // block
        chunks = 2 * per_side

        def tile_stores(number):
            strip = (core ^ (number // per_side)) * per_side + number % per_side
            slot = number % 2
            return strip_copies(
                me, tile_out.at[slot], out_targets, tile_out_sems.at[slot], strip, by_chips
            )

        def pre_store(number):
            side, part = number // per_side, number % per_side
            strip = (core ^ side) * per_side + part
            units = pl.ds(pl.multiple_of(part * chunk, chunk), chunk)
            return pltpu.make_async_copy(
                grad_pre.at[side, :, units], pre_hbm.at[strip], pre_sems.at[number]
            )

        def through(index, carry):
            number, inside = index // per_chunk, index % per_chunk
            side, part = number // per_side, number % per_side
            first = part * chunk + inside * block
            unit_cols = pl.ds(pl.multiple_of(first, block), block)
            unit_row = (core ^ side) * (per_side * chunk) + first
            unit_rows = pl.ds(pl.multiple_of(unit_row, block), block)

            @pl.when(index == per_side * per_chunk)
            def _():
                wait_all(in_loads[1])

            @pl.when((inside == 0) & (number >= 2))
            def _():
                wait_all(tile_stores(number - 2))

            pre = nn(normed[...], w_in[side, :, unit_cols])
            square = pre * pre
            slope = jnp.tanh(pre * (root + (root * bend) * square))
            opened = 0.5 + 0.5 * slope
            gate = opened + pre * (1.0 - slope * slope) * (
                0.5 * root + (1.5 * bend * root) * square
            )
            acted = low(pre * opened)
            act[side, :, unit_cols] = acted
            grad_pre[side, :, unit_cols] = low(nt(cot[...], w_out[unit_rows, :]) * gate)
            tile_out[number % 2, cols_of(inside), :] = low(tn(acted, cot[...]))

            @pl.when(inside == per_chunk - 1)
            def _():
                start_all(tile_stores(number))
                pre_store(number).start()

            return carry

        lax.fori_loop(0, chunks * per_chunk, through, 0)

        half = hidden_cols // 2
        halves = [pl.ds(pl.multiple_of((core ^ side) * half, block), half) for side in range(2)]

        def sums_of(index, carry):
            cols = cols_of(index)
            value = nn(act[0], w_out[halves[0], cols]) + nn(act[1], w_out[halves[1], cols])
            x[:, cols] = low(hidden[:, cols] + value)
            sum_g[:, cols] = nt(grad_pre[0], w_in[0, cols, :]) + nt(grad_pre[1], w_in[1, cols, :])
            return carry

        lax.fori_loop(0, count, sums_of, 0)

        def after(index, carry):
            where = rows_of(index)
            value = hidden[where, :]
            scale = norm_scale(value)
            back = rms_back(value * scale, scale, gain, sum_g[where, :])
            normed[where, :] = low(wide(cot[where, :]) + back)
            return carry

        y_store = pltpu.make_async_copy(x, y_hbm, store_sems.at[0])
        y_store.start()
        lax.fori_loop(0, blocks, after, 0)
        branch_store = pltpu.make_async_copy(normed, branch_hbm, store_sems.at[1])
        branch_store.start()

        def mixed_back(index, carry):
            cols = cols_of(index)
            att[:, cols] = low(nt(normed[...], w_o[cols, :]))
            return carry

        lax.fori_loop(0, count, mixed_back, 0)
        last = [pltpu.make_async_copy(att, back_hbm, store_sems.at[2])]
        last[0].start()
        last += [flip_store, y_store, branch_store]
        for number in range(chunks):
            last.append(pre_store(number))
            if number >= chunks - 2:
                last += tile_stores(number)
        wait_all(last)

    sums = jax.ShapeDtypeStruct
    flat = sums((slots, width), jnp.bfloat16)
    devices = lax.axis_size("fsdp")
    if by_chips:
        line = devices // 8
        out_shapes = [sums((4, line, hidden_cols // devices, width), jnp.bfloat16)] * 2
    else:
        out_shapes = [sums((hidden_cols, width), jnp.bfloat16)]
    outs = [
        flat,
        flat,
        flat,
        sums((width, slots), jnp.bfloat16),
        sums((hidden_cols // chunk, slots, chunk), jnp.bfloat16),
    ] + out_shapes
    bf16, f32 = jnp.bfloat16, jnp.float32
    result = pl.pallas_call(
        kernel,
        out_shape=outs,
        in_specs=[IN_SMEM, IN_HBM, IN_HBM, IN_VMEM]
        + [IN_HBM] * (count_att + len(in_sources) + len(out_sources)),
        out_specs=[IN_HBM] * len(outs),
        scratch_shapes=[
            pltpu.VMEM((slots, width), bf16),
            pltpu.VMEM((slots, width), bf16),
            pltpu.VMEM((slots, width), bf16),
            pltpu.VMEM((width, width), bf16),
            pltpu.VMEM((2, width, hidden_cols // 2), bf16),
            pltpu.VMEM((hidden_cols, width), bf16),
            pltpu.VMEM((slots, width), f32),
            pltpu.VMEM((slots, width), bf16),
            pltpu.VMEM((width, slots), bf16),
            pltpu.VMEM((slots, width), f32),
            pltpu.VMEM((2, slots, hidden_cols // 2), bf16),
            pltpu.VMEM((2, slots, hidden_cols // 2), bf16),
            pltpu.VMEM((2, chunk, width), bf16),
            pltpu.SemaphoreType.DMA((2 + count_att,)),
            pltpu.SemaphoreType.DMA((2, 16)),
            pltpu.SemaphoreType.DMA((2, 16)),
            pltpu.SemaphoreType.DMA((2, 16)),
            pltpu.SemaphoreType.DMA((4,)),
            pltpu.SemaphoreType.DMA((2 * per_side,)),
            pltpu.SemaphoreType.DMA((2, 8)),
        ],
        compiler_params=pltpu.CompilerParams(vmem_limit_bytes=56 * MIB),
        cost_estimate=cost(
            slots * width * (12 * hidden_cols + 6 * width), 60 * MIB
        ),
    )(place, tokens, cotangent, gains, *attended, *in_sources, *out_sources)
    output, back, *rest = result
    return output, back, tuple(rest[:3]), tuple(rest[3:])


def in_weights_back(place, attended, branch, flipped, grad_pre, by_chips):
    slots, width = branch.shape
    strips, _, chunk = grad_pre.shape
    side_cols = width // 2
    per_side = strips // 2
    packed = side_cols + per_side * chunk
    count_att = len(attended)

    def kernel(place_ref, branch_hbm, flipped_hbm, pre_hbm, *refs):
        att_hbm, refs = refs[:count_att], refs[count_att:]
        targets, refs = refs[:-9], refs[-9:]
        token_ref, att, branch, flipped, pre, tile, load_sems, tile_sems, o_sems = refs
        token_ref[0, 0] = 0.0
        me = place_ref[0]
        core = me % 2

        def place_of(number):
            return 1 - number // per_side, number % per_side

        def pre_load(number):
            side, part = place_of(number)
            return pltpu.make_async_copy(
                pre_hbm.at[(core ^ side) * per_side + part], pre.at[number], load_sems.at[number]
            )

        pre_loads = [pre_load(number) for number in range(strips)]
        flip_load = pltpu.make_async_copy(flipped_hbm, flipped, load_sems.at[strips])
        loads = [pltpu.make_async_copy(branch_hbm, branch, load_sems.at[strips + 1])]
        cols = 0
        for number, source in enumerate(att_hbm):
            loads.append(
                pltpu.make_async_copy(
                    source,
                    att.at[:, pl.ds(cols, source.shape[1])],
                    load_sems.at[strips + 2 + number],
                )
            )
            cols += source.shape[1]
        flip_load.start()
        start_all(pre_loads)
        start_all(loads)
        flip_load.wait()
        block = 256
        per_chunk = chunk // block

        def stores(number, side, part):
            return half_copies(
                me,
                tile.at[number % 2],
                targets,
                tile_sems.at[number % 2],
                side,
                by_chips,
                (pl.multiple_of(side_cols + part * chunk, 128), chunk),
            )

        for half in range(2):
            side = 1 - half

            def one(index, carry):
                part, inside = index // per_chunk, index % per_chunk
                number = half * per_side + part

                @pl.when(inside == 0)
                def _():
                    pre_load(number).wait()

                if half:

                    @pl.when(inside == 0)
                    def _():
                        wait_all(stores(part, 1, part))

                cols = pl.ds(pl.multiple_of(inside * block, block), block)
                tile[part % 2, :, cols] = low(nn(flipped[...], pre[number, :, cols]))

                @pl.when(inside == per_chunk - 1)
                def _():
                    start_all(stores(part, side, part))

                return carry

            lax.fori_loop(0, per_side * per_chunk, one, 0)
        wait_all(loads)
        wait_all(stores(0, 0, 0))

        def last(index, carry):
            some = pl.ds(pl.multiple_of(index * block, block), block)
            tile[0, some, :] = low(tn(att[:, some], branch[...]))
            return carry

        lax.fori_loop(0, width // block, last, 0)
        copies = []
        for side in range(2):
            o_cols = pl.ds(pl.multiple_of((core ^ side) * side_cols, 128), side_cols)
            copies += half_copies(
                me,
                tile.at[0, :, o_cols],
                targets,
                o_sems.at[side],
                side,
                by_chips,
                (0, side_cols),
            )
        start_all(copies)
        wait_all(stores(1, 0, 1))
        wait_all(copies)

    sums = jax.ShapeDtypeStruct
    bf16 = jnp.bfloat16
    if by_chips:
        line = lax.axis_size("fsdp") // 8
        shapes = [sums((4, line, width // (4 * line), packed), bf16)] * 2
    else:
        shapes = [sums((2, width, packed), bf16)]
    result = pl.pallas_call(
        kernel,
        out_shape=shapes + [TOKEN_SHAPE],
        in_specs=[IN_SMEM, IN_HBM, IN_HBM, IN_HBM] + [IN_HBM] * count_att,
        out_specs=[IN_HBM] * len(shapes) + [IN_SMEM],
        scratch_shapes=[
            pltpu.VMEM((slots, width), bf16),
            pltpu.VMEM((slots, width), bf16),
            pltpu.VMEM((width, slots), bf16),
            pltpu.VMEM((strips, slots, chunk), bf16),
            pltpu.VMEM((2, width, chunk), bf16),
            pltpu.SemaphoreType.DMA((strips + 2 + count_att,)),
            pltpu.SemaphoreType.DMA((2, 16)),
            pltpu.SemaphoreType.DMA((2, 16)),
        ],
        compiler_params=pltpu.CompilerParams(vmem_limit_bytes=56 * MIB),
        cost_estimate=cost(2 * slots * width * (width + strips * chunk), 20 * MIB),
    )(place, branch, flipped, grad_pre, *attended)
    return result[:-1], result[-1]


def back_places(grads, side_cols):
    places, first = [], 0
    for number, some in enumerate(grads):
        for col in range(0, some[0].shape[1], 128):
            half, start = divmod(first + col, side_cols)
            places += [
                (3 * number + part, col, half, part * side_cols + start) for part in range(3)
            ]
        first += some[0].shape[1]
    return [grad for some in grads for grad in some], places


def put_columns(refs, places, parts, rows):
    for number, col, half, start in places:
        parts[half, :, start : start + 128] = refs[number][rows, col : col + 128]


def weights_back(place, normed_attn, grads, diagonals, by_chips, after=()):
    slots, width = normed_attn.shape
    side_cols = width // 2
    flat_grads, places = back_places(grads, side_cols)

    onehot = np.pad(
        (line_ids()[:, None] == np.arange(NB)[None, :]).astype(np.float32), ((0, 0), (0, 128 - NB))
    )
    pairs = len(diagonals)
    heads = sum(2 * some.shape[0] for some in diagonals)
    table_rows = -(-heads // 8) * 8

    def kernel(place_ref, normed_ref, onehot_ref, *refs):
        diag_refs, refs = refs[:pairs], refs[pairs:]
        g_refs = refs[: len(flat_grads)]
        refs = refs[len(flat_grads) + len(after) :]
        targets, (table_ref, token_ref, parts, tile) = refs[:-4], refs[-4:]
        token_ref[0, 0] = 0.0
        me = place_ref[0]
        core = me % 2
        put_columns(g_refs, places, parts, slice(None))
        rows = [
            ref[one, head : head + 1, :]
            for ref in diag_refs
            for one in range(ref.shape[0])
            for head in range(2)
        ]
        if table_rows > heads:
            rows.append(jnp.zeros((table_rows - heads, 2 * SEQ), jnp.float32))
        table_ref[...] = lax.dot_general(
            jnp.concatenate(rows, 0),
            onehot_ref[...],
            (((1,), (0,)), ((), ())),
            precision=lax.Precision.HIGHEST,
            preferred_element_type=jnp.float32,
        )
        for side in range(2):
            half = core ^ side
            for first in range(0, 3 * side_cols, 512):
                some = slice(first, min(first + 512, 3 * side_cols))
                tile[:, some] = low(tn(normed_ref[...], parts[half, :, some]))
            if not by_chips:
                targets[0][half] = tile[...]
                continue
            planes, line, rows = targets[side].shape[:3]
            for plane in range(planes):
                for hop in range(line):
                    start = pl.multiple_of(((me // 2) ^ (4 * hop + plane)) * rows, 16)
                    targets[side][plane, hop] = tile[pl.ds(start, rows), :]

    sums = jax.ShapeDtypeStruct
    if by_chips:
        line = lax.axis_size("fsdp") // 8
        shapes = [sums((4, line, width // (4 * line), 3 * side_cols), jnp.bfloat16)] * 2
    else:
        shapes = [sums((2, width, 3 * side_cols), jnp.bfloat16)]
    result = pl.pallas_call(
        kernel,
        out_shape=shapes + [sums((table_rows, 128), jnp.float32), TOKEN_SHAPE],
        in_specs=[IN_SMEM] + [IN_VMEM] * (2 + pairs + len(flat_grads)) + [IN_HBM] * len(after),
        out_specs=[IN_VMEM] * (len(shapes) + 1) + [IN_SMEM],
        scratch_shapes=[
            pltpu.VMEM((2, slots, 3 * side_cols), jnp.bfloat16),
            pltpu.VMEM((width, 3 * side_cols), jnp.bfloat16),
        ],
        compiler_params=pltpu.CompilerParams(vmem_limit_bytes=24 * MIB),
        cost_estimate=cost(6 * slots * width * width, 15 * MIB),
    )(place, normed_attn, jnp.asarray(onehot), *diagonals, *flat_grads, *after)
    return result[:-2], result[-2], result[-1]


def inputs_back(
    tokens, gains, branch, grads, weights, place, first, count, done=None, after=()
):
    slots, width = tokens.shape
    side_cols = width // 2
    flat_grads, places = back_places(grads, side_cols)
    block = 256
    held = () if done is None else (done,)

    def kernel(place_ref, x_ref, gains_ref, branch_ref, weights_ref, *refs):
        g_refs, refs = refs[: len(flat_grads)], refs[len(flat_grads) + len(after) + len(held) :]
        out_hbm, token_ref, parts, out, summed, out_sems = refs
        token_ref[0, 0] = 0.0
        core = place_ref[0] % 2
        gain = gains_ref[0:1, :]
        put_columns(g_refs, places, parts, slice(first, first + count))

        def back(index, carry):
            cols = pl.ds(pl.multiple_of(index * block, block), block)
            summed[:, cols] = nt(parts[core], weights_ref[0, cols, : 3 * side_cols]) + nt(
                parts[1 - core], weights_ref[1, cols, : 3 * side_cols]
            )
            return carry

        lax.fori_loop(0, width // block, back, 0)

        def finish(index, carry):
            here = pl.ds(pl.multiple_of(index * block, block), block)
            where = pl.ds(pl.multiple_of(first + index * block, block), block)
            rows = wide(x_ref[where, :])
            scale = norm_scale(rows)
            back = rms_back(rows * scale, scale, gain, summed[here, :])
            out[here, :] = low(wide(branch_ref[where, :]) + back)
            return carry

        lax.fori_loop(0, count // block, finish, 0)
        last = pltpu.make_async_copy(out, out_hbm.at[pl.ds(first, count)], out_sems.at[0])
        last.start()
        last.wait()

    bf16, f32 = jnp.bfloat16, jnp.float32
    return pl.pallas_call(
        kernel,
        out_shape=[jax.ShapeDtypeStruct((slots, width), bf16), TOKEN_SHAPE],
        in_specs=[IN_SMEM]
        + [IN_VMEM] * (4 + len(flat_grads))
        + [IN_HBM] * (len(after) + len(held)),
        out_specs=[IN_HBM, IN_SMEM],
        scratch_shapes=[
            pltpu.VMEM((2, count, 3 * side_cols), bf16),
            pltpu.VMEM((count, width), bf16),
            pltpu.VMEM((count, width), f32),
            pltpu.SemaphoreType.DMA((1,)),
        ],
        compiler_params=pltpu.CompilerParams(vmem_limit_bytes=20 * MIB),
        cost_estimate=cost(6 * count * width * width, 15 * MIB),
        input_output_aliases={5 + len(flat_grads) + len(after): 0} if held else {},
    )(place, tokens, gains, branch, weights, *flat_grads, *after, *held)


def pack_halves(place, gain_attn, gain_ffn, shards_qkv, shards_in):
    rows = shards_qkv[0].shape[0]
    groups = (shards_qkv, shards_in)
    counts = [sum(shard.shape[1] for shard in group) // 2 for group in groups]

    def kernel(place_ref, attn_ref, ffn_ref, *refs):
        ins, outs = refs[: -2 * len(groups)], refs[-2 * len(groups) :]
        core = place_ref[0] % 2
        first = 0
        for number, group in enumerate(groups):
            for other in range(2):
                out, col = outs[2 * number + other], 0
                for ref in ins[first : first + len(group)]:
                    half = ref.shape[1] // 2
                    start = pl.multiple_of((core ^ other) * half, 128)
                    out[:, col : col + half] = ref[:, pl.ds(start, half)]
                    col += half
            first += len(group)
        same = lax.broadcasted_iota(jnp.int32, (rows, rows), 0) == lax.broadcasted_iota(
            jnp.int32, (rows, rows), 1
        )
        lane = lax.broadcasted_iota(jnp.int32, (rows, 128), 1)
        cols = jnp.zeros((rows, 128), jnp.float32)
        for number, ref in enumerate((attn_ref, ffn_ref)):
            row = wide(ref[...])
            col = jnp.sum(jnp.where(same, row, 0.0), axis=1, keepdims=True)
            cols = jnp.where(lane == number, col, cols)
        for other in range(2):
            outs[other][:, counts[0] :] = low(cols)

    shapes = [
        jax.ShapeDtypeStruct((rows, count + extra), jnp.bfloat16)
        for count, extra in zip(counts, (128, 0))
        for _ in range(2)
    ]
    return pl.pallas_call(
        kernel,
        out_shape=shapes,
        in_specs=[IN_SMEM] + [IN_VMEM] * (2 + len(shards_qkv) + len(shards_in)),
        out_specs=[IN_VMEM] * len(shapes),
    )(place, gain_attn, gain_ffn, *shards_qkv, *shards_in)


def prepare(compute, operands, shapes, after=(), place=None, pair=()):
    scalars = [] if place is None else [place]

    def kernel(*refs):
        refs = list(refs)
        where = [ref[0] for ref in refs[: len(scalars)]]
        ins, refs = refs[len(scalars) :][: len(operands)], refs[len(scalars) + len(operands) :]
        outs = refs[len(pair) + len(after) :]
        outs[-1][0, 0] = 0.0
        if pair:
            outs[-2][...] = refs[0][...] + refs[1][...]
        compute(*where, ins, outs)

    result = pl.pallas_call(
        kernel,
        out_shape=list(shapes) + [like(array, *array.shape) for array in pair[:1]] + [TOKEN_SHAPE],
        in_specs=[IN_SMEM] * len(scalars)
        + [IN_VMEM] * (len(operands) + len(pair))
        + [IN_HBM] * len(after),
        out_specs=[IN_VMEM] * (len(shapes) + len(pair[:1])) + [IN_SMEM],
        compiler_params=pltpu.CompilerParams(vmem_limit_bytes=8 * MIB),
        cost_estimate=cost(0, sum(2 * array.size for array in operands)),
    )(*scalars, *operands, *pair, *after)
    return result[:-1], result[-1]


def like(array, *shape):
    return jax.ShapeDtypeStruct(shape, array.dtype)


def chip_unit(place, mine, got, after=()):
    def compute(me, ins, outs):
        first = me % 2 == 0
        own, other = wide(ins[0][...]), wide(ins[1][...])
        outs[0][...] = low(
            jnp.concatenate([jnp.where(first, own, other), jnp.where(first, other, own)], 0)
        )

    shape = like(mine, 2 * mine.shape[0], mine.shape[1])
    (unit,), token = prepare(compute, [mine, got], [shape], after, place)
    return unit, token


def stack_and_unit(place, parts, mine, got, after=()):
    def compute(me, ins, outs):
        for number in range(len(parts)):
            outs[0][number] = ins[number][...]
        first = me % 2 == 0
        own, other = wide(ins[-2][...]), wide(ins[-1][...])
        outs[1][...] = low(
            jnp.concatenate([jnp.where(first, own, other), jnp.where(first, other, own)], 0)
        )

    shapes = [
        like(parts[0], len(parts), *parts[0].shape),
        like(mine, 2 * mine.shape[0], mine.shape[1]),
    ]
    operands = list(tuple(parts) + (mine, got))
    return prepare(compute, operands, shapes, after, place)


def stack_and_copies(parts, arrays, after=()):
    def compute(ins, outs):
        for number in range(len(parts)):
            outs[0][number] = ins[number][...]
        for number in range(len(arrays)):
            outs[1 + number][...] = ins[len(parts) + number][...]

    shapes = [like(parts[0], len(parts), *parts[0].shape)]
    shapes += [like(array, *array.shape) for array in arrays]
    return prepare(compute, [*parts, *arrays], shapes, after)


def copied(arrays, after=()):
    def compute(ins, outs):
        for number in range(len(arrays)):
            outs[number][...] = ins[number][...]

    shapes = [like(array, *array.shape) for array in arrays]
    return prepare(compute, list(arrays), shapes, after)


def far_and_copies(over_x, over_y, arrays, after=()):
    half = over_x.shape[0] // 2

    def compute(ins, outs):
        outs[0][...] = ins[0][:half]
        outs[1][...] = ins[1][half:]
        for number in range(len(arrays)):
            outs[2 + number][...] = ins[2 + number][...]

    shapes = [like(over_x, half, *over_x.shape[1:])] * 2
    shapes += [like(array, *array.shape) for array in arrays]
    return prepare(compute, [over_y, over_x, *arrays], shapes, after)


def first_sends(keep, got, after=(), pair=()):
    places = ((3, 0), (1, 0), (3, 1), (2, 1))
    half = keep.shape[1] // 2

    def compute(ins, outs):
        for number, (plane, late) in enumerate(places):
            for hop in range(half):
                at = late * half + hop
                outs[number // 2][number % 2, hop] = low(
                    wide(ins[0][plane, at]) + wide(ins[1][plane, at])
                )

    shapes = [like(keep, 2, half, *keep.shape[2:])] * 2
    return prepare(compute, [keep, got], shapes, after, pair=pair)


def second_sends(keep, got, first, after=(), pair=()):
    half = keep.shape[1] // 2

    def compute(ins, outs):
        for number, (plane, late) in enumerate(((2, 0), (1, 1))):
            for hop in range(half):
                at = late * half + hop
                outs[number][hop] = low(
                    wide(ins[0][plane, at])
                    + wide(ins[1][plane, at])
                    + wide(ins[2 + number][0, hop])
                )

    shapes = [like(keep, half, *keep.shape[2:])] * 2
    return prepare(compute, [keep, got, *first], shapes, after, pair=pair)


def line_sums(keep, got, first, second, after=(), pair=()):
    line = keep.shape[1]
    half = line // 2

    def compute(ins, outs):
        for at in range(line):
            direct, merged = ins[2 + at // half], ins[4 + at // half]
            total = wide(ins[0][0, at]) + wide(ins[1][0, at]) + wide(direct[1, at % half])
            outs[at][...] = low(total + wide(merged[at % half]))

    operands = [keep, got, *first, *second]
    return prepare(compute, operands, [like(keep, *keep.shape[2:])] * line, after, pair=pair)


def chip_sum_halves(place, terms, copied=(), after=(), pair=()):
    rows, cols = terms[0].shape

    def compute(me, ins, outs):
        total = add(*[ref[...] for ref in ins[: len(terms)]])
        first = me % 2 == 0
        upper, lower = total[: rows // 2], total[rows // 2 :]
        outs[0][...] = jnp.where(first, upper, lower)
        outs[1][...] = jnp.where(first, lower, upper)
        for number in range(len(copied)):
            outs[2 + number][...] = ins[len(terms) + number][...]

    shape = jax.ShapeDtypeStruct((rows // 2, cols), jnp.float32)
    shapes = [shape, shape] + [like(array, *array.shape) for array in copied]
    operands = list(tuple(terms) + tuple(copied))
    return prepare(compute, operands, shapes, after, place, pair=pair)


def join_halves(place, mine, other, parts, factor, gain, weights, after=()):
    rows = mine.shape[0]
    skipped = len(parts) - len(weights)

    def compute(me, ins, outs):
        core = me % 2
        first = 0
        for count, out in zip(parts, outs):
            for ref, half in ((ins[0], core), (ins[1], 1 - core)):
                start = pl.multiple_of(half * count, 128)
                out[:, pl.ds(start, count)] = ref[:, first : first + count] * factor
            first += count
        total = jnp.zeros((rows, 1), jnp.float32)
        for number, weight in enumerate(ins[3:]):
            product = wide(weight[...]) * outs[skipped + number][...]
            total = total + jnp.sum(product, axis=1, keepdims=True)
        same = lax.broadcasted_iota(jnp.int32, (rows, rows), 0) == lax.broadcasted_iota(
            jnp.int32, (rows, rows), 1
        )
        column = jnp.sum(jnp.where(same, wide(ins[2][...]), 0.0), axis=1, keepdims=True)
        outs[len(parts)][...] = jnp.broadcast_to(total / column, (rows, 128))

    shapes = [jax.ShapeDtypeStruct((rows, 2 * count), jnp.float32) for count in parts]
    shapes.append(jax.ShapeDtypeStruct((rows, 128), jnp.float32))
    operands = list((mine, other, gain[None]) + tuple(weights))
    return prepare(compute, operands, shapes, after, place)[0]


def gather_plain(shards):
    full = [lax.all_gather(shard, "fsdp", axis=0, tiled=True) for shard in shards]
    gain_attn, w_query, w_key, w_value, w_attn_out, gain_ffn, w_ffn_in, w_ffn_out = full
    gains = jnp.pad(jnp.stack([gain_attn, gain_ffn], 1), ((0, 0), (0, 126)))
    return (
        (halves_of(w_query, w_key, w_value, jnp.concatenate([gains, gains], 1)),),
        (halves_of(w_attn_out, w_ffn_in),),
        (w_ffn_out,),
    )


def gain_back(gain, weights, grads):
    return sum(
        jnp.sum(weight.astype(jnp.float32) * grad, axis=1) for weight, grad in zip(weights, grads)
    ) / gain.astype(jnp.float32)


def per_device(
    tokens,
    lengths,
    gain_attn,
    w_query,
    w_key,
    w_value,
    w_attn_out,
    gain_ffn,
    w_ffn_in,
    w_ffn_out,
    bucket_bias_matrix,
    cotangent,
):
    slot_count, width = tokens.shape
    heads = bucket_bias_matrix.shape[1]
    devices = lax.axis_size("fsdp")
    factor = 1.0 / math.sqrt(slot_count * devices)
    place = lax.axis_index("fsdp").astype(jnp.int32)[None]
    side = width // 2
    by_chips = devices == 32
    pairs = heads // 2
    done, shared, attended, backs = [0], [], [], []

    def forward(count, after=()):
        out, prob, token = attend(
            lengths, qkv, planes, done[0], count, tuple(shared), after
        )
        done[0] += count
        attended.append(out)
        shared[:] = [prob]
        return token

    def backward(count, after=()):
        first = sum(some[0].shape[1] for some in backs) * heads // (2 * width)
        result = attend_back(qkv, grad_attended, prob, first, count, heads, after)
        backs.append(result[:4])
        return result[4]

    def weights(after=()):
        grads, diagonals = [some[:3] for some in backs], [some[3] for some in backs]
        return weights_back(place, normed_attn, grads, diagonals, by_chips, after)

    def inputs(first, count, done=None, after=()):
        grads = [some[:3] for some in backs]
        return inputs_back(
            tokens, gains, saved[0], grads, weights_qkv, place, first, count, done, after
        )

    if by_chips:
        mine_qkv, for_qkv, mine_in, for_in = pack_halves(
            place,
            gain_attn[None],
            gain_ffn[None],
            (w_query, w_key, w_value),
            (w_attn_out, w_ffn_in),
        )
        unit, token = chip_unit(place, mine_qkv, swap(for_qkv, 1))
        line = gather_line(unit)
        planes, token = bias_planes(bucket_bias_matrix, (token,))

        (near_qkv, unit), token = stack_and_copies(line, (w_ffn_out,), (token,))
        plane_qkv = gather_plane(near_qkv)
        line = gather_line(unit)

        parts, token = far_and_copies(*plane_qkv, (near_qkv,) + plane_qkv, line + (token,))
        far_qkv = gather_far(*parts[:2])
        other_qkv = tuple(swap(part, 1) for part in parts[2:])

        (near_out, unit), token = stack_and_unit(
            place, line, mine_in, swap(for_in, 1), far_qkv + other_qkv + (token,)
        )
        plane_out = gather_plane(near_out)
        other_qkv = other_qkv + (swap(far_qkv[0], 1), swap(far_qkv[1], 1))
        in_qkv = (near_qkv,) + plane_qkv + far_qkv + other_qkv
        qkv, normed_attn, weights_qkv, gains, token = project_qkv(
            place, tokens, in_qkv, by_chips, (planes, token)
        )

        parts, token = far_and_copies(*plane_out, (unit,), (token,))
        far_out = gather_far(*parts[:2])
        line = gather_line(parts[2])
        token = forward(2, (token,))

        parts, token = stack_and_copies(line, (near_out,) + plane_out, far_out + (token,))
        near_in = parts[0]
        plane_in = gather_plane(near_in)
        other_out = tuple(swap(part, 1) for part in parts[1:])
        token = forward(2, (token,))

        parts, token = far_and_copies(*plane_in, far_out + (near_in,), other_out + (token,))
        far_in = gather_far(*parts[:2])
        other_out = other_out + (swap(parts[2], 1), swap(parts[3], 1))
        other_in = (swap(parts[4], 1),)
        token = forward(1, (token,))

        parts, token = copied(plane_in + far_in, other_in + other_out[3:] + (token,))
        other_in = other_in + tuple(swap(part, 1) for part in parts)
        token = forward(1, (token,))

        in_ffn = (near_in,) + plane_in + far_in + other_in
        in_out = (near_out,) + plane_out + far_out + other_out
    else:
        planes, _ = bias_planes(bucket_bias_matrix)
        in_qkv, in_ffn, in_out = gather_plain(
            (gain_attn, w_query, w_key, w_value, w_attn_out, gain_ffn, w_ffn_in, w_ffn_out)
        )
        qkv, normed_attn, weights_qkv, gains, _ = project_qkv(place, tokens, in_qkv, by_chips)
        for _ in range(pairs):
            forward(1)

    (prob,) = shared
    output, grad_attended, saved, part_out = feed_forward(
        place, tokens, attended, cotangent, gains, in_ffn, in_out, by_chips
    )

    if by_chips:
        keep_out, send_out = part_out
        got_out = swap(send_out, 1)
        (keep_in, send_in), token = in_weights_back(place, attended, *saved, by_chips)

        sends, token = first_sends(keep_out, got_out, (token,))
        first_out = scatter_first(sends)
        got_in = swap(send_in, 1)
        token = backward(2, (token,))

        sends, token = second_sends(keep_out, got_out, first_out, (got_in, token))
        second_out = scatter_second(sends)
        token = backward(1, (token,))

        sums, token = line_sums(keep_out, got_out, first_out, second_out, (token,))
        last_out = scatter_line(sums)
        sends, token = first_sends(keep_in, got_in, (token,))
        first_in = scatter_first(sends)
        token = backward(2, (token,))

        sends, token = second_sends(keep_in, got_in, first_in, last_out + (token,))
        second_in = scatter_second(sends)
        token = backward(1, (token,))

        sums, token = line_sums(keep_in, got_in, first_in, second_in, (token,))
        last_in = scatter_line(sums)
        (keep_qkv, send_qkv), table, token = weights(last_out + (token,))

        parts, token = chip_sum_halves(place, last_in, (send_qkv, table), (token,))
        mine_in, for_in, send_qkv, table = parts
        got_qkv, got_in, got = swap(send_qkv, 1), swap(for_in, 1), swap(table, 1)
        grad_tokens, token = inputs(0, slot_count // 2, None, (token,))

        parts, token = first_sends(keep_qkv, got_qkv, (got_in, token), (table, got))
        first_qkv = scatter_first(parts[:2])
        table, got = parts[2], swap(parts[2], 2)
        grad_tokens, token = inputs(slot_count // 2, slot_count // 2, grad_tokens, (token,))

        parts, token = second_sends(keep_qkv, got_qkv, first_qkv, (token,), (table, got))
        second_qkv = scatter_second(parts[:2])
        table, got = parts[2], swap(parts[2], 4)
        sum_out = add(*last_out) * factor

        parts, token = line_sums(
            keep_qkv, got_qkv, first_qkv, second_qkv, (token,), (table, got)
        )
        last_qkv = scatter_line(parts[:-1])
        table, got = parts[-1], swap(parts[-1], 8)
        sum_o, sum_in, grad_gain_ffn = join_halves(
            place,
            mine_in,
            got_in,
            (side, keep_in.shape[-1] - side),
            factor,
            gain_ffn,
            (w_ffn_in,),
            (token,),
        )

        parts, token = chip_sum_halves(place, last_qkv, (), (token,), (table, got))
        mine_qkv, for_qkv, table = parts
        got_qkv, got = swap(for_qkv, 1), swap(table, 16)
        table = table + got
        sum_q, sum_k, sum_v, grad_gain_attn = join_halves(
            place,
            mine_qkv,
            got_qkv,
            (side, side, side),
            factor,
            gain_attn,
            (w_query, w_key, w_value),
        )
        grad_gain_attn, grad_gain_ffn = grad_gain_attn[:, 0], grad_gain_ffn[:, 0]
        sums = (sum_q, sum_k, sum_v, sum_o, sum_in, sum_out)
    else:
        for _ in range(pairs):
            backward(1)
        part_in, _ = in_weights_back(place, attended, *saved, by_chips)
        part_qkv, table, _ = weights()
        grad_tokens, _ = inputs(0, slot_count)
        sums = sum_plain(
            jnp.concatenate([part_qkv[0], part_in[0][:, :, :side]], 2),
            part_in[0][:, :, side:],
            part_out[0],
        )
        sums = [total * factor for total in sums]
        table = lax.psum(table, "fsdp")
        grad_gain_attn = gain_back(gain_attn, (w_query, w_key, w_value), sums[:3])
        grad_gain_ffn = gain_back(gain_ffn, (w_ffn_in,), sums[4:5])

    return (
        output,
        grad_tokens,
        grad_gain_attn,
        sums[0],
        sums[1],
        sums[2],
        sums[3],
        grad_gain_ffn,
        sums[4],
        sums[5],
        table[:heads, :NB].T * factor,
    )


def solution(mesh):
    placed = (
        P("fsdp", None),
        P("fsdp", None),
        P("fsdp"),
        P("fsdp", None),
        P("fsdp", None),
        P("fsdp", None),
        P("fsdp", None),
        P("fsdp"),
        P("fsdp", None),
        P("fsdp", None),
        P(),
        P("fsdp", None),
    )
    return jax.shard_map(
        per_device,
        mesh=mesh,
        in_specs=placed,
        out_specs=(
            P("fsdp", None),
            P("fsdp", None),
            P("fsdp"),
            P("fsdp", None),
            P("fsdp", None),
            P("fsdp", None),
            P("fsdp", None),
            P("fsdp"),
            P("fsdp", None),
            P("fsdp", None),
            P(),
        ),
        check_vma=False,
    )
```

```python
import functools
import math

import jax
import jax.numpy as jnp
import numpy as np
from jax import lax
from jax.experimental import pallas as pl
from jax.experimental.pallas import tpu as pltpu
from jax.sharding import PartitionSpec as P

NB = 32
MAXD = 128
SEQ = 512
MIB = 1024 * 1024


def bucket_ids(span_length):
    offset = np.arange(span_length)[None, :] - np.arange(span_length)[:, None]
    half_count = NB // 2
    exact_count = half_count // 2
    result = np.where(offset > 0, half_count, 0)
    distance = np.abs(offset)
    spread = exact_count + np.floor(
        np.log(np.maximum(distance, 1) / exact_count)
        / math.log(MAXD / exact_count)
        * (half_count - exact_count)
    )
    spread = np.minimum(spread, half_count - 1)
    result = result + np.where(distance < exact_count, distance, spread)
    return result.astype(np.int32)


def flip(mask, count):
    return [(i, i ^ mask) for i in range(count)]


def swap(array, mask):
    return lax.ppermute(array, "fsdp", flip(mask, lax.axis_size("fsdp")))


def gather_line(unit):
    line = lax.axis_size("fsdp") // 8
    return (unit,) + tuple(swap(unit, 8 * hop) for hop in range(1, line))


def gather_plane(near):
    return swap(near, 2), swap(near, 4)


def gather_far(first, second):
    return swap(first, 2), swap(second, 4)


def chip_distances():
    line = lax.axis_size("fsdp") // 8
    half = line // 2
    blocks = []
    for part, (plane, first, last) in enumerate(
        ((0, 0, line), (1, 0, line), (2, 0, line), (3, 0, half), (3, half, line))
    ):
        blocks += [(part, hop - first, 4 * hop + plane) for hop in range(first, last)]
    return blocks


def add(*terms):
    return sum(term.astype(jnp.float32) for term in terms)


def scatter_first(sends):
    return swap(sends[0], 2), swap(sends[1], 4)


def scatter_second(sends):
    return swap(sends[0], 4), swap(sends[1], 2)


def scatter_line(sums):
    return (sums[0],) + tuple(swap(total, 8 * hop) for hop, total in enumerate(sums) if hop)


def halves_of(*arrays):
    return jnp.stack(
        [
            jnp.concatenate(
                [
                    array[:, part * array.shape[1] // 2 : (part + 1) * array.shape[1] // 2]
                    for array in arrays
                ],
                1,
            )
            for part in range(2)
        ]
    )


def sum_plain(half_attn, half_in, grad_out):
    side = half_attn.shape[-1] // 4

    def owned(array):
        return lax.psum_scatter(
            array.astype(jnp.float32), "fsdp", scatter_dimension=0, tiled=True
        )

    grads = [
        jnp.concatenate([part[0], part[1]], 1)
        for part in [half_attn[:, :, k * side : (k + 1) * side] for k in range(4)] + [half_in]
    ]
    return [owned(grad) for grad in grads + [grad_out]]


def nn(left, right):
    return lax.dot_general(
        left, right, (((1,), (0,)), ((), ())), preferred_element_type=jnp.float32
    )


def nt(left, right):
    return lax.dot_general(
        left, right, (((1,), (1,)), ((), ())), preferred_element_type=jnp.float32
    )


def tn(left, right):
    return lax.dot_general(
        left, right, (((0,), (0,)), ((), ())), preferred_element_type=jnp.float32
    )


def low(value):
    return value.astype(jnp.bfloat16)


def wide(value):
    return value.astype(jnp.float32)


def norm_scale(values):
    return lax.rsqrt(jnp.mean(values * values, axis=-1, keepdims=True) + 1e-06)


def rms_back(scaled, scale, gain, grad_normed):
    weighted = grad_normed * gain
    return scale * (weighted - scaled * jnp.mean(weighted * scaled, axis=-1, keepdims=True))


IN_HBM = pl.BlockSpec(memory_space=pl.ANY)
ONLY_HBM = pl.BlockSpec(memory_space=pltpu.HBM)
IN_SMEM = pl.BlockSpec(memory_space=pltpu.SMEM)
IN_VMEM = pl.BlockSpec(memory_space=pltpu.VMEM)
TOKEN_SHAPE = jax.ShapeDtypeStruct((1, 1), jnp.float32)
TOKEN = pl.BlockSpec((1, 1), lambda *_: (0, 0), memory_space=pltpu.SMEM)


def cost(flops, bytes_moved):
    return pl.CostEstimate(flops=flops, bytes_accessed=bytes_moved, transcendentals=0)


def plan(me, rows, by_chips, side, per_core):
    chip, core = me // 2, me % 2
    if not by_chips:
        return []
    count = 5
    found = []
    for part, index, distance in chip_distances():
        number = chip ^ distance
        if per_core:
            number = number * 2 + (core ^ side)
        found.append((side * count + part, index, pl.multiple_of(number * rows, 16)))
    return found


def column_copies(me, sources, target, sems, side, by_chips, columns):
    first, last = columns
    if not by_chips:
        half = (me % 2) ^ side
        return [
            pltpu.make_async_copy(sources[0].at[half, :, pl.ds(first, last - first)], target, sems.at[0])
        ]
    rows = sources[0].shape[1]
    return [
        pltpu.make_async_copy(
            sources[part].at[index, :, pl.ds(first, last - first)],
            target.at[pl.ds(start, rows), :],
            sems.at[number],
        )
        for number, (part, index, start) in enumerate(plan(me, rows, True, side, False))
    ]


def row_copies(me, sources, target, sems, side, by_chips):
    if not by_chips:
        half = target.shape[0] // 2
        where = pl.ds(side * half, half)
        return [pltpu.make_async_copy(sources[0].at[where, :], target.at[where, :], sems.at[0])]
    rows = sources[0].shape[1]
    return [
        pltpu.make_async_copy(
            sources[part].at[index], target.at[pl.ds(start, rows), :], sems.at[number]
        )
        for number, (part, index, start) in enumerate(plan(me, rows, True, side, True))
    ]


def start_all(copies):
    for copy in copies:
        copy.start()


def wait_all(copies):
    for copy in copies:
        copy.wait()


def half_copies(me, tile, targets, sems, side, by_chips, columns):
    first, count = columns
    if not by_chips:
        half = (me % 2) ^ side
        return [
            pltpu.make_async_copy(tile, targets[0].at[half, :, pl.ds(first, count)], sems.at[0])
        ]
    planes, line, rows = targets[side].shape[:3]
    chip = me // 2
    return [
        pltpu.make_async_copy(
            tile.at[pl.ds(pl.multiple_of((chip ^ (4 * hop + plane)) * rows, 16), rows), :],
            targets[side].at[plane, hop, :, pl.ds(first, count)],
            sems.at[plane * line + hop],
        )
        for plane in range(planes)
        for hop in range(line)
    ]


def strip_copies(me, tile, targets, sems, strip, by_chips):
    if not by_chips:
        rows = tile.shape[0]
        return [
            pltpu.make_async_copy(
                tile, targets[0].at[pl.ds(pl.multiple_of(strip * rows, 16), rows), :], sems.at[0]
            )
        ]
    planes, line, rows = targets[0].shape[:3]
    chip, core = me // 2, me % 2
    return [
        pltpu.make_async_copy(
            tile.at[
                pl.ds(pl.multiple_of((((chip % 4) ^ plane) * 2 + (core ^ side)) * rows, 16), rows), :
            ],
            targets[side].at[plane, (chip // 4) ^ strip],
            sems.at[side * planes + plane],
        )
        for side in range(2)
        for plane in range(planes)
    ]


def bias_planes(table, after=()):
    heads = table.shape[1]
    ids = bucket_ids(SEQ)
    flat = np.concatenate([ids[:, 0], ids[0, :1], ids[0, :0:-1]])
    onehot = (np.arange(table.shape[0])[:, None] == flat[None, :]).astype(np.float32)

    def kernel(table_ref, onehot_ref, *refs):
        plane_ref, token_ref, rows = refs[len(after) :]
        token_ref[0, 0] = 0.0
        head = pl.program_id(0)

        @pl.when(head == 0)
        def _():
            rows[:heads] = lax.dot_general(
                wide(table_ref[...]),
                onehot_ref[...],
                (((0,), (0,)), ((), ())),
                precision=lax.Precision.HIGHEST,
                preferred_element_type=jnp.float32,
            )

        spread = jnp.broadcast_to(rows[pl.ds(head, 1), :], (SEQ, 2 * SEQ))
        moved = pltpu.roll(spread, 0, 1, stride=1, stride_axis=0)
        plane_ref[0] = low(moved[:, :SEQ])

    return pl.pallas_call(
        kernel,
        grid=(heads,),
        out_shape=[jax.ShapeDtypeStruct((heads, SEQ, SEQ), jnp.bfloat16), TOKEN_SHAPE],
        in_specs=[IN_VMEM, IN_VMEM] + [IN_HBM] * len(after),
        out_specs=[pl.BlockSpec((1, SEQ, SEQ), lambda head: (head, 0, 0)), TOKEN],
        scratch_shapes=[pltpu.VMEM((-(-heads // 8) * 8, 2 * SEQ), jnp.float32)],
        compiler_params=pltpu.CompilerParams(vmem_limit_bytes=16 * MIB),
    )(table, jnp.asarray(onehot), *after)


def line_ids():
    ids = bucket_ids(SEQ)
    ahead = (np.arange(2 * SEQ) - (SEQ - 128) + SEQ) % (2 * SEQ) - SEQ
    return np.where(ahead >= 0, ids[np.maximum(ahead, 0), 0], ids[0, np.minimum(-ahead, SEQ - 1)])


def project_qkv(place, tokens, sources, by_chips, after=()):
    slots, width = tokens.shape
    side_cols = width // 2
    packed = sources[0].shape[-1]
    block = 256

    def kernel(place_ref, x_ref, *refs):
        ins, refs = refs[: len(sources)], refs[len(sources) + len(after) :]
        out_ref, normed_hbm, weights_hbm, gains_ref, token_ref, normed_ref, weights, sems = refs
        token_ref[0, 0] = 0.0
        me = place_ref[0]
        core = me % 2

        def put(side):
            if not by_chips:
                weights[side] = ins[0][(me % 2) ^ side]
                return
            rows = ins[0].shape[1]
            for part, index, start in plan(me, rows, True, side, False):
                weights[side, pl.ds(start, rows), :] = ins[part][index]

        put(0)
        gains = jnp.transpose(wide(weights[0, :, 3 * side_cols :]))
        gains_ref[...] = gains[:8]

        def normalise(index, carry):
            where = pl.ds(pl.multiple_of(index * block, block), block)
            rows = wide(x_ref[where, :])
            normed_ref[where, :] = low(rows * norm_scale(rows) * gains_ref[0:1, :])
            return carry

        lax.fori_loop(0, slots // block, normalise, 0)
        put(1)
        stores = [
            pltpu.make_async_copy(normed_ref, normed_hbm, sems.at[0]),
            pltpu.make_async_copy(weights, weights_hbm, sems.at[1]),
        ]
        start_all(stores)

        def one(index, carry):
            side, part = index // 3, index % 3
            here = pl.ds(pl.multiple_of(part * side_cols, 128), side_cols)
            cols = pl.ds(pl.multiple_of((core ^ side) * side_cols, 128), side_cols)
            out_ref[part, :, cols] = low(nn(normed_ref[...], weights[side, :, here]))
            return carry

        lax.fori_loop(0, 6, one, 0)
        wait_all(stores)

    sums = jax.ShapeDtypeStruct
    return pl.pallas_call(
        kernel,
        out_shape=[
            sums((3, slots, width), jnp.bfloat16),
            sums((slots, width), jnp.bfloat16),
            sums((2, width, packed), jnp.bfloat16),
            sums((8, width), jnp.float32),
            TOKEN_SHAPE,
        ],
        in_specs=[IN_SMEM] + [IN_VMEM] * (1 + len(sources)) + [IN_HBM] * len(after),
        out_specs=[IN_VMEM, ONLY_HBM, ONLY_HBM, IN_VMEM, IN_SMEM],
        scratch_shapes=[
            pltpu.VMEM((slots, width), jnp.bfloat16),
            pltpu.VMEM((2, width, packed), jnp.bfloat16),
            pltpu.SemaphoreType.DMA((2,)),
        ],
        compiler_params=pltpu.CompilerParams(vmem_limit_bytes=24 * MIB),
        cost_estimate=cost(6 * slots * width * width, 12 * slots * width),
    )(place, tokens, *sources, *after)


def attend(lengths, qkv, planes, first, count, after=()):
    _, slots, width = qkv.shape
    seqs = slots // SEQ
    heads = planes.shape[0]
    pair_cols = 2 * width // heads
    head_size = pair_cols // 2

    def kernel(lengths_ref, qkv_ref, planes_ref, *refs):
        q, k, v = (qkv_ref.at[part] for part in range(3))
        out, prob, token_ref, scores = refs[len(after) :]
        token_ref[0, 0] = 0.0

        own_lane = lax.broadcasted_iota(jnp.int32, (1, pair_cols), 1) < head_size
        key_number = lax.broadcasted_iota(jnp.int32, (SEQ, 1), 0)
        zero = jnp.zeros((), jnp.bfloat16)

        def both_heads(rows):
            return jnp.concatenate(
                [jnp.where(own_lane, rows, zero), jnp.where(own_lane, zero, rows)], 0
            )

        def one(step, carry):
            pair, seq = step // seqs, step % seqs
            rows = pl.ds(pl.multiple_of(seq * SEQ, SEQ), SEQ)
            own = pl.ds(pl.multiple_of(pair * pair_cols, pair_cols), pair_cols)
            lanes = pl.ds(pl.multiple_of((first + pair) * pair_cols, pair_cols), pair_cols)

            permitted = key_number < lengths_ref[seq, 0] + lengths_ref[seq, 1]
            scores[...] = nt(both_heads(k[rows, lanes]), q[rows, lanes])
            for head in range(2):
                these = scores[head * SEQ : (head + 1) * SEQ, :] + wide(planes_ref[2 * (first + pair) + head])
                these = jnp.where(permitted, these, -1e30)
                raised = jnp.exp(these - jnp.max(these, axis=0, keepdims=True))
                total = jnp.sum(raised, axis=0, keepdims=True)
                prob[seq, 2 * pair + head] = low(raised * (1.0 / total))
            both = prob[seq, pl.ds(2 * pair, 2)].reshape(2 * SEQ, SEQ)
            mixed = tn(both, both_heads(v[rows, lanes]))
            out[rows, own] = low(mixed)
            return carry

        lax.fori_loop(0, count * seqs, one, 0)

    return pl.pallas_call(
        kernel,
        out_shape=[
            jax.ShapeDtypeStruct((slots, count * pair_cols), jnp.bfloat16),
            jax.ShapeDtypeStruct((seqs, 2 * count, SEQ, SEQ), jnp.bfloat16),
            TOKEN_SHAPE,
        ],
        in_specs=[IN_SMEM] + [IN_VMEM] * 2 + [IN_HBM] * len(after),
        out_specs=[IN_VMEM, IN_VMEM, IN_SMEM],
        scratch_shapes=[
            pltpu.VMEM((2 * SEQ, SEQ), jnp.float32),
        ],
        compiler_params=pltpu.CompilerParams(vmem_limit_bytes=12 * MIB),
        cost_estimate=cost(count * slots * SEQ * 2048, count * slots * SEQ * 8),
    )(lengths, qkv, planes, *after)


def attend_back(qkv, grad_mixed, prob, first, count, heads, after=()):
    _, slots, width = qkv.shape
    seqs = slots // SEQ
    pair_cols = 2 * width // heads
    head_size = pair_cols // 2
    steps = count * seqs

    def kernel(qkv_ref, g, prob_ref, *refs):
        q, k, v = (qkv_ref.at[part] for part in range(3))
        dq, dk, dv, table_ref, token_ref, grads, scored, planes = refs[len(after) :]
        token_ref[0, 0] = 0.0

        own_lane = lax.broadcasted_iota(jnp.int32, (1, pair_cols), 1) < head_size
        zero = jnp.zeros((), jnp.bfloat16)

        def both_heads(rows):
            return jnp.concatenate(
                [jnp.where(own_lane, rows, zero), jnp.where(own_lane, zero, rows)], 0
            )

        def one(step, carry):
            pair, seq = step // seqs, step % seqs
            prob = prob_ref.at[seq, pl.ds(2 * pair, 2)]
            rows = pl.ds(pl.multiple_of(seq * SEQ, SEQ), SEQ)
            own = pl.ds(pl.multiple_of(pair * pair_cols, pair_cols), pair_cols)
            lanes = pl.ds(pl.multiple_of((first + pair) * pair_cols, pair_cols), pair_cols)

            grads[...] = nt(both_heads(v[rows, lanes]), g[rows, lanes])
            summed = nn(prob[...].reshape(2 * SEQ, SEQ), g[rows, lanes])
            dv[rows, own] = low(jnp.where(own_lane, summed[:SEQ], summed[SEQ:]))
            keep = jnp.where(seq == 0, 0.0, 1.0)
            for head in range(2):
                there = slice(head * SEQ, (head + 1) * SEQ)
                weights = wide(prob[head])
                weighted = weights * grads[there, :]
                dot = jnp.sum(weighted, axis=0, keepdims=True)
                grad_scores = weighted - weights * dot
                planes[head] = planes[head] * keep + grad_scores
                scored[there, :] = low(grad_scores)
            summed = nn(scored[...], q[rows, lanes])
            dk[rows, own] = low(jnp.where(own_lane, summed[:SEQ], summed[SEQ:]))
            dq[rows, own] = low(tn(scored[...], both_heads(k[rows, lanes])))

            @pl.when(seq == seqs - 1)
            def _():
                for head in range(2):
                    lined = jnp.zeros((8, 2 * SEQ), jnp.float32)
                    for low_row in range(0, 128, 8):
                        frame = jnp.zeros((8, 2 * SEQ), jnp.float32)
                        for high_row in range(0, SEQ, 128):
                            some = planes[head, high_row + low_row : high_row + low_row + 8, :]
                            ahead = SEQ - 128 - high_row
                            filled = [some, jnp.zeros((8, SEQ - ahead), jnp.float32)]
                            if ahead:
                                filled = [jnp.zeros((8, ahead), jnp.float32)] + filled
                            frame = frame + jnp.concatenate(filled, 1)
                        if low_row:
                            frame = pltpu.roll(frame, 2 * SEQ - low_row, 1)
                        lined = lined + frame
                    moved = lined[:1]
                    for row in range(1, 8):
                        moved = moved + pltpu.roll(lined[row : row + 1], 2 * SEQ - row, 1)
                    table_ref[pair, head : head + 1, :] = moved

            return carry

        planes[...] = jnp.zeros_like(planes)
        lax.fori_loop(0, steps, one, 0)

    result = jax.ShapeDtypeStruct((slots, count * pair_cols), jnp.bfloat16)
    return pl.pallas_call(
        kernel,
        in_specs=[IN_VMEM] * 3 + [IN_HBM] * len(after),
        out_specs=[IN_VMEM] * 4 + [IN_SMEM],
        out_shape=[result] * 3
        + [jax.ShapeDtypeStruct((count, 8, 2 * SEQ), jnp.float32), TOKEN_SHAPE],
        scratch_shapes=[
            pltpu.VMEM((2 * SEQ, SEQ), jnp.float32),
            pltpu.VMEM((2 * SEQ, SEQ), jnp.bfloat16),
            pltpu.VMEM((2, SEQ, SEQ), jnp.float32),
        ],
        compiler_params=pltpu.CompilerParams(vmem_limit_bytes=16 * MIB),
        cost_estimate=cost(count * slots * SEQ * 4096, count * slots * SEQ * 8),
    )(qkv, grad_mixed, prob, *after)


def feed_forward(place, tokens, attended, cotangent, gains, in_sources, out_sources, by_chips):
    slots, width = tokens.shape
    side_cols = width // 2
    hidden_cols = 2 * (in_sources[0].shape[-1] - side_cols)
    block = 256
    blocks = slots // block
    chunk = 768
    per_side = hidden_cols // 2 // chunk
    count_att = len(attended)
    root, bend = math.sqrt(2.0 / math.pi), 0.044715

    def kernel(place_ref, x_hbm, cot_hbm, gains_ref, *refs):
        refs = list(refs)

        def take(number):
            taken, refs[:] = refs[:number], refs[number:]
            return taken

        att_hbm, in_hbm, out_hbm = take(count_att), take(len(in_sources)), take(len(out_sources))
        y_hbm, back_hbm, branch_hbm, flipped_hbm, pre_hbm = take(5)
        out_targets = take(2 if by_chips else 1)
        x, att, cot, w_o, w_in, w_out, hidden, normed, flipped = take(9)
        sum_g, act, grad_pre, tile_out = take(4)
        load_sems, o_sems, in_sems, out_sems, store_sems, pre_sems, tile_out_sems = take(7)
        me = place_ref[0]
        core = me % 2
        gain = gains_ref[1:2, :]

        def rows_of(index):
            return pl.ds(pl.multiple_of(index * block, block), block)

        loads = [
            pltpu.make_async_copy(x_hbm, x, load_sems.at[0]),
            pltpu.make_async_copy(cot_hbm, cot, load_sems.at[1]),
        ]
        cols = 0
        for number, source in enumerate(att_hbm):
            loads.append(
                pltpu.make_async_copy(
                    source, att.at[:, pl.ds(cols, source.shape[1])], load_sems.at[2 + number]
                )
            )
            cols += source.shape[1]
        o_loads, in_loads, out_loads = [], [], []
        for side in range(2):
            o_cols = pl.ds(pl.multiple_of((core ^ side) * side_cols, 128), side_cols)
            o_loads += column_copies(
                me, in_hbm, w_o.at[:, o_cols], o_sems.at[side], side, by_chips, (0, side_cols)
            )
            in_loads.append(
                column_copies(
                    me,
                    in_hbm,
                    w_in.at[side],
                    in_sems.at[side],
                    side,
                    by_chips,
                    (side_cols, in_sources[0].shape[-1]),
                )
            )
            out_loads += row_copies(me, out_hbm, w_out, out_sems.at[side], side, by_chips)
        start_all(loads[2:])
        start_all(o_loads)
        start_all(loads[:2])
        start_all(in_loads[0])
        start_all(out_loads)
        wait_all(loads)
        wait_all(o_loads)
        start_all(in_loads[1])

        count = width // block

        def cols_of(index):
            return pl.ds(pl.multiple_of(index * block, block), block)

        def residual(index, carry):
            cols = cols_of(index)
            hidden[:, cols] = wide(x[:, cols]) + nn(att[...], w_o[:, cols])
            return carry

        lax.fori_loop(0, count, residual, 0)

        def before(index, carry):
            where = rows_of(index)
            value = hidden[where, :]
            rows = value * norm_scale(value) * gain
            normed[where, :] = low(rows)
            flipped[:, where] = low(jnp.transpose(rows))
            return carry

        lax.fori_loop(0, blocks, before, 0)
        flip_store = pltpu.make_async_copy(flipped, flipped_hbm, store_sems.at[3])
        flip_store.start()
        wait_all(in_loads[0])
        wait_all(out_loads)

        per_chunk = chunk // block
        chunks = 2 * per_side

        def tile_stores(number):
            strip = (core ^ (number // per_side)) * per_side + number % per_side
            slot = number % 2
            return strip_copies(
                me, tile_out.at[slot], out_targets, tile_out_sems.at[slot], strip, by_chips
            )

        def pre_store(number):
            side, part = number // per_side, number % per_side
            strip = (core ^ side) * per_side + part
            units = pl.ds(pl.multiple_of(part * chunk, chunk), chunk)
            return pltpu.make_async_copy(
                grad_pre.at[side, :, units], pre_hbm.at[strip], pre_sems.at[number]
            )

        def through(index, carry):
            number, inside = index // per_chunk, index % per_chunk
            side, part = number // per_side, number % per_side
            first = part * chunk + inside * block
            unit_cols = pl.ds(pl.multiple_of(first, block), block)
            unit_row = (core ^ side) * (per_side * chunk) + first
            unit_rows = pl.ds(pl.multiple_of(unit_row, block), block)

            @pl.when(index == per_side * per_chunk)
            def _():
                wait_all(in_loads[1])

            @pl.when((inside == 0) & (number >= 2))
            def _():
                wait_all(tile_stores(number - 2))

            pre = nn(normed[...], w_in[side, :, unit_cols])
            square = pre * pre
            slope = jnp.tanh(pre * (root + (root * bend) * square))
            opened = 0.5 + 0.5 * slope
            gate = opened + pre * (1.0 - slope * slope) * (
                0.5 * root + (1.5 * bend * root) * square
            )
            acted = low(pre * opened)
            act[side, :, unit_cols] = acted
            grad_pre[side, :, unit_cols] = low(nt(cot[...], w_out[unit_rows, :]) * gate)
            tile_out[number % 2, cols_of(inside), :] = low(tn(acted, cot[...]))

            @pl.when(inside == per_chunk - 1)
            def _():
                start_all(tile_stores(number))
                pre_store(number).start()

            return carry

        lax.fori_loop(0, chunks * per_chunk, through, 0)

        half = hidden_cols // 2
        halves = [pl.ds(pl.multiple_of((core ^ side) * half, block), half) for side in range(2)]

        def sums_of(index, carry):
            cols = cols_of(index)
            value = nn(act[0], w_out[halves[0], cols]) + nn(act[1], w_out[halves[1], cols])
            x[:, cols] = low(hidden[:, cols] + value)
            sum_g[:, cols] = nt(grad_pre[0], w_in[0, cols, :]) + nt(grad_pre[1], w_in[1, cols, :])
            return carry

        lax.fori_loop(0, count, sums_of, 0)

        def after(index, carry):
            where = rows_of(index)
            value = hidden[where, :]
            scale = norm_scale(value)
            back = rms_back(value * scale, scale, gain, sum_g[where, :])
            normed[where, :] = low(wide(cot[where, :]) + back)
            return carry

        y_store = pltpu.make_async_copy(x, y_hbm, store_sems.at[0])
        y_store.start()
        lax.fori_loop(0, blocks, after, 0)
        branch_store = pltpu.make_async_copy(normed, branch_hbm, store_sems.at[1])
        branch_store.start()

        def mixed_back(index, carry):
            cols = cols_of(index)
            att[:, cols] = low(nt(normed[...], w_o[cols, :]))
            return carry

        lax.fori_loop(0, count, mixed_back, 0)
        last = [pltpu.make_async_copy(att, back_hbm, store_sems.at[2])]
        last[0].start()
        last += [flip_store, y_store, branch_store]
        for number in range(chunks):
            last.append(pre_store(number))
            if number >= chunks - 2:
                last += tile_stores(number)
        wait_all(last)

    sums = jax.ShapeDtypeStruct
    flat = sums((slots, width), jnp.bfloat16)
    devices = lax.axis_size("fsdp")
    if by_chips:
        line = devices // 8
        out_shapes = [sums((4, line, hidden_cols // devices, width), jnp.bfloat16)] * 2
    else:
        out_shapes = [sums((hidden_cols, width), jnp.bfloat16)]
    outs = [
        flat,
        flat,
        flat,
        sums((width, slots), jnp.bfloat16),
        sums((hidden_cols // chunk, slots, chunk), jnp.bfloat16),
    ] + out_shapes
    bf16, f32 = jnp.bfloat16, jnp.float32
    result = pl.pallas_call(
        kernel,
        out_shape=outs,
        in_specs=[IN_SMEM, IN_HBM, IN_HBM, IN_VMEM]
        + [IN_HBM] * (count_att + len(in_sources) + len(out_sources)),
        out_specs=[IN_HBM] * len(outs),
        scratch_shapes=[
            pltpu.VMEM((slots, width), bf16),
            pltpu.VMEM((slots, width), bf16),
            pltpu.VMEM((slots, width), bf16),
            pltpu.VMEM((width, width), bf16),
            pltpu.VMEM((2, width, hidden_cols // 2), bf16),
            pltpu.VMEM((hidden_cols, width), bf16),
            pltpu.VMEM((slots, width), f32),
            pltpu.VMEM((slots, width), bf16),
            pltpu.VMEM((width, slots), bf16),
            pltpu.VMEM((slots, width), f32),
            pltpu.VMEM((2, slots, hidden_cols // 2), bf16),
            pltpu.VMEM((2, slots, hidden_cols // 2), bf16),
            pltpu.VMEM((2, chunk, width), bf16),
            pltpu.SemaphoreType.DMA((2 + count_att,)),
            pltpu.SemaphoreType.DMA((2, 16)),
            pltpu.SemaphoreType.DMA((2, 16)),
            pltpu.SemaphoreType.DMA((2, 16)),
            pltpu.SemaphoreType.DMA((4,)),
            pltpu.SemaphoreType.DMA((2 * per_side,)),
            pltpu.SemaphoreType.DMA((2, 8)),
        ],
        compiler_params=pltpu.CompilerParams(vmem_limit_bytes=56 * MIB),
        cost_estimate=cost(
            slots * width * (12 * hidden_cols + 6 * width), 60 * MIB
        ),
    )(place, tokens, cotangent, gains, *attended, *in_sources, *out_sources)
    output, back, *rest = result
    return output, back, tuple(rest[:3]), tuple(rest[3:])


def in_weights_back(place, attended, branch, flipped, grad_pre, by_chips):
    slots, width = branch.shape
    strips, _, chunk = grad_pre.shape
    side_cols = width // 2
    per_side = strips // 2
    packed = side_cols + per_side * chunk
    count_att = len(attended)

    def kernel(place_ref, branch_hbm, flipped_hbm, pre_hbm, *refs):
        att_hbm, refs = refs[:count_att], refs[count_att:]
        targets, refs = refs[:-9], refs[-9:]
        token_ref, att, branch, flipped, pre, tile, load_sems, tile_sems, o_sems = refs
        token_ref[0, 0] = 0.0
        me = place_ref[0]
        core = me % 2

        def place_of(number):
            return 1 - number // per_side, number % per_side

        def pre_load(number):
            side, part = place_of(number)
            return pltpu.make_async_copy(
                pre_hbm.at[(core ^ side) * per_side + part], pre.at[number], load_sems.at[number]
            )

        pre_loads = [pre_load(number) for number in range(strips)]
        flip_load = pltpu.make_async_copy(flipped_hbm, flipped, load_sems.at[strips])
        loads = [pltpu.make_async_copy(branch_hbm, branch, load_sems.at[strips + 1])]
        cols = 0
        for number, source in enumerate(att_hbm):
            loads.append(
                pltpu.make_async_copy(
                    source,
                    att.at[:, pl.ds(cols, source.shape[1])],
                    load_sems.at[strips + 2 + number],
                )
            )
            cols += source.shape[1]
        flip_load.start()
        start_all(pre_loads)
        start_all(loads)
        flip_load.wait()
        block = 256
        per_chunk = chunk // block

        def stores(number, side, part):
            return half_copies(
                me,
                tile.at[number % 2],
                targets,
                tile_sems.at[number % 2],
                side,
                by_chips,
                (pl.multiple_of(side_cols + part * chunk, 128), chunk),
            )

        for half in range(2):
            side = 1 - half

            def one(index, carry):
                part, inside = index // per_chunk, index % per_chunk
                number = half * per_side + part

                @pl.when(inside == 0)
                def _():
                    pre_load(number).wait()

                if half:

                    @pl.when(inside == 0)
                    def _():
                        wait_all(stores(part, 1, part))

                cols = pl.ds(pl.multiple_of(inside * block, block), block)
                tile[part % 2, :, cols] = low(nn(flipped[...], pre[number, :, cols]))

                @pl.when(inside == per_chunk - 1)
                def _():
                    start_all(stores(part, side, part))

                return carry

            lax.fori_loop(0, per_side * per_chunk, one, 0)
        wait_all(loads)
        wait_all(stores(0, 0, 0))

        def last(index, carry):
            some = pl.ds(pl.multiple_of(index * block, block), block)
            tile[0, some, :] = low(tn(att[:, some], branch[...]))
            return carry

        lax.fori_loop(0, width // block, last, 0)
        copies = []
        for side in range(2):
            o_cols = pl.ds(pl.multiple_of((core ^ side) * side_cols, 128), side_cols)
            copies += half_copies(
                me,
                tile.at[0, :, o_cols],
                targets,
                o_sems.at[side],
                side,
                by_chips,
                (0, side_cols),
            )
        start_all(copies)
        wait_all(stores(1, 0, 1))
        wait_all(copies)

    sums = jax.ShapeDtypeStruct
    bf16 = jnp.bfloat16
    if by_chips:
        line = lax.axis_size("fsdp") // 8
        shapes = [sums((4, line, width // (4 * line), packed), bf16)] * 2
    else:
        shapes = [sums((2, width, packed), bf16)]
    result = pl.pallas_call(
        kernel,
        out_shape=shapes + [TOKEN_SHAPE],
        in_specs=[IN_SMEM] + [IN_HBM] * (3 + count_att),
        out_specs=[IN_HBM] * len(shapes) + [IN_SMEM],
        scratch_shapes=[
            pltpu.VMEM((slots, width), bf16),
            pltpu.VMEM((slots, width), bf16),
            pltpu.VMEM((width, slots), bf16),
            pltpu.VMEM((strips, slots, chunk), bf16),
            pltpu.VMEM((2, width, chunk), bf16),
            pltpu.SemaphoreType.DMA((strips + 2 + count_att,)),
            pltpu.SemaphoreType.DMA((2, 16)),
            pltpu.SemaphoreType.DMA((2, 16)),
        ],
        compiler_params=pltpu.CompilerParams(vmem_limit_bytes=56 * MIB),
        cost_estimate=cost(2 * slots * width * (width + strips * chunk), 20 * MIB),
    )(place, branch, flipped, grad_pre, *attended)
    return result[:-1], result[-1]


def back_places(grads, side_cols):
    places, first = [], 0
    for number, some in enumerate(grads):
        for col in range(0, some[0].shape[1], 128):
            half, start = divmod(first + col, side_cols)
            places += [
                (3 * number + part, col, half, part * side_cols + start) for part in range(3)
            ]
        first += some[0].shape[1]
    return [grad for some in grads for grad in some], places


def put_columns(refs, places, parts, rows):
    for number, col, half, start in places:
        parts[half, :, start : start + 128] = refs[number][rows, col : col + 128]


def weights_back(place, normed_attn, grads, diagonals, by_chips, after=()):
    slots, width = normed_attn.shape
    side_cols = width // 2
    flat_grads, places = back_places(grads, side_cols)

    onehot = np.pad(
        (line_ids()[:, None] == np.arange(NB)[None, :]).astype(np.float32), ((0, 0), (0, 128 - NB))
    )
    pairs = len(diagonals)
    heads = sum(2 * some.shape[0] for some in diagonals)
    table_rows = -(-heads // 8) * 8

    def kernel(place_ref, normed_ref, onehot_ref, *refs):
        diag_refs, refs = refs[:pairs], refs[pairs:]
        g_refs = refs[: len(flat_grads)]
        refs = refs[len(flat_grads) + len(after) :]
        targets, (table_ref, token_ref, parts, tile) = refs[:-4], refs[-4:]
        token_ref[0, 0] = 0.0
        me = place_ref[0]
        core = me % 2
        put_columns(g_refs, places, parts, slice(None))
        rows = [
            ref[one, head : head + 1, :]
            for ref in diag_refs
            for one in range(ref.shape[0])
            for head in range(2)
        ]
        if table_rows > heads:
            rows.append(jnp.zeros((table_rows - heads, 2 * SEQ), jnp.float32))
        table_ref[...] = lax.dot_general(
            jnp.concatenate(rows, 0),
            onehot_ref[...],
            (((1,), (0,)), ((), ())),
            precision=lax.Precision.HIGHEST,
            preferred_element_type=jnp.float32,
        )
        for side in range(2):
            half = core ^ side
            for first in range(0, 3 * side_cols, 512):
                some = slice(first, min(first + 512, 3 * side_cols))
                tile[:, some] = low(tn(normed_ref[...], parts[half, :, some]))
            if not by_chips:
                targets[0][half] = tile[...]
                continue
            planes, line, rows = targets[side].shape[:3]
            for plane in range(planes):
                for hop in range(line):
                    start = pl.multiple_of(((me // 2) ^ (4 * hop + plane)) * rows, 16)
                    targets[side][plane, hop] = tile[pl.ds(start, rows), :]

    sums = jax.ShapeDtypeStruct
    if by_chips:
        line = lax.axis_size("fsdp") // 8
        shapes = [sums((4, line, width // (4 * line), 3 * side_cols), jnp.bfloat16)] * 2
    else:
        shapes = [sums((2, width, 3 * side_cols), jnp.bfloat16)]
    result = pl.pallas_call(
        kernel,
        out_shape=shapes + [sums((table_rows, 128), jnp.float32), TOKEN_SHAPE],
        in_specs=[IN_SMEM] + [IN_VMEM] * (2 + pairs + len(flat_grads)) + [IN_HBM] * len(after),
        out_specs=[IN_VMEM] * (len(shapes) + 1) + [IN_SMEM],
        scratch_shapes=[
            pltpu.VMEM((2, slots, 3 * side_cols), jnp.bfloat16),
            pltpu.VMEM((width, 3 * side_cols), jnp.bfloat16),
        ],
        compiler_params=pltpu.CompilerParams(vmem_limit_bytes=24 * MIB),
        cost_estimate=cost(6 * slots * width * width, 15 * MIB),
    )(place, normed_attn, jnp.asarray(onehot), *diagonals, *flat_grads, *after)
    return result[:-2], result[-2], result[-1]


def inputs_back(
    tokens, gains, branch, grads, weights, place, first, count, done=None, after=()
):
    slots, width = tokens.shape
    side_cols = width // 2
    flat_grads, places = back_places(grads, side_cols)
    block = 256
    held = () if done is None else (done,)

    def kernel(place_ref, x_ref, gains_ref, branch_ref, weights_ref, *refs):
        g_refs, refs = refs[: len(flat_grads)], refs[len(flat_grads) + len(after) + len(held) :]
        out_hbm, token_ref, parts, out, summed, out_sems = refs
        token_ref[0, 0] = 0.0
        core = place_ref[0] % 2
        gain = gains_ref[0:1, :]
        put_columns(g_refs, places, parts, slice(first, first + count))

        def back(index, carry):
            cols = pl.ds(pl.multiple_of(index * block, block), block)
            summed[:, cols] = nt(parts[core], weights_ref[0, cols, : 3 * side_cols]) + nt(
                parts[1 - core], weights_ref[1, cols, : 3 * side_cols]
            )
            return carry

        lax.fori_loop(0, width // block, back, 0)

        def finish(index, carry):
            here = pl.ds(pl.multiple_of(index * block, block), block)
            where = pl.ds(pl.multiple_of(first + index * block, block), block)
            rows = wide(x_ref[where, :])
            scale = norm_scale(rows)
            back = rms_back(rows * scale, scale, gain, summed[here, :])
            out[here, :] = low(wide(branch_ref[where, :]) + back)
            return carry

        lax.fori_loop(0, count // block, finish, 0)
        last = pltpu.make_async_copy(out, out_hbm.at[pl.ds(first, count)], out_sems.at[0])
        last.start()
        last.wait()

    bf16, f32 = jnp.bfloat16, jnp.float32
    return pl.pallas_call(
        kernel,
        out_shape=[jax.ShapeDtypeStruct((slots, width), bf16), TOKEN_SHAPE],
        in_specs=[IN_SMEM]
        + [IN_VMEM] * (4 + len(flat_grads))
        + [IN_HBM] * (len(after) + len(held)),
        out_specs=[IN_HBM, IN_SMEM],
        scratch_shapes=[
            pltpu.VMEM((2, count, 3 * side_cols), bf16),
            pltpu.VMEM((count, width), bf16),
            pltpu.VMEM((count, width), f32),
            pltpu.SemaphoreType.DMA((1,)),
        ],
        compiler_params=pltpu.CompilerParams(vmem_limit_bytes=20 * MIB),
        cost_estimate=cost(6 * count * width * width, 15 * MIB),
        input_output_aliases={5 + len(flat_grads) + len(after): 0} if held else {},
    )(place, tokens, gains, branch, weights, *flat_grads, *after, *held)


def pack_halves(place, gain_attn, gain_ffn, shards_qkv, shards_in):
    rows = shards_qkv[0].shape[0]
    groups = (shards_qkv, shards_in)
    counts = [sum(shard.shape[1] for shard in group) // 2 for group in groups]

    def kernel(place_ref, attn_ref, ffn_ref, *refs):
        ins, outs = refs[: -2 * len(groups)], refs[-2 * len(groups) :]
        core = place_ref[0] % 2
        first = 0
        for number, group in enumerate(groups):
            for other in range(2):
                out, col = outs[2 * number + other], 0
                for ref in ins[first : first + len(group)]:
                    half = ref.shape[1] // 2
                    start = pl.multiple_of((core ^ other) * half, 128)
                    out[:, col : col + half] = ref[:, pl.ds(start, half)]
                    col += half
            first += len(group)
        same = lax.broadcasted_iota(jnp.int32, (rows, rows), 0) == lax.broadcasted_iota(
            jnp.int32, (rows, rows), 1
        )
        lane = lax.broadcasted_iota(jnp.int32, (rows, 128), 1)
        cols = jnp.zeros((rows, 128), jnp.float32)
        for number, ref in enumerate((attn_ref, ffn_ref)):
            row = wide(ref[...])
            col = jnp.sum(jnp.where(same, row, 0.0), axis=1, keepdims=True)
            cols = jnp.where(lane == number, col, cols)
        for other in range(2):
            outs[other][:, counts[0] :] = low(cols)

    shapes = [
        jax.ShapeDtypeStruct((rows, count + extra), jnp.bfloat16)
        for count, extra in zip(counts, (128, 0))
        for _ in range(2)
    ]
    return pl.pallas_call(
        kernel,
        out_shape=shapes,
        in_specs=[IN_SMEM] + [IN_VMEM] * (2 + len(shards_qkv) + len(shards_in)),
        out_specs=[IN_VMEM] * len(shapes),
    )(place, gain_attn, gain_ffn, *shards_qkv, *shards_in)


def prepare(compute, operands, shapes, after=(), place=None, pair=()):
    scalars = [] if place is None else [place]

    def kernel(*refs):
        refs = list(refs)
        where = [ref[0] for ref in refs[: len(scalars)]]
        ins, refs = refs[len(scalars) :][: len(operands)], refs[len(scalars) + len(operands) :]
        outs = refs[len(pair) + len(after) :]
        outs[-1][0, 0] = 0.0
        if pair:
            outs[-2][...] = refs[0][...] + refs[1][...]
        compute(*where, ins, outs)

    result = pl.pallas_call(
        kernel,
        out_shape=list(shapes) + [like(array, *array.shape) for array in pair[:1]] + [TOKEN_SHAPE],
        in_specs=[IN_SMEM] * len(scalars)
        + [IN_VMEM] * (len(operands) + len(pair))
        + [IN_HBM] * len(after),
        out_specs=[IN_VMEM] * (len(shapes) + len(pair[:1])) + [IN_SMEM],
        compiler_params=pltpu.CompilerParams(vmem_limit_bytes=8 * MIB),
        cost_estimate=cost(0, sum(2 * array.size for array in operands)),
    )(*scalars, *operands, *pair, *after)
    return result[:-1], result[-1]


def like(array, *shape):
    return jax.ShapeDtypeStruct(shape, array.dtype)


def chip_unit(place, mine, got, after=()):
    def compute(me, ins, outs):
        first = me % 2 == 0
        own, other = wide(ins[0][...]), wide(ins[1][...])
        outs[0][...] = low(
            jnp.concatenate([jnp.where(first, own, other), jnp.where(first, other, own)], 0)
        )

    shape = like(mine, 2 * mine.shape[0], mine.shape[1])
    (unit,), token = prepare(compute, [mine, got], [shape], after, place)
    return unit, token


def stack_and_unit(place, parts, mine, got, after=()):
    def compute(me, ins, outs):
        for number in range(len(parts)):
            outs[0][number] = ins[number][...]
        first = me % 2 == 0
        own, other = wide(ins[-2][...]), wide(ins[-1][...])
        outs[1][...] = low(
            jnp.concatenate([jnp.where(first, own, other), jnp.where(first, other, own)], 0)
        )

    shapes = [
        like(parts[0], len(parts), *parts[0].shape),
        like(mine, 2 * mine.shape[0], mine.shape[1]),
    ]
    operands = list(tuple(parts) + (mine, got))
    return prepare(compute, operands, shapes, after, place)


def stack_and_copies(parts, arrays, after=()):
    def compute(ins, outs):
        for number in range(len(parts)):
            outs[0][number] = ins[number][...]
        for number in range(len(arrays)):
            outs[1 + number][...] = ins[len(parts) + number][...]

    shapes = [like(parts[0], len(parts), *parts[0].shape)]
    shapes += [like(array, *array.shape) for array in arrays]
    return prepare(compute, [*parts, *arrays], shapes, after)


def copied(arrays, after=()):
    def compute(ins, outs):
        for number in range(len(arrays)):
            outs[number][...] = ins[number][...]

    shapes = [like(array, *array.shape) for array in arrays]
    return prepare(compute, list(arrays), shapes, after)


def far_and_copies(over_x, over_y, arrays, after=()):
    half = over_x.shape[0] // 2

    def compute(ins, outs):
        outs[0][...] = ins[0][:half]
        outs[1][...] = ins[1][half:]
        for number in range(len(arrays)):
            outs[2 + number][...] = ins[2 + number][...]

    shapes = [like(over_x, half, *over_x.shape[1:])] * 2
    shapes += [like(array, *array.shape) for array in arrays]
    return prepare(compute, [over_y, over_x, *arrays], shapes, after)


def first_sends(keep, got, after=(), pair=()):
    places = ((3, 0), (1, 0), (3, 1), (2, 1))
    half = keep.shape[1] // 2

    def compute(ins, outs):
        for number, (plane, late) in enumerate(places):
            for hop in range(half):
                at = late * half + hop
                outs[number // 2][number % 2, hop] = low(
                    wide(ins[0][plane, at]) + wide(ins[1][plane, at])
                )

    shapes = [like(keep, 2, half, *keep.shape[2:])] * 2
    return prepare(compute, [keep, got], shapes, after, pair=pair)


def second_sends(keep, got, first, after=(), pair=()):
    half = keep.shape[1] // 2

    def compute(ins, outs):
        for number, (plane, late) in enumerate(((2, 0), (1, 1))):
            for hop in range(half):
                at = late * half + hop
                outs[number][hop] = low(
                    wide(ins[0][plane, at])
                    + wide(ins[1][plane, at])
                    + wide(ins[2 + number][0, hop])
                )

    shapes = [like(keep, half, *keep.shape[2:])] * 2
    return prepare(compute, [keep, got, *first], shapes, after, pair=pair)


def line_sums(keep, got, first, second, after=(), pair=()):
    line = keep.shape[1]
    half = line // 2

    def compute(ins, outs):
        for at in range(line):
            direct, merged = ins[2 + at // half], ins[4 + at // half]
            total = wide(ins[0][0, at]) + wide(ins[1][0, at]) + wide(direct[1, at % half])
            outs[at][...] = low(total + wide(merged[at % half]))

    operands = [keep, got, *first, *second]
    return prepare(compute, operands, [like(keep, *keep.shape[2:])] * line, after, pair=pair)


def chip_sum_halves(place, terms, copied=(), after=(), pair=()):
    rows, cols = terms[0].shape

    def compute(me, ins, outs):
        total = add(*[ref[...] for ref in ins[: len(terms)]])
        first = me % 2 == 0
        upper, lower = total[: rows // 2], total[rows // 2 :]
        outs[0][...] = jnp.where(first, upper, lower)
        outs[1][...] = jnp.where(first, lower, upper)
        for number in range(len(copied)):
            outs[2 + number][...] = ins[len(terms) + number][...]

    shape = jax.ShapeDtypeStruct((rows // 2, cols), jnp.float32)
    shapes = [shape, shape] + [like(array, *array.shape) for array in copied]
    operands = list(tuple(terms) + tuple(copied))
    return prepare(compute, operands, shapes, after, place, pair=pair)


def join_halves(place, mine, other, parts, factor, gain, weights, after=()):
    rows = mine.shape[0]
    skipped = len(parts) - len(weights)

    def compute(me, ins, outs):
        core = me % 2
        first = 0
        for count, out in zip(parts, outs):
            for ref, half in ((ins[0], core), (ins[1], 1 - core)):
                start = pl.multiple_of(half * count, 128)
                out[:, pl.ds(start, count)] = ref[:, first : first + count] * factor
            first += count
        total = jnp.zeros((rows, 1), jnp.float32)
        for number, weight in enumerate(ins[3:]):
            product = wide(weight[...]) * outs[skipped + number][...]
            total = total + jnp.sum(product, axis=1, keepdims=True)
        same = lax.broadcasted_iota(jnp.int32, (rows, rows), 0) == lax.broadcasted_iota(
            jnp.int32, (rows, rows), 1
        )
        column = jnp.sum(jnp.where(same, wide(ins[2][...]), 0.0), axis=1, keepdims=True)
        outs[len(parts)][...] = jnp.broadcast_to(total / column, (rows, 128))

    shapes = [jax.ShapeDtypeStruct((rows, 2 * count), jnp.float32) for count in parts]
    shapes.append(jax.ShapeDtypeStruct((rows, 128), jnp.float32))
    operands = list((mine, other, gain[None]) + tuple(weights))
    return prepare(compute, operands, shapes, after, place)[0]


def gather_plain(shards):
    full = [lax.all_gather(shard, "fsdp", axis=0, tiled=True) for shard in shards]
    gain_attn, w_query, w_key, w_value, w_attn_out, gain_ffn, w_ffn_in, w_ffn_out = full
    gains = jnp.pad(jnp.stack([gain_attn, gain_ffn], 1), ((0, 0), (0, 126)))
    return (
        (halves_of(w_query, w_key, w_value, jnp.concatenate([gains, gains], 1)),),
        (halves_of(w_attn_out, w_ffn_in),),
        (w_ffn_out,),
    )


def gain_back(gain, weights, grads):
    return sum(
        jnp.sum(weight.astype(jnp.float32) * grad, axis=1) for weight, grad in zip(weights, grads)
    ) / gain.astype(jnp.float32)


def per_device(
    tokens,
    lengths,
    gain_attn,
    w_query,
    w_key,
    w_value,
    w_attn_out,
    gain_ffn,
    w_ffn_in,
    w_ffn_out,
    bucket_bias_matrix,
    cotangent,
):
    slot_count, width = tokens.shape
    heads = bucket_bias_matrix.shape[1]
    devices = lax.axis_size("fsdp")
    factor = 1.0 / math.sqrt(slot_count * devices)
    place = lax.axis_index("fsdp").astype(jnp.int32)[None]
    side = width // 2
    by_chips = devices == 32
    pairs = heads // 2
    attended, probs, backs = [], [], []

    def pairs_of(arrays):
        return sum(array.shape[1] for array in arrays) * heads // (2 * width)

    def forward(count, after=()):
        out, prob, token = attend(lengths, qkv, planes, pairs_of(attended), count, after)
        attended.append(out)
        probs.append(prob)
        return token

    def backward(after=()):
        number = len(backs)
        first, count = pairs_of(attended[:number]), pairs_of(attended[number : number + 1])
        result = attend_back(qkv, grad_attended, probs[number], first, count, heads, after)
        backs.append(result[:4])
        return result[4]

    def weights(after=()):
        grads, diagonals = [some[:3] for some in backs], [some[3] for some in backs]
        return weights_back(place, normed_attn, grads, diagonals, by_chips, after)

    def inputs(first, count, done=None, after=()):
        grads = [some[:3] for some in backs]
        return inputs_back(
            tokens, gains, saved[0], grads, weights_qkv, place, first, count, done, after
        )

    if by_chips:
        mine_qkv, for_qkv, mine_in, for_in = pack_halves(
            place,
            gain_attn[None],
            gain_ffn[None],
            (w_query, w_key, w_value),
            (w_attn_out, w_ffn_in),
        )
        unit, token = chip_unit(place, mine_qkv, swap(for_qkv, 1))
        line = gather_line(unit)
        planes, token = bias_planes(bucket_bias_matrix, (token,))

        (near_qkv, unit), token = stack_and_copies(line, (w_ffn_out,), (token,))
        plane_qkv = gather_plane(near_qkv)
        line = gather_line(unit)

        parts, token = far_and_copies(*plane_qkv, (near_qkv,) + plane_qkv, line + (token,))
        far_qkv = gather_far(*parts[:2])
        other_qkv = tuple(swap(part, 1) for part in parts[2:])

        (near_out, unit), token = stack_and_unit(
            place, line, mine_in, swap(for_in, 1), far_qkv + other_qkv + (token,)
        )
        plane_out = gather_plane(near_out)
        other_qkv = other_qkv + (swap(far_qkv[0], 1), swap(far_qkv[1], 1))
        in_qkv = (near_qkv,) + plane_qkv + far_qkv + other_qkv
        qkv, normed_attn, weights_qkv, gains, token = project_qkv(
            place, tokens, in_qkv, by_chips, (planes, token)
        )

        parts, token = far_and_copies(*plane_out, (unit,), (token,))
        far_out = gather_far(*parts[:2])
        line = gather_line(parts[2])
        token = forward(2, (token,))

        parts, token = stack_and_copies(line, (near_out,) + plane_out, far_out + (token,))
        near_in = parts[0]
        plane_in = gather_plane(near_in)
        other_out = tuple(swap(part, 1) for part in parts[1:])
        token = forward(1, (token,))

        parts, token = far_and_copies(*plane_in, far_out + (near_in,), other_out + (token,))
        far_in = gather_far(*parts[:2])
        other_out = other_out + (swap(parts[2], 1), swap(parts[3], 1))
        other_in = (swap(parts[4], 1),)
        token = forward(2, (token,))

        parts, token = copied(plane_in + far_in, other_in + other_out[3:] + (token,))
        other_in = other_in + tuple(swap(part, 1) for part in parts)
        token = forward(1, (token,))

        in_ffn = (near_in,) + plane_in + far_in + other_in
        in_out = (near_out,) + plane_out + far_out + other_out
    else:
        planes, _ = bias_planes(bucket_bias_matrix)
        in_qkv, in_ffn, in_out = gather_plain(
            (gain_attn, w_query, w_key, w_value, w_attn_out, gain_ffn, w_ffn_in, w_ffn_out)
        )
        qkv, normed_attn, weights_qkv, gains, _ = project_qkv(place, tokens, in_qkv, by_chips)
        for _ in range(pairs):
            forward(1)

    output, grad_attended, saved, part_out = feed_forward(
        place, tokens, attended, cotangent, gains, in_ffn, in_out, by_chips
    )

    if by_chips:
        keep_out, send_out = part_out
        got_out = swap(send_out, 1)
        (keep_in, send_in), token = in_weights_back(place, attended, *saved, by_chips)

        sends, token = first_sends(keep_out, got_out, (token,))
        first_out = scatter_first(sends)
        got_in = swap(send_in, 1)
        token = backward((token,))

        sends, token = second_sends(keep_out, got_out, first_out, (got_in, token))
        second_out = scatter_second(sends)
        token = backward((token,))

        sums, token = line_sums(keep_out, got_out, first_out, second_out, (token,))
        last_out = scatter_line(sums)
        sends, token = first_sends(keep_in, got_in, (token,))
        first_in = scatter_first(sends)
        token = backward((token,))

        sends, token = second_sends(keep_in, got_in, first_in, last_out + (token,))
        second_in = scatter_second(sends)
        token = backward((token,))

        sums, token = line_sums(keep_in, got_in, first_in, second_in, (token,))
        last_in = scatter_line(sums)
        (keep_qkv, send_qkv), table, token = weights(last_out + (token,))

        parts, token = chip_sum_halves(place, last_in, (send_qkv, table), (token,))
        mine_in, for_in, send_qkv, table = parts
        got_qkv, got_in, got = swap(send_qkv, 1), swap(for_in, 1), swap(table, 1)
        grad_tokens, token = inputs(0, slot_count // 2, None, (token,))

        parts, token = first_sends(keep_qkv, got_qkv, (got_in, token), (table, got))
        first_qkv = scatter_first(parts[:2])
        table, got = parts[2], swap(parts[2], 2)
        grad_tokens, token = inputs(slot_count // 2, slot_count // 2, grad_tokens, (token,))

        parts, token = second_sends(keep_qkv, got_qkv, first_qkv, (token,), (table, got))
        second_qkv = scatter_second(parts[:2])
        table, got = parts[2], swap(parts[2], 4)
        sum_out = add(*last_out) * factor

        parts, token = line_sums(
            keep_qkv, got_qkv, first_qkv, second_qkv, (token,), (table, got)
        )
        last_qkv = scatter_line(parts[:-1])
        table, got = parts[-1], swap(parts[-1], 8)
        sum_o, sum_in, grad_gain_ffn = join_halves(
            place,
            mine_in,
            got_in,
            (side, keep_in.shape[-1] - side),
            factor,
            gain_ffn,
            (w_ffn_in,),
            (token,),
        )

        parts, token = chip_sum_halves(place, last_qkv, (), (token,), (table, got))
        mine_qkv, for_qkv, table = parts
        got_qkv, got = swap(for_qkv, 1), swap(table, 16)
        table = table + got
        sum_q, sum_k, sum_v, grad_gain_attn = join_halves(
            place,
            mine_qkv,
            got_qkv,
            (side, side, side),
            factor,
            gain_attn,
            (w_query, w_key, w_value),
        )
        grad_gain_attn, grad_gain_ffn = grad_gain_attn[:, 0], grad_gain_ffn[:, 0]
        sums = (sum_q, sum_k, sum_v, sum_o, sum_in, sum_out)
    else:
        for _ in range(pairs):
            backward()
        part_in, _ = in_weights_back(place, attended, *saved, by_chips)
        part_qkv, table, _ = weights()
        grad_tokens, _ = inputs(0, slot_count)
        sums = sum_plain(
            jnp.concatenate([part_qkv[0], part_in[0][:, :, :side]], 2),
            part_in[0][:, :, side:],
            part_out[0],
        )
        sums = [total * factor for total in sums]
        table = lax.psum(table, "fsdp")
        grad_gain_attn = gain_back(gain_attn, (w_query, w_key, w_value), sums[:3])
        grad_gain_ffn = gain_back(gain_ffn, (w_ffn_in,), sums[4:5])

    return (
        output,
        grad_tokens,
        grad_gain_attn,
        sums[0],
        sums[1],
        sums[2],
        sums[3],
        grad_gain_ffn,
        sums[4],
        sums[5],
        table[:heads, :NB].T * factor,
    )


def solution(mesh):
    placed = (
        P("fsdp", None),
        P("fsdp", None),
        P("fsdp"),
        P("fsdp", None),
        P("fsdp", None),
        P("fsdp", None),
        P("fsdp", None),
        P("fsdp"),
        P("fsdp", None),
        P("fsdp", None),
        P(),
        P("fsdp", None),
    )
    return jax.shard_map(
        per_device,
        mesh=mesh,
        in_specs=placed,
        out_specs=(
            P("fsdp", None),
            P("fsdp", None),
            P("fsdp"),
            P("fsdp", None),
            P("fsdp", None),
            P("fsdp", None),
            P("fsdp", None),
            P("fsdp"),
            P("fsdp", None),
            P("fsdp", None),
            P(),
        ),
        check_vma=False,
    )
```

```python
import functools
import math

import jax
import jax.numpy as jnp
import numpy as np
from jax import lax
from jax.experimental import pallas as pl
from jax.experimental.pallas import tpu as pltpu
from jax.sharding import PartitionSpec as P

NB = 32
MAXD = 128
SEQ = 512
MIB = 1024 * 1024


def bucket_ids(span_length):
    offset = np.arange(span_length)[None, :] - np.arange(span_length)[:, None]
    half_count = NB // 2
    exact_count = half_count // 2
    result = np.where(offset > 0, half_count, 0)
    distance = np.abs(offset)
    spread = exact_count + np.floor(
        np.log(np.maximum(distance, 1) / exact_count)
        / math.log(MAXD / exact_count)
        * (half_count - exact_count)
    )
    spread = np.minimum(spread, half_count - 1)
    result = result + np.where(distance < exact_count, distance, spread)
    return result.astype(np.int32)


def flip(mask, count):
    return [(i, i ^ mask) for i in range(count)]


def swap(array, mask):
    return lax.ppermute(array, "fsdp", flip(mask, lax.axis_size("fsdp")))


def gather_line(unit):
    line = lax.axis_size("fsdp") // 8
    return (unit,) + tuple(swap(unit, 8 * hop) for hop in range(1, line))


def gather_plane(near):
    return swap(near, 2), swap(near, 4)


def gather_far(first, second):
    return swap(first, 2), swap(second, 4)


def chip_distances():
    line = lax.axis_size("fsdp") // 8
    half = line // 2
    blocks = []
    for part, (plane, first, last) in enumerate(
        ((0, 0, line), (1, 0, line), (2, 0, line), (3, 0, half), (3, half, line))
    ):
        blocks += [(part, hop - first, 4 * hop + plane) for hop in range(first, last)]
    return blocks


def add(*terms):
    return sum(term.astype(jnp.float32) for term in terms)


def scatter_first(sends):
    return swap(sends[0], 2), swap(sends[1], 4)


def scatter_second(sends):
    return swap(sends[0], 4), swap(sends[1], 2)


def scatter_line(sums):
    return (sums[0],) + tuple(swap(total, 8 * hop) for hop, total in enumerate(sums) if hop)


def halves_of(*arrays):
    return jnp.stack(
        [
            jnp.concatenate(
                [
                    array[:, part * array.shape[1] // 2 : (part + 1) * array.shape[1] // 2]
                    for array in arrays
                ],
                1,
            )
            for part in range(2)
        ]
    )


def sum_plain(half_attn, half_in, grad_out):
    side = half_attn.shape[-1] // 4

    def owned(array):
        return lax.psum_scatter(
            array.astype(jnp.float32), "fsdp", scatter_dimension=0, tiled=True
        )

    grads = [
        jnp.concatenate([part[0], part[1]], 1)
        for part in [half_attn[:, :, k * side : (k + 1) * side] for k in range(4)] + [half_in]
    ]
    return [owned(grad) for grad in grads + [grad_out]]


def nn(left, right):
    return lax.dot_general(
        left, right, (((1,), (0,)), ((), ())), preferred_element_type=jnp.float32
    )


def nt(left, right):
    return lax.dot_general(
        left, right, (((1,), (1,)), ((), ())), preferred_element_type=jnp.float32
    )


def tn(left, right):
    return lax.dot_general(
        left, right, (((0,), (0,)), ((), ())), preferred_element_type=jnp.float32
    )


def low(value):
    return value.astype(jnp.bfloat16)


def wide(value):
    return value.astype(jnp.float32)


def norm_scale(values):
    return lax.rsqrt(jnp.mean(values * values, axis=-1, keepdims=True) + 1e-06)


def rms_back(scaled, scale, gain, grad_normed):
    weighted = grad_normed * gain
    return scale * (weighted - scaled * jnp.mean(weighted * scaled, axis=-1, keepdims=True))


IN_HBM = pl.BlockSpec(memory_space=pl.ANY)
ONLY_HBM = pl.BlockSpec(memory_space=pltpu.HBM)
IN_SMEM = pl.BlockSpec(memory_space=pltpu.SMEM)
IN_VMEM = pl.BlockSpec(memory_space=pltpu.VMEM)
TOKEN_SHAPE = jax.ShapeDtypeStruct((1, 1), jnp.float32)
TOKEN = pl.BlockSpec((1, 1), lambda *_: (0, 0), memory_space=pltpu.SMEM)


def cost(flops, bytes_moved):
    return pl.CostEstimate(flops=flops, bytes_accessed=bytes_moved, transcendentals=0)


def plan(me, rows, by_chips, side, per_core):
    chip, core = me // 2, me % 2
    if not by_chips:
        return []
    count = 5
    found = []
    for part, index, distance in chip_distances():
        number = chip ^ distance
        if per_core:
            number = number * 2 + (core ^ side)
        found.append((side * count + part, index, pl.multiple_of(number * rows, 16)))
    return found


def column_copies(me, sources, target, sems, side, by_chips, columns):
    first, last = columns
    if not by_chips:
        half = (me % 2) ^ side
        return [
            pltpu.make_async_copy(sources[0].at[half, :, pl.ds(first, last - first)], target, sems.at[0])
        ]
    rows = sources[0].shape[1]
    return [
        pltpu.make_async_copy(
            sources[part].at[index, :, pl.ds(first, last - first)],
            target.at[pl.ds(start, rows), :],
            sems.at[number],
        )
        for number, (part, index, start) in enumerate(plan(me, rows, True, side, False))
    ]


def row_copies(me, sources, target, sems, side, by_chips):
    if not by_chips:
        half = target.shape[0] // 2
        where = pl.ds(side * half, half)
        return [pltpu.make_async_copy(sources[0].at[where, :], target.at[where, :], sems.at[0])]
    rows = sources[0].shape[1]
    return [
        pltpu.make_async_copy(
            sources[part].at[index], target.at[pl.ds(start, rows), :], sems.at[number]
        )
        for number, (part, index, start) in enumerate(plan(me, rows, True, side, True))
    ]


def start_all(copies):
    for copy in copies:
        copy.start()


def wait_all(copies):
    for copy in copies:
        copy.wait()


def half_copies(me, tile, targets, sems, side, by_chips, columns):
    first, count = columns
    if not by_chips:
        half = (me % 2) ^ side
        return [
            pltpu.make_async_copy(tile, targets[0].at[half, :, pl.ds(first, count)], sems.at[0])
        ]
    planes, line, rows = targets[side].shape[:3]
    chip = me // 2
    return [
        pltpu.make_async_copy(
            tile.at[pl.ds(pl.multiple_of((chip ^ (4 * hop + plane)) * rows, 16), rows), :],
            targets[side].at[plane, hop, :, pl.ds(first, count)],
            sems.at[plane * line + hop],
        )
        for plane in range(planes)
        for hop in range(line)
    ]


def strip_copies(me, tile, targets, sems, strip, by_chips):
    if not by_chips:
        rows = tile.shape[0]
        return [
            pltpu.make_async_copy(
                tile, targets[0].at[pl.ds(pl.multiple_of(strip * rows, 16), rows), :], sems.at[0]
            )
        ]
    planes, line, rows = targets[0].shape[:3]
    chip, core = me // 2, me % 2
    return [
        pltpu.make_async_copy(
            tile.at[
                pl.ds(pl.multiple_of((((chip % 4) ^ plane) * 2 + (core ^ side)) * rows, 16), rows), :
            ],
            targets[side].at[plane, (chip // 4) ^ strip],
            sems.at[side * planes + plane],
        )
        for side in range(2)
        for plane in range(planes)
    ]


def bias_planes(table, after=()):
    heads = table.shape[1]
    ids = bucket_ids(SEQ)
    flat = np.concatenate([ids[:, 0], ids[0, :1], ids[0, :0:-1]])
    onehot = (np.arange(table.shape[0])[:, None] == flat[None, :]).astype(np.float32)

    def kernel(table_ref, onehot_ref, *refs):
        plane_ref, token_ref, rows = refs[len(after) :]
        token_ref[0, 0] = 0.0
        head = pl.program_id(0)

        @pl.when(head == 0)
        def _():
            rows[:heads] = lax.dot_general(
                wide(table_ref[...]),
                onehot_ref[...],
                (((0,), (0,)), ((), ())),
                precision=lax.Precision.HIGHEST,
                preferred_element_type=jnp.float32,
            )

        spread = jnp.broadcast_to(rows[pl.ds(head, 1), :], (SEQ, 2 * SEQ))
        moved = pltpu.roll(spread, 0, 1, stride=1, stride_axis=0)
        plane_ref[0] = low(moved[:, :SEQ])

    return pl.pallas_call(
        kernel,
        grid=(heads,),
        out_shape=[jax.ShapeDtypeStruct((heads, SEQ, SEQ), jnp.bfloat16), TOKEN_SHAPE],
        in_specs=[IN_VMEM, IN_VMEM] + [IN_HBM] * len(after),
        out_specs=[pl.BlockSpec((1, SEQ, SEQ), lambda head: (head, 0, 0)), TOKEN],
        scratch_shapes=[pltpu.VMEM((-(-heads // 8) * 8, 2 * SEQ), jnp.float32)],
        compiler_params=pltpu.CompilerParams(vmem_limit_bytes=16 * MIB),
    )(table, jnp.asarray(onehot), *after)


def line_ids():
    ids = bucket_ids(SEQ)
    ahead = (np.arange(2 * SEQ) - (SEQ - 128) + SEQ) % (2 * SEQ) - SEQ
    return np.where(ahead >= 0, ids[np.maximum(ahead, 0), 0], ids[0, np.minimum(-ahead, SEQ - 1)])


def project_qkv(place, tokens, sources, by_chips, after=()):
    slots, width = tokens.shape
    side_cols = width // 2
    packed = sources[0].shape[-1]
    block = 256

    def kernel(place_ref, x_ref, *refs):
        ins, refs = refs[: len(sources)], refs[len(sources) + len(after) :]
        out_ref, normed_hbm, weights_hbm, gains_ref, token_ref, normed_ref, weights, sems = refs
        token_ref[0, 0] = 0.0
        me = place_ref[0]
        core = me % 2

        def put(side):
            if not by_chips:
                weights[side] = ins[0][(me % 2) ^ side]
                return
            rows = ins[0].shape[1]
            for part, index, start in plan(me, rows, True, side, False):
                weights[side, pl.ds(start, rows), :] = ins[part][index]

        put(0)
        gains = jnp.transpose(wide(weights[0, :, 3 * side_cols :]))
        gains_ref[...] = gains[:8]

        def normalise(index, carry):
            where = pl.ds(pl.multiple_of(index * block, block), block)
            rows = wide(x_ref[where, :])
            normed_ref[where, :] = low(rows * norm_scale(rows) * gains_ref[0:1, :])
            return carry

        lax.fori_loop(0, slots // block, normalise, 0)
        put(1)
        stores = [
            pltpu.make_async_copy(normed_ref, normed_hbm, sems.at[0]),
            pltpu.make_async_copy(weights, weights_hbm, sems.at[1]),
        ]
        start_all(stores)

        def one(index, carry):
            side, part = index // 3, index % 3
            here = pl.ds(pl.multiple_of(part * side_cols, 128), side_cols)
            cols = pl.ds(pl.multiple_of((core ^ side) * side_cols, 128), side_cols)
            out_ref[part, :, cols] = low(nn(normed_ref[...], weights[side, :, here]))
            return carry

        lax.fori_loop(0, 6, one, 0)
        wait_all(stores)

    sums = jax.ShapeDtypeStruct
    return pl.pallas_call(
        kernel,
        out_shape=[
            sums((3, slots, width), jnp.bfloat16),
            sums((slots, width), jnp.bfloat16),
            sums((2, width, packed), jnp.bfloat16),
            sums((8, width), jnp.float32),
            TOKEN_SHAPE,
        ],
        in_specs=[IN_SMEM] + [IN_VMEM] * (1 + len(sources)) + [IN_HBM] * len(after),
        out_specs=[IN_VMEM, ONLY_HBM, ONLY_HBM, IN_VMEM, IN_SMEM],
        scratch_shapes=[
            pltpu.VMEM((slots, width), jnp.bfloat16),
            pltpu.VMEM((2, width, packed), jnp.bfloat16),
            pltpu.SemaphoreType.DMA((2,)),
        ],
        compiler_params=pltpu.CompilerParams(vmem_limit_bytes=24 * MIB),
        cost_estimate=cost(6 * slots * width * width, 12 * slots * width),
    )(place, tokens, *sources, *after)


def attend(lengths, qkv, planes, first, count, after=()):
    _, slots, width = qkv.shape
    seqs = slots // SEQ
    heads = planes.shape[0]
    pair_cols = 2 * width // heads
    head_size = pair_cols // 2

    def kernel(lengths_ref, qkv_ref, planes_ref, *refs):
        q, k, v = (qkv_ref.at[part] for part in range(3))
        out, prob, token_ref, scores = refs[len(after) :]
        token_ref[0, 0] = 0.0

        own_lane = lax.broadcasted_iota(jnp.int32, (1, pair_cols), 1) < head_size
        key_number = lax.broadcasted_iota(jnp.int32, (SEQ, 1), 0)
        zero = jnp.zeros((), jnp.bfloat16)

        def both_heads(rows):
            return jnp.concatenate(
                [jnp.where(own_lane, rows, zero), jnp.where(own_lane, zero, rows)], 0
            )

        def one(step, carry):
            pair, seq = step // seqs, step % seqs
            rows = pl.ds(pl.multiple_of(seq * SEQ, SEQ), SEQ)
            own = pl.ds(pl.multiple_of(pair * pair_cols, pair_cols), pair_cols)
            lanes = pl.ds(pl.multiple_of((first + pair) * pair_cols, pair_cols), pair_cols)

            permitted = key_number < lengths_ref[seq, 0] + lengths_ref[seq, 1]
            scores[...] = nt(both_heads(k[rows, lanes]), q[rows, lanes])
            for head in range(2):
                these = scores[head * SEQ : (head + 1) * SEQ, :] + wide(planes_ref[2 * (first + pair) + head])
                these = jnp.where(permitted, these, -1e30)
                raised = jnp.exp(these - jnp.max(these, axis=0, keepdims=True))
                total = jnp.sum(raised, axis=0, keepdims=True)
                prob[seq, 2 * pair + head] = low(raised * (1.0 / total))
            both = prob[seq, pl.ds(2 * pair, 2)].reshape(2 * SEQ, SEQ)
            mixed = tn(both, both_heads(v[rows, lanes]))
            out[rows, own] = low(mixed)
            return carry

        lax.fori_loop(0, count * seqs, one, 0)

    return pl.pallas_call(
        kernel,
        out_shape=[
            jax.ShapeDtypeStruct((slots, count * pair_cols), jnp.bfloat16),
            jax.ShapeDtypeStruct((seqs, 2 * count, SEQ, SEQ), jnp.bfloat16),
            TOKEN_SHAPE,
        ],
        in_specs=[IN_SMEM] + [IN_VMEM] * 2 + [IN_HBM] * len(after),
        out_specs=[IN_VMEM, IN_VMEM, IN_SMEM],
        scratch_shapes=[
            pltpu.VMEM((2 * SEQ, SEQ), jnp.float32),
        ],
        compiler_params=pltpu.CompilerParams(vmem_limit_bytes=12 * MIB),
        cost_estimate=cost(count * slots * SEQ * 2048, count * slots * SEQ * 8),
    )(lengths, qkv, planes, *after)


def attend_back(qkv, grad_mixed, prob, first, count, heads, after=()):
    _, slots, width = qkv.shape
    seqs = slots // SEQ
    pair_cols = 2 * width // heads
    head_size = pair_cols // 2
    steps = count * seqs

    def kernel(qkv_ref, g, prob_ref, *refs):
        q, k, v = (qkv_ref.at[part] for part in range(3))
        dq, dk, dv, table_ref, token_ref, grads, scored, planes = refs[len(after) :]
        token_ref[0, 0] = 0.0

        own_lane = lax.broadcasted_iota(jnp.int32, (1, pair_cols), 1) < head_size
        zero = jnp.zeros((), jnp.bfloat16)

        def both_heads(rows):
            return jnp.concatenate(
                [jnp.where(own_lane, rows, zero), jnp.where(own_lane, zero, rows)], 0
            )

        def one(step, carry):
            pair, seq = step // seqs, step % seqs
            prob = prob_ref.at[seq, pl.ds(2 * pair, 2)]
            rows = pl.ds(pl.multiple_of(seq * SEQ, SEQ), SEQ)
            own = pl.ds(pl.multiple_of(pair * pair_cols, pair_cols), pair_cols)
            lanes = pl.ds(pl.multiple_of((first + pair) * pair_cols, pair_cols), pair_cols)

            grads[...] = nt(both_heads(v[rows, lanes]), g[rows, lanes])
            summed = nn(prob[...].reshape(2 * SEQ, SEQ), g[rows, lanes])
            dv[rows, own] = low(jnp.where(own_lane, summed[:SEQ], summed[SEQ:]))
            keep = jnp.where(seq == 0, 0.0, 1.0)
            for head in range(2):
                there = slice(head * SEQ, (head + 1) * SEQ)
                weights = wide(prob[head])
                weighted = weights * grads[there, :]
                dot = jnp.sum(weighted, axis=0, keepdims=True)
                grad_scores = weighted - weights * dot
                planes[head] = planes[head] * keep + grad_scores
                scored[there, :] = low(grad_scores)
            summed = nn(scored[...], q[rows, lanes])
            dk[rows, own] = low(jnp.where(own_lane, summed[:SEQ], summed[SEQ:]))
            dq[rows, own] = low(tn(scored[...], both_heads(k[rows, lanes])))

            @pl.when(seq == seqs - 1)
            def _():
                for head in range(2):
                    lined = jnp.zeros((8, 2 * SEQ), jnp.float32)
                    for low_row in range(0, 128, 8):
                        frame = jnp.zeros((8, 2 * SEQ), jnp.float32)
                        for high_row in range(0, SEQ, 128):
                            some = planes[head, high_row + low_row : high_row + low_row + 8, :]
                            ahead = SEQ - 128 - high_row
                            filled = [some, jnp.zeros((8, SEQ - ahead), jnp.float32)]
                            if ahead:
                                filled = [jnp.zeros((8, ahead), jnp.float32)] + filled
                            frame = frame + jnp.concatenate(filled, 1)
                        if low_row:
                            frame = pltpu.roll(frame, 2 * SEQ - low_row, 1)
                        lined = lined + frame
                    moved = lined[:1]
                    for row in range(1, 8):
                        moved = moved + pltpu.roll(lined[row : row + 1], 2 * SEQ - row, 1)
                    table_ref[pair, head : head + 1, :] = moved

            return carry

        planes[...] = jnp.zeros_like(planes)
        lax.fori_loop(0, steps, one, 0)

    result = jax.ShapeDtypeStruct((slots, count * pair_cols), jnp.bfloat16)
    return pl.pallas_call(
        kernel,
        in_specs=[IN_VMEM] * 3 + [IN_HBM] * len(after),
        out_specs=[IN_VMEM] * 4 + [IN_SMEM],
        out_shape=[result] * 3
        + [jax.ShapeDtypeStruct((count, 8, 2 * SEQ), jnp.float32), TOKEN_SHAPE],
        scratch_shapes=[
            pltpu.VMEM((2 * SEQ, SEQ), jnp.float32),
            pltpu.VMEM((2 * SEQ, SEQ), jnp.bfloat16),
            pltpu.VMEM((2, SEQ, SEQ), jnp.float32),
        ],
        compiler_params=pltpu.CompilerParams(vmem_limit_bytes=16 * MIB),
        cost_estimate=cost(count * slots * SEQ * 4096, count * slots * SEQ * 8),
    )(qkv, grad_mixed, prob, *after)


def feed_forward(place, tokens, attended, cotangent, gains, in_sources, out_sources, by_chips):
    slots, width = tokens.shape
    side_cols = width // 2
    hidden_cols = 2 * (in_sources[0].shape[-1] - side_cols)
    block = 256
    blocks = slots // block
    chunk = 768
    per_side = hidden_cols // 2 // chunk
    count_att = len(attended)
    root, bend = math.sqrt(2.0 / math.pi), 0.044715

    def kernel(place_ref, x_hbm, cot_hbm, gains_ref, *refs):
        refs = list(refs)

        def take(number):
            taken, refs[:] = refs[:number], refs[number:]
            return taken

        att_hbm, in_hbm, out_hbm = take(count_att), take(len(in_sources)), take(len(out_sources))
        y_hbm, back_hbm, branch_hbm, flipped_hbm, pre_hbm = take(5)
        out_targets = take(2 if by_chips else 1)
        x, att, cot, w_o, w_in, w_out, hidden, normed, flipped = take(9)
        sum_g, act, grad_pre, tile_out = take(4)
        load_sems, o_sems, in_sems, out_sems, store_sems, pre_sems, tile_out_sems = take(7)
        me = place_ref[0]
        core = me % 2
        gain = gains_ref[1:2, :]

        def rows_of(index):
            return pl.ds(pl.multiple_of(index * block, block), block)

        loads = [
            pltpu.make_async_copy(x_hbm, x, load_sems.at[0]),
            pltpu.make_async_copy(cot_hbm, cot, load_sems.at[1]),
        ]
        cols = 0
        for number, source in enumerate(att_hbm):
            loads.append(
                pltpu.make_async_copy(
                    source, att.at[:, pl.ds(cols, source.shape[1])], load_sems.at[2 + number]
                )
            )
            cols += source.shape[1]
        o_loads, in_loads, out_loads = [], [], []
        for side in range(2):
            o_cols = pl.ds(pl.multiple_of((core ^ side) * side_cols, 128), side_cols)
            o_loads += column_copies(
                me, in_hbm, w_o.at[:, o_cols], o_sems.at[side], side, by_chips, (0, side_cols)
            )
            in_loads.append(
                column_copies(
                    me,
                    in_hbm,
                    w_in.at[side],
                    in_sems.at[side],
                    side,
                    by_chips,
                    (side_cols, in_sources[0].shape[-1]),
                )
            )
            out_loads += row_copies(me, out_hbm, w_out, out_sems.at[side], side, by_chips)
        start_all(loads[2:])
        start_all(o_loads)
        start_all(loads[:2])
        start_all(in_loads[0])
        start_all(out_loads)
        wait_all(loads)
        wait_all(o_loads)
        start_all(in_loads[1])

        count = width // block

        def cols_of(index):
            return pl.ds(pl.multiple_of(index * block, block), block)

        def residual(index, carry):
            cols = cols_of(index)
            hidden[:, cols] = wide(x[:, cols]) + nn(att[...], w_o[:, cols])
            return carry

        lax.fori_loop(0, count, residual, 0)

        def before(index, carry):
            where = rows_of(index)
            value = hidden[where, :]
            rows = value * norm_scale(value) * gain
            normed[where, :] = low(rows)
            flipped[:, where] = low(jnp.transpose(rows))
            return carry

        lax.fori_loop(0, blocks, before, 0)
        flip_store = pltpu.make_async_copy(flipped, flipped_hbm, store_sems.at[3])
        flip_store.start()
        wait_all(in_loads[0])
        wait_all(out_loads)

        per_chunk = chunk // block
        chunks = 2 * per_side

        def tile_stores(number):
            strip = (core ^ (number // per_side)) * per_side + number % per_side
            slot = number % 2
            return strip_copies(
                me, tile_out.at[slot], out_targets, tile_out_sems.at[slot], strip, by_chips
            )

        def pre_store(number):
            side, part = number // per_side, number % per_side
            strip = (core ^ side) * per_side + part
            units = pl.ds(pl.multiple_of(part * chunk, chunk), chunk)
            return pltpu.make_async_copy(
                grad_pre.at[side, :, units], pre_hbm.at[strip], pre_sems.at[number]
            )

        def through(index, carry):
            number, inside = index // per_chunk, index % per_chunk
            side, part = number // per_side, number % per_side
            first = part * chunk + inside * block
            unit_cols = pl.ds(pl.multiple_of(first, block), block)
            unit_row = (core ^ side) * (per_side * chunk) + first
            unit_rows = pl.ds(pl.multiple_of(unit_row, block), block)

            @pl.when(index == per_side * per_chunk)
            def _():
                wait_all(in_loads[1])

            @pl.when((inside == 0) & (number >= 2))
            def _():
                wait_all(tile_stores(number - 2))

            pre = nn(normed[...], w_in[side, :, unit_cols])
            square = pre * pre
            slope = jnp.tanh(pre * (root + (root * bend) * square))
            opened = 0.5 + 0.5 * slope
            gate = opened + pre * (1.0 - slope * slope) * (
                0.5 * root + (1.5 * bend * root) * square
            )
            acted = low(pre * opened)
            act[side, :, unit_cols] = acted
            grad_pre[side, :, unit_cols] = low(nt(cot[...], w_out[unit_rows, :]) * gate)
            tile_out[number % 2, cols_of(inside), :] = low(tn(acted, cot[...]))

            @pl.when(inside == per_chunk - 1)
            def _():
                start_all(tile_stores(number))
                pre_store(number).start()

            return carry

        lax.fori_loop(0, chunks * per_chunk, through, 0)

        half = hidden_cols // 2
        halves = [pl.ds(pl.multiple_of((core ^ side) * half, block), half) for side in range(2)]

        def sums_of(index, carry):
            cols = cols_of(index)
            value = nn(act[0], w_out[halves[0], cols]) + nn(act[1], w_out[halves[1], cols])
            x[:, cols] = low(hidden[:, cols] + value)
            sum_g[:, cols] = nt(grad_pre[0], w_in[0, cols, :]) + nt(grad_pre[1], w_in[1, cols, :])
            return carry

        lax.fori_loop(0, count, sums_of, 0)

        def after(index, carry):
            where = rows_of(index)
            value = hidden[where, :]
            scale = norm_scale(value)
            back = rms_back(value * scale, scale, gain, sum_g[where, :])
            normed[where, :] = low(wide(cot[where, :]) + back)
            return carry

        y_store = pltpu.make_async_copy(x, y_hbm, store_sems.at[0])
        y_store.start()
        lax.fori_loop(0, blocks, after, 0)
        branch_store = pltpu.make_async_copy(normed, branch_hbm, store_sems.at[1])
        branch_store.start()

        def mixed_back(index, carry):
            cols = cols_of(index)
            att[:, cols] = low(nt(normed[...], w_o[cols, :]))
            return carry

        lax.fori_loop(0, count, mixed_back, 0)
        last = [pltpu.make_async_copy(att, back_hbm, store_sems.at[2])]
        last[0].start()
        last += [flip_store, y_store, branch_store]
        for number in range(chunks):
            last.append(pre_store(number))
            if number >= chunks - 2:
                last += tile_stores(number)
        wait_all(last)

    sums = jax.ShapeDtypeStruct
    flat = sums((slots, width), jnp.bfloat16)
    devices = lax.axis_size("fsdp")
    if by_chips:
        line = devices // 8
        out_shapes = [sums((4, line, hidden_cols // devices, width), jnp.bfloat16)] * 2
    else:
        out_shapes = [sums((hidden_cols, width), jnp.bfloat16)]
    outs = [
        flat,
        flat,
        flat,
        sums((width, slots), jnp.bfloat16),
        sums((hidden_cols // chunk, slots, chunk), jnp.bfloat16),
    ] + out_shapes
    bf16, f32 = jnp.bfloat16, jnp.float32
    result = pl.pallas_call(
        kernel,
        out_shape=outs,
        in_specs=[IN_SMEM, IN_HBM, IN_HBM, IN_VMEM]
        + [IN_HBM] * (count_att + len(in_sources) + len(out_sources)),
        out_specs=[IN_HBM] * len(outs),
        scratch_shapes=[
            pltpu.VMEM((slots, width), bf16),
            pltpu.VMEM((slots, width), bf16),
            pltpu.VMEM((slots, width), bf16),
            pltpu.VMEM((width, width), bf16),
            pltpu.VMEM((2, width, hidden_cols // 2), bf16),
            pltpu.VMEM((hidden_cols, width), bf16),
            pltpu.VMEM((slots, width), f32),
            pltpu.VMEM((slots, width), bf16),
            pltpu.VMEM((width, slots), bf16),
            pltpu.VMEM((slots, width), f32),
            pltpu.VMEM((2, slots, hidden_cols // 2), bf16),
            pltpu.VMEM((2, slots, hidden_cols // 2), bf16),
            pltpu.VMEM((2, chunk, width), bf16),
            pltpu.SemaphoreType.DMA((2 + count_att,)),
            pltpu.SemaphoreType.DMA((2, 16)),
            pltpu.SemaphoreType.DMA((2, 16)),
            pltpu.SemaphoreType.DMA((2, 16)),
            pltpu.SemaphoreType.DMA((4,)),
            pltpu.SemaphoreType.DMA((2 * per_side,)),
            pltpu.SemaphoreType.DMA((2, 8)),
        ],
        compiler_params=pltpu.CompilerParams(vmem_limit_bytes=56 * MIB),
        cost_estimate=cost(
            slots * width * (12 * hidden_cols + 6 * width), 60 * MIB
        ),
    )(place, tokens, cotangent, gains, *attended, *in_sources, *out_sources)
    output, back, *rest = result
    return output, back, tuple(rest[:3]), tuple(rest[3:])


def in_weights_back(place, attended, branch, flipped, grad_pre, by_chips):
    slots, width = branch.shape
    strips, _, chunk = grad_pre.shape
    side_cols = width // 2
    per_side = strips // 2
    packed = side_cols + per_side * chunk
    count_att = len(attended)

    def kernel(place_ref, branch_hbm, flipped_hbm, pre_hbm, *refs):
        att_hbm, refs = refs[:count_att], refs[count_att:]
        targets, refs = refs[:-9], refs[-9:]
        token_ref, att, branch, flipped, pre, tile, load_sems, tile_sems, o_sems = refs
        token_ref[0, 0] = 0.0
        me = place_ref[0]
        core = me % 2

        def place_of(number):
            return 1 - number // per_side, number % per_side

        def pre_load(number):
            side, part = place_of(number)
            return pltpu.make_async_copy(
                pre_hbm.at[(core ^ side) * per_side + part], pre.at[number], load_sems.at[number]
            )

        pre_loads = [pre_load(number) for number in range(strips)]
        flip_load = pltpu.make_async_copy(flipped_hbm, flipped, load_sems.at[strips])
        loads = [pltpu.make_async_copy(branch_hbm, branch, load_sems.at[strips + 1])]
        cols = 0
        for number, source in enumerate(att_hbm):
            loads.append(
                pltpu.make_async_copy(
                    source,
                    att.at[:, pl.ds(cols, source.shape[1])],
                    load_sems.at[strips + 2 + number],
                )
            )
            cols += source.shape[1]
        flip_load.start()
        start_all(pre_loads)
        start_all(loads)
        flip_load.wait()
        block = 256
        per_chunk = chunk // block

        def stores(number, side, part):
            return half_copies(
                me,
                tile.at[number % 2],
                targets,
                tile_sems.at[number % 2],
                side,
                by_chips,
                (pl.multiple_of(side_cols + part * chunk, 128), chunk),
            )

        for half in range(2):
            side = 1 - half

            def one(index, carry):
                part, inside = index // per_chunk, index % per_chunk
                number = half * per_side + part

                @pl.when(inside == 0)
                def _():
                    pre_load(number).wait()

                if half:

                    @pl.when(inside == 0)
                    def _():
                        wait_all(stores(part, 1, part))

                cols = pl.ds(pl.multiple_of(inside * block, block), block)
                tile[part % 2, :, cols] = low(nn(flipped[...], pre[number, :, cols]))

                @pl.when(inside == per_chunk - 1)
                def _():
                    start_all(stores(part, side, part))

                return carry

            lax.fori_loop(0, per_side * per_chunk, one, 0)
        wait_all(loads)
        wait_all(stores(0, 0, 0))

        def last(index, carry):
            some = pl.ds(pl.multiple_of(index * block, block), block)
            tile[0, some, :] = low(tn(att[:, some], branch[...]))
            return carry

        lax.fori_loop(0, width // block, last, 0)
        copies = []
        for side in range(2):
            o_cols = pl.ds(pl.multiple_of((core ^ side) * side_cols, 128), side_cols)
            copies += half_copies(
                me,
                tile.at[0, :, o_cols],
                targets,
                o_sems.at[side],
                side,
                by_chips,
                (0, side_cols),
            )
        start_all(copies)
        wait_all(stores(1, 0, 1))
        wait_all(copies)

    sums = jax.ShapeDtypeStruct
    bf16 = jnp.bfloat16
    if by_chips:
        line = lax.axis_size("fsdp") // 8
        shapes = [sums((4, line, width // (4 * line), packed), bf16)] * 2
    else:
        shapes = [sums((2, width, packed), bf16)]
    result = pl.pallas_call(
        kernel,
        out_shape=shapes + [TOKEN_SHAPE],
        in_specs=[IN_SMEM] + [IN_HBM] * (3 + count_att),
        out_specs=[IN_HBM] * len(shapes) + [IN_SMEM],
        scratch_shapes=[
            pltpu.VMEM((slots, width), bf16),
            pltpu.VMEM((slots, width), bf16),
            pltpu.VMEM((width, slots), bf16),
            pltpu.VMEM((strips, slots, chunk), bf16),
            pltpu.VMEM((2, width, chunk), bf16),
            pltpu.SemaphoreType.DMA((strips + 2 + count_att,)),
            pltpu.SemaphoreType.DMA((2, 16)),
            pltpu.SemaphoreType.DMA((2, 16)),
        ],
        compiler_params=pltpu.CompilerParams(vmem_limit_bytes=40 * MIB),
        cost_estimate=cost(2 * slots * width * (width + strips * chunk), 20 * MIB),
    )(place, branch, flipped, grad_pre, *attended)
    return result[:-1], result[-1]


def back_places(grads, side_cols):
    places, first = [], 0
    for number, some in enumerate(grads):
        for col in range(0, some[0].shape[1], 128):
            half, start = divmod(first + col, side_cols)
            places += [
                (3 * number + part, col, half, part * side_cols + start) for part in range(3)
            ]
        first += some[0].shape[1]
    return [grad for some in grads for grad in some], places


def put_columns(refs, places, parts, rows):
    for number, col, half, start in places:
        parts[half, :, start : start + 128] = refs[number][rows, col : col + 128]


def weights_back(place, normed_attn, grads, diagonals, by_chips, after=()):
    slots, width = normed_attn.shape
    side_cols = width // 2
    flat_grads, places = back_places(grads, side_cols)

    onehot = np.pad(
        (line_ids()[:, None] == np.arange(NB)[None, :]).astype(np.float32), ((0, 0), (0, 128 - NB))
    )
    pairs = len(diagonals)
    heads = sum(2 * some.shape[0] for some in diagonals)
    table_rows = -(-heads // 8) * 8

    def kernel(place_ref, normed_ref, onehot_ref, *refs):
        diag_refs, refs = refs[:pairs], refs[pairs:]
        g_refs = refs[: len(flat_grads)]
        refs = refs[len(flat_grads) + len(after) :]
        targets, (table_ref, token_ref, parts, tile) = refs[:-4], refs[-4:]
        token_ref[0, 0] = 0.0
        me = place_ref[0]
        core = me % 2
        put_columns(g_refs, places, parts, slice(None))
        rows = [
            ref[one, head : head + 1, :]
            for ref in diag_refs
            for one in range(ref.shape[0])
            for head in range(2)
        ]
        if table_rows > heads:
            rows.append(jnp.zeros((table_rows - heads, 2 * SEQ), jnp.float32))
        table_ref[...] = lax.dot_general(
            jnp.concatenate(rows, 0),
            onehot_ref[...],
            (((1,), (0,)), ((), ())),
            precision=lax.Precision.HIGHEST,
            preferred_element_type=jnp.float32,
        )
        for side in range(2):
            half = core ^ side
            for first in range(0, 3 * side_cols, 512):
                some = slice(first, min(first + 512, 3 * side_cols))
                tile[:, some] = low(tn(normed_ref[...], parts[half, :, some]))
            if not by_chips:
                targets[0][half] = tile[...]
                continue
            planes, line, rows = targets[side].shape[:3]
            for plane in range(planes):
                for hop in range(line):
                    start = pl.multiple_of(((me // 2) ^ (4 * hop + plane)) * rows, 16)
                    targets[side][plane, hop] = tile[pl.ds(start, rows), :]

    sums = jax.ShapeDtypeStruct
    if by_chips:
        line = lax.axis_size("fsdp") // 8
        shapes = [sums((4, line, width // (4 * line), 3 * side_cols), jnp.bfloat16)] * 2
    else:
        shapes = [sums((2, width, 3 * side_cols), jnp.bfloat16)]
    result = pl.pallas_call(
        kernel,
        out_shape=shapes + [sums((table_rows, 128), jnp.float32), TOKEN_SHAPE],
        in_specs=[IN_SMEM] + [IN_VMEM] * (2 + pairs + len(flat_grads)) + [IN_HBM] * len(after),
        out_specs=[IN_VMEM] * (len(shapes) + 1) + [IN_SMEM],
        scratch_shapes=[
            pltpu.VMEM((2, slots, 3 * side_cols), jnp.bfloat16),
            pltpu.VMEM((width, 3 * side_cols), jnp.bfloat16),
        ],
        compiler_params=pltpu.CompilerParams(vmem_limit_bytes=24 * MIB),
        cost_estimate=cost(6 * slots * width * width, 15 * MIB),
    )(place, normed_attn, jnp.asarray(onehot), *diagonals, *flat_grads, *after)
    return result[:-2], result[-2], result[-1]


def inputs_back(
    tokens, gains, branch, grads, weights, place, first, count, done=None, after=()
):
    slots, width = tokens.shape
    side_cols = width // 2
    flat_grads, places = back_places(grads, side_cols)
    block = 256
    held = () if done is None else (done,)

    def kernel(place_ref, x_ref, gains_ref, branch_ref, weights_ref, *refs):
        g_refs, refs = refs[: len(flat_grads)], refs[len(flat_grads) + len(after) + len(held) :]
        out_hbm, token_ref, parts, out, summed, out_sems = refs
        token_ref[0, 0] = 0.0
        core = place_ref[0] % 2
        gain = gains_ref[0:1, :]
        put_columns(g_refs, places, parts, slice(first, first + count))

        def back(index, carry):
            cols = pl.ds(pl.multiple_of(index * block, block), block)
            summed[:, cols] = nt(parts[core], weights_ref[0, cols, : 3 * side_cols]) + nt(
                parts[1 - core], weights_ref[1, cols, : 3 * side_cols]
            )
            return carry

        lax.fori_loop(0, width // block, back, 0)

        def finish(index, carry):
            here = pl.ds(pl.multiple_of(index * block, block), block)
            where = pl.ds(pl.multiple_of(first + index * block, block), block)
            rows = wide(x_ref[where, :])
            scale = norm_scale(rows)
            back = rms_back(rows * scale, scale, gain, summed[here, :])
            out[here, :] = low(wide(branch_ref[where, :]) + back)
            return carry

        lax.fori_loop(0, count // block, finish, 0)
        last = pltpu.make_async_copy(out, out_hbm.at[pl.ds(first, count)], out_sems.at[0])
        last.start()
        last.wait()

    bf16, f32 = jnp.bfloat16, jnp.float32
    return pl.pallas_call(
        kernel,
        out_shape=[jax.ShapeDtypeStruct((slots, width), bf16), TOKEN_SHAPE],
        in_specs=[IN_SMEM]
        + [IN_VMEM] * (4 + len(flat_grads))
        + [IN_HBM] * (len(after) + len(held)),
        out_specs=[IN_HBM, IN_SMEM],
        scratch_shapes=[
            pltpu.VMEM((2, count, 3 * side_cols), bf16),
            pltpu.VMEM((count, width), bf16),
            pltpu.VMEM((count, width), f32),
            pltpu.SemaphoreType.DMA((1,)),
        ],
        compiler_params=pltpu.CompilerParams(vmem_limit_bytes=20 * MIB),
        cost_estimate=cost(6 * count * width * width, 15 * MIB),
        input_output_aliases={5 + len(flat_grads) + len(after): 0} if held else {},
    )(place, tokens, gains, branch, weights, *flat_grads, *after, *held)


def pack_halves(place, gain_attn, gain_ffn, shards_qkv, shards_in):
    rows = shards_qkv[0].shape[0]
    groups = (shards_qkv, shards_in)
    counts = [sum(shard.shape[1] for shard in group) // 2 for group in groups]

    def kernel(place_ref, attn_ref, ffn_ref, *refs):
        ins, outs = refs[: -2 * len(groups)], refs[-2 * len(groups) :]
        core = place_ref[0] % 2
        first = 0
        for number, group in enumerate(groups):
            for other in range(2):
                out, col = outs[2 * number + other], 0
                for ref in ins[first : first + len(group)]:
                    half = ref.shape[1] // 2
                    start = pl.multiple_of((core ^ other) * half, 128)
                    out[:, col : col + half] = ref[:, pl.ds(start, half)]
                    col += half
            first += len(group)
        same = lax.broadcasted_iota(jnp.int32, (rows, rows), 0) == lax.broadcasted_iota(
            jnp.int32, (rows, rows), 1
        )
        lane = lax.broadcasted_iota(jnp.int32, (rows, 128), 1)
        cols = jnp.zeros((rows, 128), jnp.float32)
        for number, ref in enumerate((attn_ref, ffn_ref)):
            row = wide(ref[...])
            col = jnp.sum(jnp.where(same, row, 0.0), axis=1, keepdims=True)
            cols = jnp.where(lane == number, col, cols)
        for other in range(2):
            outs[other][:, counts[0] :] = low(cols)

    shapes = [
        jax.ShapeDtypeStruct((rows, count + extra), jnp.bfloat16)
        for count, extra in zip(counts, (128, 0))
        for _ in range(2)
    ]
    return pl.pallas_call(
        kernel,
        out_shape=shapes,
        in_specs=[IN_SMEM] + [IN_VMEM] * (2 + len(shards_qkv) + len(shards_in)),
        out_specs=[IN_VMEM] * len(shapes),
    )(place, gain_attn, gain_ffn, *shards_qkv, *shards_in)


def prepare(compute, operands, shapes, after=(), place=None, pair=()):
    scalars = [] if place is None else [place]

    def kernel(*refs):
        refs = list(refs)
        where = [ref[0] for ref in refs[: len(scalars)]]
        ins, refs = refs[len(scalars) :][: len(operands)], refs[len(scalars) + len(operands) :]
        outs = refs[len(pair) + len(after) :]
        outs[-1][0, 0] = 0.0
        if pair:
            outs[-2][...] = refs[0][...] + refs[1][...]
        compute(*where, ins, outs)

    result = pl.pallas_call(
        kernel,
        out_shape=list(shapes) + [like(array, *array.shape) for array in pair[:1]] + [TOKEN_SHAPE],
        in_specs=[IN_SMEM] * len(scalars)
        + [IN_VMEM] * (len(operands) + len(pair))
        + [IN_HBM] * len(after),
        out_specs=[IN_VMEM] * (len(shapes) + len(pair[:1])) + [IN_SMEM],
        compiler_params=pltpu.CompilerParams(vmem_limit_bytes=8 * MIB),
        cost_estimate=cost(0, sum(2 * array.size for array in operands)),
    )(*scalars, *operands, *pair, *after)
    return result[:-1], result[-1]


def like(array, *shape):
    return jax.ShapeDtypeStruct(shape, array.dtype)


def chip_unit(place, mine, got, after=()):
    def compute(me, ins, outs):
        first = me % 2 == 0
        own, other = wide(ins[0][...]), wide(ins[1][...])
        outs[0][...] = low(
            jnp.concatenate([jnp.where(first, own, other), jnp.where(first, other, own)], 0)
        )

    shape = like(mine, 2 * mine.shape[0], mine.shape[1])
    (unit,), token = prepare(compute, [mine, got], [shape], after, place)
    return unit, token


def stack_and_unit(place, parts, mine, got, after=()):
    def compute(me, ins, outs):
        for number in range(len(parts)):
            outs[0][number] = ins[number][...]
        first = me % 2 == 0
        own, other = wide(ins[-2][...]), wide(ins[-1][...])
        outs[1][...] = low(
            jnp.concatenate([jnp.where(first, own, other), jnp.where(first, other, own)], 0)
        )

    shapes = [
        like(parts[0], len(parts), *parts[0].shape),
        like(mine, 2 * mine.shape[0], mine.shape[1]),
    ]
    operands = list(tuple(parts) + (mine, got))
    return prepare(compute, operands, shapes, after, place)


def stack_and_copies(parts, arrays, after=()):
    def compute(ins, outs):
        for number in range(len(parts)):
            outs[0][number] = ins[number][...]
        for number in range(len(arrays)):
            outs[1 + number][...] = ins[len(parts) + number][...]

    shapes = [like(parts[0], len(parts), *parts[0].shape)]
    shapes += [like(array, *array.shape) for array in arrays]
    return prepare(compute, [*parts, *arrays], shapes, after)


def copied(arrays, after=()):
    def compute(ins, outs):
        for number in range(len(arrays)):
            outs[number][...] = ins[number][...]

    shapes = [like(array, *array.shape) for array in arrays]
    return prepare(compute, list(arrays), shapes, after)


def far_and_copies(over_x, over_y, arrays, after=()):
    half = over_x.shape[0] // 2

    def compute(ins, outs):
        outs[0][...] = ins[0][:half]
        outs[1][...] = ins[1][half:]
        for number in range(len(arrays)):
            outs[2 + number][...] = ins[2 + number][...]

    shapes = [like(over_x, half, *over_x.shape[1:])] * 2
    shapes += [like(array, *array.shape) for array in arrays]
    return prepare(compute, [over_y, over_x, *arrays], shapes, after)


def first_sends(keep, got, after=(), pair=()):
    places = ((3, 0), (1, 0), (3, 1), (2, 1))
    half = keep.shape[1] // 2

    def compute(ins, outs):
        for number, (plane, late) in enumerate(places):
            for hop in range(half):
                at = late * half + hop
                outs[number // 2][number % 2, hop] = low(
                    wide(ins[0][plane, at]) + wide(ins[1][plane, at])
                )

    shapes = [like(keep, 2, half, *keep.shape[2:])] * 2
    return prepare(compute, [keep, got], shapes, after, pair=pair)


def second_sends(keep, got, first, after=(), pair=()):
    half = keep.shape[1] // 2

    def compute(ins, outs):
        for number, (plane, late) in enumerate(((2, 0), (1, 1))):
            for hop in range(half):
                at = late * half + hop
                outs[number][hop] = low(
                    wide(ins[0][plane, at])
                    + wide(ins[1][plane, at])
                    + wide(ins[2 + number][0, hop])
                )

    shapes = [like(keep, half, *keep.shape[2:])] * 2
    return prepare(compute, [keep, got, *first], shapes, after, pair=pair)


def line_sums(keep, got, first, second, after=(), pair=()):
    line = keep.shape[1]
    half = line // 2

    def compute(ins, outs):
        for at in range(line):
            direct, merged = ins[2 + at // half], ins[4 + at // half]
            total = wide(ins[0][0, at]) + wide(ins[1][0, at]) + wide(direct[1, at % half])
            outs[at][...] = low(total + wide(merged[at % half]))

    operands = [keep, got, *first, *second]
    return prepare(compute, operands, [like(keep, *keep.shape[2:])] * line, after, pair=pair)


def chip_sum_halves(place, terms, copied=(), after=(), pair=()):
    rows, cols = terms[0].shape

    def compute(me, ins, outs):
        total = add(*[ref[...] for ref in ins[: len(terms)]])
        first = me % 2 == 0
        upper, lower = total[: rows // 2], total[rows // 2 :]
        outs[0][...] = jnp.where(first, upper, lower)
        outs[1][...] = jnp.where(first, lower, upper)
        for number in range(len(copied)):
            outs[2 + number][...] = ins[len(terms) + number][...]

    shape = jax.ShapeDtypeStruct((rows // 2, cols), jnp.float32)
    shapes = [shape, shape] + [like(array, *array.shape) for array in copied]
    operands = list(tuple(terms) + tuple(copied))
    return prepare(compute, operands, shapes, after, place, pair=pair)


def join_halves(place, mine, other, parts, factor, gain, weights, after=()):
    rows = mine.shape[0]
    skipped = len(parts) - len(weights)

    def compute(me, ins, outs):
        core = me % 2
        first = 0
        for count, out in zip(parts, outs):
            for ref, half in ((ins[0], core), (ins[1], 1 - core)):
                start = pl.multiple_of(half * count, 128)
                out[:, pl.ds(start, count)] = ref[:, first : first + count] * factor
            first += count
        total = jnp.zeros((rows, 1), jnp.float32)
        for number, weight in enumerate(ins[3:]):
            product = wide(weight[...]) * outs[skipped + number][...]
            total = total + jnp.sum(product, axis=1, keepdims=True)
        same = lax.broadcasted_iota(jnp.int32, (rows, rows), 0) == lax.broadcasted_iota(
            jnp.int32, (rows, rows), 1
        )
        column = jnp.sum(jnp.where(same, wide(ins[2][...]), 0.0), axis=1, keepdims=True)
        outs[len(parts)][...] = jnp.broadcast_to(total / column, (rows, 128))

    shapes = [jax.ShapeDtypeStruct((rows, 2 * count), jnp.float32) for count in parts]
    shapes.append(jax.ShapeDtypeStruct((rows, 128), jnp.float32))
    operands = list((mine, other, gain[None]) + tuple(weights))
    return prepare(compute, operands, shapes, after, place)[0]


def gather_plain(shards):
    full = [lax.all_gather(shard, "fsdp", axis=0, tiled=True) for shard in shards]
    gain_attn, w_query, w_key, w_value, w_attn_out, gain_ffn, w_ffn_in, w_ffn_out = full
    gains = jnp.pad(jnp.stack([gain_attn, gain_ffn], 1), ((0, 0), (0, 126)))
    return (
        (halves_of(w_query, w_key, w_value, jnp.concatenate([gains, gains], 1)),),
        (halves_of(w_attn_out, w_ffn_in),),
        (w_ffn_out,),
    )


def gain_back(gain, weights, grads):
    return sum(
        jnp.sum(weight.astype(jnp.float32) * grad, axis=1) for weight, grad in zip(weights, grads)
    ) / gain.astype(jnp.float32)


def per_device(
    tokens,
    lengths,
    gain_attn,
    w_query,
    w_key,
    w_value,
    w_attn_out,
    gain_ffn,
    w_ffn_in,
    w_ffn_out,
    bucket_bias_matrix,
    cotangent,
):
    slot_count, width = tokens.shape
    heads = bucket_bias_matrix.shape[1]
    devices = lax.axis_size("fsdp")
    factor = 1.0 / math.sqrt(slot_count * devices)
    place = lax.axis_index("fsdp").astype(jnp.int32)[None]
    side = width // 2
    by_chips = devices == 32
    pairs = heads // 2
    attended, probs, backs = [], [], []

    def pairs_of(arrays):
        return sum(array.shape[1] for array in arrays) * heads // (2 * width)

    def forward(count, after=()):
        out, prob, token = attend(lengths, qkv, planes, pairs_of(attended), count, after)
        attended.append(out)
        probs.append(prob)
        return token

    def backward(after=()):
        number = len(backs)
        first, count = pairs_of(attended[:number]), pairs_of(attended[number : number + 1])
        result = attend_back(qkv, grad_attended, probs[number], first, count, heads, after)
        backs.append(result[:4])
        return result[4]

    def weights(after=()):
        grads, diagonals = [some[:3] for some in backs], [some[3] for some in backs]
        return weights_back(place, normed_attn, grads, diagonals, by_chips, after)

    def inputs(first, count, done=None, after=()):
        grads = [some[:3] for some in backs]
        return inputs_back(
            tokens, gains, saved[0], grads, weights_qkv, place, first, count, done, after
        )

    if by_chips:
        mine_qkv, for_qkv, mine_in, for_in = pack_halves(
            place,
            gain_attn[None],
            gain_ffn[None],
            (w_query, w_key, w_value),
            (w_attn_out, w_ffn_in),
        )
        unit, token = chip_unit(place, mine_qkv, swap(for_qkv, 1))
        line = gather_line(unit)
        planes, token = bias_planes(bucket_bias_matrix, (token,))

        (near_qkv, unit), token = stack_and_copies(line, (w_ffn_out,), (token,))
        plane_qkv = gather_plane(near_qkv)
        line = gather_line(unit)

        parts, token = far_and_copies(*plane_qkv, (near_qkv,) + plane_qkv, line + (token,))
        far_qkv = gather_far(*parts[:2])
        other_qkv = tuple(swap(part, 1) for part in parts[2:])

        (near_out, unit), token = stack_and_unit(
            place, line, mine_in, swap(for_in, 1), far_qkv + other_qkv + (token,)
        )
        plane_out = gather_plane(near_out)
        other_qkv = other_qkv + (swap(far_qkv[0], 1), swap(far_qkv[1], 1))
        in_qkv = (near_qkv,) + plane_qkv + far_qkv + other_qkv
        qkv, normed_attn, weights_qkv, gains, token = project_qkv(
            place, tokens, in_qkv, by_chips, (planes, token)
        )

        parts, token = far_and_copies(*plane_out, (unit,), (token,))
        far_out = gather_far(*parts[:2])
        line = gather_line(parts[2])
        token = forward(2, (token,))

        parts, token = stack_and_copies(line, (near_out,) + plane_out, far_out + (token,))
        near_in = parts[0]
        plane_in = gather_plane(near_in)
        other_out = tuple(swap(part, 1) for part in parts[1:])
        token = forward(1, (token,))

        parts, token = far_and_copies(*plane_in, far_out + (near_in,), other_out + (token,))
        far_in = gather_far(*parts[:2])
        other_out = other_out + (swap(parts[2], 1), swap(parts[3], 1))
        other_in = (swap(parts[4], 1),)
        token = forward(2, (token,))

        parts, token = copied(plane_in + far_in, other_in + other_out[3:] + (token,))
        other_in = other_in + tuple(swap(part, 1) for part in parts)
        token = forward(1, (token,))

        in_ffn = (near_in,) + plane_in + far_in + other_in
        in_out = (near_out,) + plane_out + far_out + other_out
    else:
        planes, _ = bias_planes(bucket_bias_matrix)
        in_qkv, in_ffn, in_out = gather_plain(
            (gain_attn, w_query, w_key, w_value, w_attn_out, gain_ffn, w_ffn_in, w_ffn_out)
        )
        qkv, normed_attn, weights_qkv, gains, _ = project_qkv(place, tokens, in_qkv, by_chips)
        for _ in range(pairs):
            forward(1)

    output, grad_attended, saved, part_out = feed_forward(
        place, tokens, attended, cotangent, gains, in_ffn, in_out, by_chips
    )

    if by_chips:
        keep_out, send_out = part_out
        got_out = swap(send_out, 1)
        (keep_in, send_in), token = in_weights_back(place, attended, *saved, by_chips)

        sends, token = first_sends(keep_out, got_out, (token,))
        first_out = scatter_first(sends)
        got_in = swap(send_in, 1)
        token = backward((token,))

        sends, token = second_sends(keep_out, got_out, first_out, (got_in, token))
        second_out = scatter_second(sends)
        token = backward((token,))

        sums, token = line_sums(keep_out, got_out, first_out, second_out, (token,))
        last_out = scatter_line(sums)
        sends, token = first_sends(keep_in, got_in, (token,))
        first_in = scatter_first(sends)
        token = backward((token,))

        sends, token = second_sends(keep_in, got_in, first_in, last_out + (token,))
        second_in = scatter_second(sends)
        token = backward((token,))

        sums, token = line_sums(keep_in, got_in, first_in, second_in, (token,))
        last_in = scatter_line(sums)
        (keep_qkv, send_qkv), table, token = weights(last_out + (token,))

        parts, token = chip_sum_halves(place, last_in, (send_qkv, table), (token,))
        mine_in, for_in, send_qkv, table = parts
        got_qkv, got_in, got = swap(send_qkv, 1), swap(for_in, 1), swap(table, 1)
        grad_tokens, token = inputs(0, slot_count // 2, None, (token,))

        parts, token = first_sends(keep_qkv, got_qkv, (got_in, token), (table, got))
        first_qkv = scatter_first(parts[:2])
        table, got = parts[2], swap(parts[2], 2)
        grad_tokens, token = inputs(slot_count // 2, slot_count // 2, grad_tokens, (token,))

        parts, token = second_sends(keep_qkv, got_qkv, first_qkv, (token,), (table, got))
        second_qkv = scatter_second(parts[:2])
        table, got = parts[2], swap(parts[2], 4)
        sum_out = add(*last_out) * factor

        parts, token = line_sums(
            keep_qkv, got_qkv, first_qkv, second_qkv, (token,), (table, got)
        )
        last_qkv = scatter_line(parts[:-1])
        table, got = parts[-1], swap(parts[-1], 8)
        sum_o, sum_in, grad_gain_ffn = join_halves(
            place,
            mine_in,
            got_in,
            (side, keep_in.shape[-1] - side),
            factor,
            gain_ffn,
            (w_ffn_in,),
            (token,),
        )

        parts, token = chip_sum_halves(place, last_qkv, (), (token,), (table, got))
        mine_qkv, for_qkv, table = parts
        got_qkv, got = swap(for_qkv, 1), swap(table, 16)
        table = table + got
        sum_q, sum_k, sum_v, grad_gain_attn = join_halves(
            place,
            mine_qkv,
            got_qkv,
            (side, side, side),
            factor,
            gain_attn,
            (w_query, w_key, w_value),
        )
        grad_gain_attn, grad_gain_ffn = grad_gain_attn[:, 0], grad_gain_ffn[:, 0]
        sums = (sum_q, sum_k, sum_v, sum_o, sum_in, sum_out)
    else:
        for _ in range(pairs):
            backward()
        part_in, _ = in_weights_back(place, attended, *saved, by_chips)
        part_qkv, table, _ = weights()
        grad_tokens, _ = inputs(0, slot_count)
        sums = sum_plain(
            jnp.concatenate([part_qkv[0], part_in[0][:, :, :side]], 2),
            part_in[0][:, :, side:],
            part_out[0],
        )
        sums = [total * factor for total in sums]
        table = lax.psum(table, "fsdp")
        grad_gain_attn = gain_back(gain_attn, (w_query, w_key, w_value), sums[:3])
        grad_gain_ffn = gain_back(gain_ffn, (w_ffn_in,), sums[4:5])

    return (
        output,
        grad_tokens,
        grad_gain_attn,
        sums[0],
        sums[1],
        sums[2],
        sums[3],
        grad_gain_ffn,
        sums[4],
        sums[5],
        table[:heads, :NB].T * factor,
    )


def solution(mesh):
    placed = (
        P("fsdp", None),
        P("fsdp", None),
        P("fsdp"),
        P("fsdp", None),
        P("fsdp", None),
        P("fsdp", None),
        P("fsdp", None),
        P("fsdp"),
        P("fsdp", None),
        P("fsdp", None),
        P(),
        P("fsdp", None),
    )
    return jax.shard_map(
        per_device,
        mesh=mesh,
        in_specs=placed,
        out_specs=(
            P("fsdp", None),
            P("fsdp", None),
            P("fsdp"),
            P("fsdp", None),
            P("fsdp", None),
            P("fsdp", None),
            P("fsdp", None),
            P("fsdp"),
            P("fsdp", None),
            P("fsdp", None),
            P(),
        ),
        check_vma=False,
    )
```
